256 devices in a mesh: top: 2 (over core), mid: 32 (over z, x), leaf: 4 (over y).
Axes of the slice: x: 4, y: 4, z: 8, core: 2. Of those that a mesh axis runs over, the one named last changes fastest.
Arguments:
- coords: float32 [3, 589824], P(None, ('top', 'mid', 'leaf')), may hold values from 0 to 4
- weights: float32 [589824, 128], P(('top', 'mid', 'leaf')), may hold values from -6 to 6
- labels: int32 [589824, 128], P(('top', 'mid', 'leaf')), may hold values 0 or 1
- order: int32 [256, 2304], P(('top', 'mid', 'leaf')), may hold values from 0 to 2303, each once within a row
- basis: float32 [589824, 64], P(('top', 'mid', 'leaf')), may hold values from -0.125 to 0.125
- transfer_leaf: float32 [256, 64, 64], P(('top', 'mid', 'leaf')), may hold values from -0.75 to 0.75
- transfer_mid: float32 [64, 64, 64], P(('top', 'mid')), may hold values from -0.75 to 0.75
- couple_leaf: float32 [256, 4, 64, 64], P(('top', 'mid', 'leaf')), may hold values from -0.75 to 0.75
- couple_mid: float32 [64, 32, 64, 64], P(('top', 'mid')), may hold values from -0.125 to 0.125
- couple_top: float32 [2, 2, 64, 64], P('top'), may hold values from -0.09375 to 0.09375
Outputs:
- trained: float32 [589824, 128], P(('top', 'mid', 'leaf'))
The draws below stay inside these ranges and needn't reach their ends.
All inputs are finite; a program needn't handle non-finite values. No bound on the sum of `labels` on one device may be relied on, other than what follows from the above.
Results may differ from the reference program's by a relative error of at most 0.0001.
Values sent between devices are 32-bit elements; how exact they have to be, the bound alone decides.
No kernel may reach another device: no remote copies, remote signals or barrier semaphores. Data moves between devices by JAX's collectives and lax.ppermute only.
A program may use at most 64 MiB of HBM per device.

```python
import jax
import jax.numpy as jnp
from jax import lax

LEAF = 2304
RANK = 64
OUT = 128
STEPS = 2
LEAVES = 256
GROUPS = 64
POINTS = 589824
N_TOP = 2
N_MID = 32
N_LEAF = 4


def plant(drawn, stream_key, smallest, largest):
    longest = drawn.shape.index(max(drawn.shape))
    spots = []
    for shift in (0, 1):
        where = [jax.random.randint(jax.random.fold_in(stream_key, axis), (), 0, length) for axis, length in enumerate(drawn.shape)]
        where[longest] = (where[longest] + shift) % drawn.shape[longest]
        spots.append(tuple(where))
    return drawn.at[spots[0]].set(smallest).at[spots[1]].set(largest)


def block_scale(stream_key, extent, split, least, largest):
    level = 1.0
    for position, parts in split:
        draws = jax.random.uniform(jax.random.fold_in(jax.random.fold_in(stream_key, 6), position), (parts,), jnp.float32, least / len(split), largest / len(split))
        level = level * jnp.repeat(jnp.exp(draws), extent[position] // parts).reshape((-1,) + (1,) * (len(extent) - 1 - position))
    return level


def gaussian(stream_key, extent, spread, limit, pieces=(), kind=jnp.bfloat16):
    loudness = block_scale(stream_key, extent, pieces, -0.22, 0.18) if pieces else 1.0
    drawn = jax.random.normal(stream_key, extent, jnp.float32) * spread * loudness
    return jnp.minimum(jnp.maximum(drawn, -limit), limit).astype(kind)


def setup_inputs(seed: int = 0) -> dict:
    seeds = jax.random.split(jax.random.key(seed), 11)
    coords = jnp.clip(4.0 * jax.random.uniform(seeds[0], (3, POINTS), jnp.float32) ** block_scale(seeds[0], (3, POINTS), ((1, 256),), -0.2, 0.2), 0.0, 4.0)
    weights = gaussian(seeds[1], (POINTS, OUT), 1.0, 6.0, ((0, 256),), jnp.float32)
    labels = plant((jax.random.randint(seeds[2], (POINTS, OUT), 0, 2) < 1).astype(jnp.int32), jax.random.fold_in(seeds[2], 1), 0, 1)
    order = jax.vmap(lambda own: jax.random.permutation(own, LEAF))(jax.random.split(seeds[3], LEAVES)).reshape((LEAVES, LEAF)).astype(jnp.int32)
    basis = gaussian(seeds[4], (POINTS, RANK), LEAF ** -0.5, 0.125, ((0, 256),), jnp.float32)
    transfer_leaf = gaussian(seeds[5], (LEAVES, RANK, RANK), RANK ** -0.5, 0.75, ((0, 256),), jnp.float32)
    transfer_mid = gaussian(seeds[6], (GROUPS, RANK, RANK), RANK ** -0.5, 0.75, ((0, 64),), jnp.float32)
    couple_leaf = gaussian(seeds[7], (LEAVES, N_LEAF, RANK, RANK), (RANK * N_LEAF // 4) ** -0.5, 0.75, ((0, 256),), jnp.float32)
    couple_mid = gaussian(seeds[8], (GROUPS, N_MID, RANK, RANK), (RANK * N_MID * N_LEAF // 4) ** -0.5, 0.125, ((0, 64),), jnp.float32)
    couple_top = gaussian(seeds[9], (N_TOP, N_TOP, RANK, RANK), (RANK * N_TOP * N_MID * N_LEAF // 4) ** -0.5, 0.09375, ((0, 2),), jnp.float32)
    return dict(coords=coords, weights=weights, labels=labels, order=order, basis=basis, transfer_leaf=transfer_leaf, transfer_mid=transfer_mid, couple_leaf=couple_leaf, couple_mid=couple_mid, couple_top=couple_top)


def leaf_kernel(points):
    diff_sq = jnp.zeros((points.shape[1], points.shape[1]), jnp.float32)
    for axis_k in range(3):
        delta = points[axis_k][:, None] - points[axis_k][None, :]
        diff_sq = diff_sq + delta * delta
    return jnp.exp(-jnp.sqrt(diff_sq)) * (4.0 / jnp.sqrt(jnp.float32(LEAF)))

def sibling_sum(blocks, skeletons):
    nodes = blocks.shape[0]
    count = blocks.shape[1]
    own_slot = jnp.arange(nodes, dtype=jnp.int32) % count
    keep = (own_slot[:, None] != jnp.arange(count, dtype=jnp.int32)[None, :]).astype(jnp.float32)
    return jnp.einsum('psab,psbo->pao', blocks * keep[:, :, None, None], skeletons, precision=lax.Precision.HIGHEST)

def reference(coords, weights, labels, order, basis, transfer_leaf, transfer_mid, couple_leaf, couple_mid, couple_top):
    hp = lax.Precision.HIGHEST
    points = jnp.transpose(coords.reshape(3, LEAVES, LEAF), (1, 0, 2))
    label_blocks = labels.reshape(LEAVES, LEAF, OUT)
    targets = jnp.take_along_axis(label_blocks, order[:, :, None].astype(jnp.int32), axis=1).astype(jnp.float32)
    bases = basis.reshape(LEAVES, LEAF, RANK)
    current = weights.reshape(LEAVES, LEAF, OUT)
    for step in range(STEPS):
        s0 = jnp.einsum('cia,cio->cao', bases, current, precision=hp)
        up0 = jnp.einsum('cba,cbo->cao', transfer_leaf, s0, precision=hp)
        s1 = up0.reshape(GROUPS, N_LEAF, RANK, OUT).sum(axis=1)
        up1 = jnp.einsum('gba,gbo->gao', transfer_mid, s1, precision=hp)
        s2 = up1.reshape(N_TOP, N_MID, RANK, OUT).sum(axis=1)
        s2_grouped = jnp.broadcast_to(s2[None], (N_TOP, N_TOP, RANK, OUT))
        g2 = sibling_sum(couple_top, s2_grouped)
        s1_grouped = jnp.broadcast_to(s1.reshape(N_TOP, 1, N_MID, RANK, OUT), (N_TOP, N_MID, N_MID, RANK, OUT)).reshape(GROUPS, N_MID, RANK, OUT)
        g1 = sibling_sum(couple_mid, s1_grouped)
        g1 = g1 + jnp.einsum('gab,gbo->gao', transfer_mid, jnp.repeat(g2, N_MID, axis=0), precision=hp)
        s0_grouped = jnp.broadcast_to(s0.reshape(GROUPS, 1, N_LEAF, RANK, OUT), (GROUPS, N_LEAF, N_LEAF, RANK, OUT)).reshape(LEAVES, N_LEAF, RANK, OUT)
        g0 = sibling_sum(couple_leaf, s0_grouped)
        g0 = g0 + jnp.einsum('cab,cbo->cao', transfer_leaf, jnp.repeat(g1, N_LEAF, axis=0), precision=hp)

        def near(item):
            pts, block_w = item
            return jnp.dot(leaf_kernel(pts), block_w, precision=hp)
        field = lax.map(near, (points, current))
        field = field + jnp.einsum('cia,cao->cio', bases, g0, precision=hp)
        current = current - (jax.nn.sigmoid(field) - targets)
    return current.reshape(POINTS, OUT)
```

```python
import functools
import math

import jax
import jax.numpy as jnp
from jax import lax
from jax.experimental import pallas as pl
from jax.experimental.pallas import tpu as pltpu
from jax.sharding import PartitionSpec as P

STEPS = 2
RANK = 64
OUT = 128
N_MID = 32
N_LEAF = 4
QROWS = RANK // N_LEAF
QCOLS = OUT // N_LEAF
HP = lax.Precision.HIGHEST
F32 = jnp.float32
BF16 = jnp.bfloat16
LOG2E = math.log2(math.e)
CHUNKS = 3
BLOCK = 256
TILE = 32
VMEM = pl.BlockSpec(memory_space=pltpu.VMEM)


def split(x):
    hi = x.astype(BF16)
    return hi, (x - hi.astype(F32)).astype(BF16)


def wide(x):
    return jnp.concatenate(split(x), axis=1)


def dot3(tall, wide_rhs):
    d = jnp.dot(tall, wide_rhs, preferred_element_type=F32)
    m, n = d.shape[0] // 2, d.shape[1] // 2
    return d[:m, :n] + (d[:m, n:] + d[m:, :n])


def lane_group():
    return lax.broadcasted_iota(jnp.int32, (QROWS, OUT), 1) // QCOLS


def pack_quarter(full, quarter):
    group = lane_group()
    out = jnp.zeros((QROWS, OUT), F32)
    for k in range(N_LEAF):
        moved = pltpu.roll(
            full[k * QROWS : (k + 1) * QROWS], lax.rem((k - quarter + N_LEAF) * QCOLS, OUT), 1
        )
        out = jnp.where(group == k, moved, out)
    return out


def expand_packed(packed):
    group = lane_group()
    zero = jnp.zeros((QROWS, OUT), F32)
    return jnp.concatenate([jnp.where(group == k, packed, zero) for k in range(N_LEAF)], axis=0)


def fold_and_pack(grouped):
    both = grouped + pltpu.roll(grouped, 2 * QCOLS, 1)
    total = both + pltpu.roll(both, QCOLS, 1)
    group = lane_group()
    out = jnp.zeros((QROWS, OUT), F32)
    for k in range(N_LEAF):
        out = jnp.where(group == k, total[k * QROWS : (k + 1) * QROWS], out)
    return out


def unpack_quarters(packed, quarters):
    group = lane_group()
    rows = []
    for k in range(N_LEAF):
        out = jnp.zeros((QROWS, OUT), F32)
        for block, quarter in zip(packed, quarters):
            moved = pltpu.roll(block, lax.rem((quarter - k + N_LEAF) * QCOLS, OUT), 1)
            out = jnp.where(group == quarter, moved, out)
        rows.append(out)
    return jnp.concatenate(rows, axis=0)


def emit_messages(s0, move, own_ref, message_refs):
    own = lax.axis_index("leaf")
    up0 = lax.dot_general(
        move, s0, (((0,), (0,)), ((), ())), precision=HP, preferred_element_type=F32
    )
    own_ref[...] = pack_quarter(up0, own)
    for k, ref in enumerate(message_refs, 1):
        ref[0:RANK, :] = s0
        ref[RANK : RANK + QROWS, :] = pack_quarter(up0, lax.rem(own + k, N_LEAF))


def first_body(basis_ref, w_ref, move_ref, bcat_ref, bcat_t_ref, whl_ref, own_ref, *message_refs):
    bcat_ref[...] = wide(basis_ref[...])
    whl_ref[...] = wide(w_ref[...])
    bcat_t_ref[...] = bcat_ref[...].T
    s0 = dot3(bcat_t_ref[...], whl_ref[...])
    emit_messages(s0, move_ref[...], own_ref, message_refs)


def near_rows(khi_ref, klo_ref, whl_ref, scale):
    a = jnp.dot(khi_ref[...], whl_ref[...], preferred_element_type=F32)
    b = jnp.dot(klo_ref[...], whl_ref[:, 0:OUT], preferred_element_type=F32)
    return (a[:, :OUT] + (a[:, OUT:] + b)) * scale


def build_body(scale, rows_ref, coords_ref, whl_ref, khi_ref, klo_ref, near_ref):
    points = coords_ref.shape[1]

    def tile(i, carry):
        rows = pl.ds(pl.multiple_of(i * TILE, TILE), TILE)
        own = rows_ref[rows, :]
        own = [jnp.broadcast_to(own[:, k : k + 1], (TILE, BLOCK)) for k in range(3)]
        for j in range(points // BLOCK):
            cols = slice(j * BLOCK, (j + 1) * BLOCK)
            diff_sq = None
            for k in range(3):
                delta = own[k] - coords_ref[k : k + 1, cols]
                diff_sq = delta * delta if diff_sq is None else diff_sq + delta * delta
            dist = diff_sq * lax.rsqrt(jnp.maximum(diff_sq, 1e-37))
            hi, lo = split(jnp.exp2(-dist))
            khi_ref[rows, cols] = hi
            klo_ref[rows, cols] = lo
        return carry

    lax.fori_loop(0, BLOCK // TILE, tile, 0)
    near_ref[...] = near_rows(khi_ref, klo_ref, whl_ref, scale)


def near_body(scale, khi_ref, klo_ref, whl_ref, near_ref):
    near_ref[...] = near_rows(khi_ref, klo_ref, whl_ref, scale)


def middle_body(own_ref, m1_ref, m2_ref, m3_ref, move_ref, out_ref):
    tail = slice(RANK, RANK + QROWS)
    s1 = (own_ref[...] + m1_ref[tail, :]) + (m2_ref[tail, :] + m3_ref[tail, :])
    up1 = lax.dot_general(
        move_ref[...], expand_packed(s1), (((0,), (0,)), ((), ())),
        precision=HP, preferred_element_type=F32,
    )
    message = jnp.concatenate([s1, fold_and_pack(up1)], axis=0)
    out_ref[...] = jnp.broadcast_to(message[None], out_ref.shape)


def couple_body(got_ref, couple_ref, g1_ref, s2_ref, spread_ref):
    s2 = jnp.zeros((QROWS, OUT), F32)
    for m in range(N_MID):
        spread_ref[m * RANK : (m + 1) * RANK, :] = wide(expand_packed(got_ref[m, 0:QROWS, :]))
        s2 = s2 + got_ref[m, QROWS:, :]
    g1_ref[...] = fold_and_pack(dot3(couple_ref[...], spread_ref[...]))
    s2_ref[...] = s2


def update_body(last, near_refs, far, w_ref, targets_ref, bcat_ref, bcat_t_ref, move_ref, outs):
    m1_ref, m2_ref, m3_ref, down_ref, tops = far
    own = lax.axis_index("leaf")
    quarters = [lax.rem(own + N_LEAF - k, N_LEAF) for k in range(N_LEAF)]
    g1 = unpack_quarters([ref[0:QROWS, :] for ref in tops], quarters)
    s2 = unpack_quarters([ref[QROWS:, :] for ref in tops], quarters)
    parts = [ref[0:RANK, :] for ref in (m1_ref, m2_ref, m3_ref)] + [g1, s2]
    g0 = dot3(down_ref[...], wide(jnp.concatenate(parts, axis=0)))
    hi, lo = split(g0)
    rhs = jnp.concatenate(
        [jnp.concatenate([hi, lo], axis=1), jnp.concatenate([hi, jnp.zeros_like(lo)], axis=1)], axis=0
    )
    chunk = near_refs[0].shape[0]
    w_out = outs[0]
    for j in range(w_ref.shape[0] // BLOCK):
        rows = slice(j * BLOCK, (j + 1) * BLOCK)
        at = j * BLOCK % chunk
        f = jnp.dot(bcat_ref[rows, :], rhs, preferred_element_type=F32)
        f = near_refs[j * BLOCK // chunk][at : at + BLOCK, :] + (f[:, :OUT] + f[:, OUT:])
        new = w_ref[rows, :] - ((0.5 * jnp.tanh(0.5 * f) + 0.5) - targets_ref[rows, :])
        w_out[rows, :] = new
        if not last:
            outs[1][rows, :] = wide(new)
    if not last:
        s0 = dot3(bcat_t_ref[...], outs[1][...])
        emit_messages(s0, move_ref[...], outs[2], outs[3:])


def update_mid_body(*refs):
    near, m, (down, *tops), rest = refs[:3], refs[3:6], refs[6:11], refs[11:]
    update_body(False, near, (*m, down, tops), *rest[:5], rest[5:])


def update_last_body(*refs):
    near, m, (down, *tops), rest = refs[:3], refs[3:6], refs[6:11], refs[11:]
    update_body(True, near, (*m, down, tops), rest[0], rest[1], rest[2], None, None, rest[3:])


def params(mib):
    return pltpu.CompilerParams(vmem_limit_bytes=mib << 20)


def shape(*dims, dtype=F32):
    return jax.ShapeDtypeStruct(dims, dtype)


def ring(k):
    return [(i, (i + k) % N_LEAF) for i in range(N_LEAF)]


def tall(x):
    hi = lax.reduce_precision(x, 8, 7)
    return jnp.concatenate([hi, x - hi], axis=0).astype(BF16)


def on_device(
    coords,
    weights,
    labels,
    order,
    basis,
    transfer_leaf,
    transfer_mid,
    couple_leaf,
    couple_mid,
    couple_top,
):
    n = weights.shape[0]
    chunk = n // CHUNKS
    scale = 4.0 / math.sqrt(n)
    own_top = lax.axis_index("top")
    own_mid = lax.axis_index("mid")
    own_leaf = lax.axis_index("leaf")
    leaf_move = transfer_leaf[0]
    mid_move = transfer_mid[0]
    message_shapes = [shape(QROWS, OUT)] + [shape(RANK + QROWS, OUT)] * 3

    bcat, bcat_t, whl, own, *messages = pl.pallas_call(
        first_body,
        out_shape=[
            shape(n, 2 * RANK, dtype=BF16),
            shape(2 * RANK, n, dtype=BF16),
            shape(n, 2 * OUT, dtype=BF16),
            *message_shapes,
        ],
        in_specs=[VMEM] * 3,
        out_specs=[VMEM] * 7,
        compiler_params=params(16),
        name="first",
    )(basis, weights, leaf_move)

    targets = jnp.take(labels, order[0], axis=0).astype(F32)
    keep = (jnp.arange(N_MID) != own_mid).astype(F32)
    couple = tall(
        jnp.transpose(couple_mid[0] * keep[:, None, None], (1, 0, 2)).reshape(RANK, N_MID * RANK)
    )
    from_top = jnp.dot(
        leaf_move, jnp.dot(mid_move, couple_top[0, 1 - own_top], precision=HP), precision=HP
    )
    siblings = [couple_leaf[0, (own_leaf + N_LEAF - k) % N_LEAF] for k in (1, 2, 3)]
    down = tall(jnp.concatenate([*siblings, leaf_move, from_top], axis=1))

    scaled = coords * LOG2E
    scaled_rows = scaled.T
    blocks = chunk // BLOCK
    k_spec = pl.BlockSpec((BLOCK, n), lambda i: (i, 0))
    whl_spec = pl.BlockSpec((n, 2 * OUT), lambda i: (0, 0))
    near_spec = pl.BlockSpec((BLOCK, OUT), lambda i: (i, 0))
    kernels, near = [], []
    for c in range(CHUNKS):
        khi, klo, rows = pl.pallas_call(
            functools.partial(build_body, scale),
            grid=(blocks,),
            out_shape=[shape(chunk, n, dtype=BF16)] * 2 + [shape(chunk, OUT)],
            in_specs=[
                pl.BlockSpec((BLOCK, 3), lambda i, c=c: (c * blocks + i, 0)),
                pl.BlockSpec((3, n), lambda i: (0, 0)),
                whl_spec,
            ],
            out_specs=[k_spec, k_spec, near_spec],
            compiler_params=params(16),
            cost_estimate=pl.CostEstimate(
                flops=chunk * n * 2 * 512, bytes_accessed=chunk * n * 4, transcendentals=2 * chunk * n
            ),
            name="build",
        )(scaled_rows, scaled, whl)
        kernels.append((khi, klo))
        near.append(rows)

    current = weights
    for step in range(STEPS):
        last = step == STEPS - 1
        if step:
            near = [
                pl.pallas_call(
                    functools.partial(near_body, scale),
                    grid=(blocks,),
                    out_shape=shape(chunk, OUT),
                    in_specs=[k_spec, k_spec, whl_spec],
                    out_specs=near_spec,
                    compiler_params=params(16),
                    cost_estimate=pl.CostEstimate(
                        flops=chunk * n * 2 * 512, bytes_accessed=chunk * n * 4, transcendentals=0
                    ),
                    name="near",
                )(khi, klo, whl)
                for khi, klo in kernels
            ]
        messages = [lax.ppermute(m, "leaf", ring(k)) for k, m in enumerate(messages, 1)]
        spread = pl.pallas_call(
            middle_body,
            out_shape=shape(N_MID, 2 * QROWS, OUT),
            in_specs=[VMEM] * 5,
            out_specs=VMEM,
            name="middle",
        )(own, *messages, mid_move)
        got = lax.all_to_all(spread, "mid", 0, 0)
        g1, s2 = pl.pallas_call(
            couple_body,
            out_shape=[shape(QROWS, OUT)] * 2,
            in_specs=[VMEM] * 2,
            out_specs=[VMEM] * 2,
            scratch_shapes=[pltpu.VMEM((N_MID * RANK, 2 * OUT), BF16)],
            compiler_params=params(16),
            name="couple",
        )(got, couple)
        s2 = lax.ppermute(s2, "top", [(0, 1), (1, 0)])
        top = jnp.concatenate([g1, s2], axis=0)
        tops = [top] + [lax.ppermute(top, "leaf", ring(k)) for k in (1, 2, 3)]
        far = (*near, *messages, down, *tops, current, targets, bcat)
        if last:
            current = pl.pallas_call(
                update_last_body,
                out_shape=shape(n, OUT),
                in_specs=[VMEM] * 14,
                out_specs=VMEM,
                compiler_params=params(16),
                name="last",
            )(*far)
        else:
            current, whl, own, *messages = pl.pallas_call(
                update_mid_body,
                out_shape=[shape(n, OUT), shape(n, 2 * OUT, dtype=BF16), *message_shapes],
                in_specs=[VMEM] * 16,
                out_specs=[VMEM] * 6,
                compiler_params=params(16),
                name="update",
            )(*far, bcat_t, leaf_move)
    return current


def solution(mesh):
    placed = (
        P(None, ("top", "mid", "leaf")),
        P(("top", "mid", "leaf"), None),
        P(("top", "mid", "leaf"), None),
        P(("top", "mid", "leaf"), None),
        P(("top", "mid", "leaf"), None),
        P(("top", "mid", "leaf"), None, None),
        P(("top", "mid"), None, None),
        P(("top", "mid", "leaf"), None, None, None),
        P(("top", "mid"), None, None, None),
        P("top", None, None, None),
    )
    return jax.shard_map(
        on_device,
        mesh=mesh,
        in_specs=placed,
        out_specs=P(("top", "mid", "leaf"), None),
        check_vma=False,
    )
```

```python
import functools
import math

import jax
import jax.numpy as jnp
from jax import lax
from jax.experimental import pallas as pl
from jax.experimental.pallas import tpu as pltpu
from jax.sharding import PartitionSpec as P

STEPS = 2
RANK = 64
OUT = 128
N_MID = 32
N_LEAF = 4
QROWS = RANK // N_LEAF
QCOLS = OUT // N_LEAF
HP = lax.Precision.HIGHEST
F32 = jnp.float32
BF16 = jnp.bfloat16
LOG2E = math.log2(math.e)
CHUNKS = 3
BLOCK = 256
TILE = 32
VMEM = pl.BlockSpec(memory_space=pltpu.VMEM)


def split(x):
    hi = x.astype(BF16)
    return hi, (x - hi.astype(F32)).astype(BF16)


def wide(x):
    return jnp.concatenate(split(x), axis=1)


def dot3(tall, wide_rhs):
    d = jnp.dot(tall, wide_rhs, preferred_element_type=F32)
    m, n = d.shape[0] // 2, d.shape[1] // 2
    return d[:m, :n] + (d[:m, n:] + d[m:, :n])


def lane_group():
    return lax.broadcasted_iota(jnp.int32, (QROWS, OUT), 1) // QCOLS


def pack_quarter(full, quarter):
    group = lane_group()
    out = jnp.zeros((QROWS, OUT), F32)
    for k in range(N_LEAF):
        moved = pltpu.roll(
            full[k * QROWS : (k + 1) * QROWS], lax.rem((k - quarter + N_LEAF) * QCOLS, OUT), 1
        )
        out = jnp.where(group == k, moved, out)
    return out


def expand_packed(packed):
    group = lane_group()
    zero = jnp.zeros((QROWS, OUT), F32)
    return jnp.concatenate([jnp.where(group == k, packed, zero) for k in range(N_LEAF)], axis=0)


def fold_and_pack(grouped):
    both = grouped + pltpu.roll(grouped, 2 * QCOLS, 1)
    total = both + pltpu.roll(both, QCOLS, 1)
    group = lane_group()
    out = jnp.zeros((QROWS, OUT), F32)
    for k in range(N_LEAF):
        out = jnp.where(group == k, total[k * QROWS : (k + 1) * QROWS], out)
    return out


def unpack_quarters(packed, quarters):
    group = lane_group()
    rows = []
    for k in range(N_LEAF):
        out = jnp.zeros((QROWS, OUT), F32)
        for block, quarter in zip(packed, quarters):
            moved = pltpu.roll(block, lax.rem((quarter - k + N_LEAF) * QCOLS, OUT), 1)
            out = jnp.where(group == quarter, moved, out)
        rows.append(out)
    return jnp.concatenate(rows, axis=0)


def tall(x):
    return jnp.concatenate(split(x), axis=0)


def dot_rows(lhs, rhs):
    return lax.dot_general(
        lhs, rhs, (((0,), (0,)), ((), ())), precision=HP, preferred_element_type=F32
    )


def emit_messages(s0, up, own_ref, message_refs):
    own = lax.axis_index("leaf")
    both = dot_rows(up, s0)

    def quarter(q):
        return jnp.concatenate([pack_quarter(both[:RANK], q), pack_quarter(both[RANK:], q)], axis=0)

    own_ref[...] = quarter(own)
    for k, ref in enumerate(message_refs, 1):
        ref[0:RANK, :] = s0
        ref[RANK:, :] = quarter(lax.rem(own + k, N_LEAF))


def first_body(basis_t_ref, w_ref, leaf_ref, mid_ref, up_ref, own_ref, *message_refs):
    through = jnp.dot(leaf_ref[0], mid_ref[0], precision=HP, preferred_element_type=F32)
    up_ref[...] = jnp.concatenate([leaf_ref[0], through], axis=1)
    s0 = dot3(tall(basis_t_ref[...]), wide(w_ref[...]))
    emit_messages(s0, up_ref[...], own_ref, message_refs)


def prepare_body(
    coords_ref, order_ref, basis_t_ref, w_ref, leaf_ref, mid_ref, couple_leaf_ref, couple_mid_ref,
    couple_top_ref, columns_ref, bcat_ref, whl_ref, couple_ref, down_ref,
):
    n = w_ref.shape[0]
    order = order_ref[...].astype(F32)
    rows = jnp.concatenate([coords_ref[...] * LOG2E, order, jnp.zeros((4, n), F32)], axis=0)
    columns_ref[...] = rows.T
    for j in range(n // BLOCK):
        cols = slice(j * BLOCK, (j + 1) * BLOCK)
        bcat_ref[cols, :] = wide(basis_t_ref[:, cols].T)
    whl_ref[...] = wide(w_ref[...])
    own_mid, own_leaf = lax.axis_index("mid"), lax.axis_index("leaf")
    for m in range(N_MID // 2):
        pair = [
            jnp.where(own_mid == i, 0.0, couple_mid_ref[0, i]) for i in (2 * m, 2 * m + 1)
        ]
        couple_ref[:, m * OUT : (m + 1) * OUT] = tall(jnp.concatenate(pair, axis=1))
    other = 1 - lax.axis_index("top")
    from_top = jnp.dot(mid_ref[0], couple_top_ref[0, other], precision=HP, preferred_element_type=F32)
    from_top = jnp.dot(leaf_ref[0], from_top, precision=HP, preferred_element_type=F32)
    siblings = [couple_leaf_ref[0, lax.rem(own_leaf + N_LEAF - k, N_LEAF)] for k in (1, 2, 3)]
    down_ref[...] = tall(jnp.concatenate([*siblings, leaf_ref[0], from_top], axis=1))


def targets_body(columns_ref, labels_ref, out_ref, labels16_ref):
    n = labels_ref.shape[0]
    labels16_ref[...] = labels_ref[...].astype(BF16)
    lane = lax.broadcasted_iota(jnp.int32, (BLOCK, n), 1).astype(F32)

    def rows(i, carry):
        at = pl.ds(pl.multiple_of(i * BLOCK, BLOCK), BLOCK)
        chosen = jnp.where(columns_ref[at, 3:4] == lane, 1.0, 0.0).astype(BF16)
        out_ref[at, :] = jnp.dot(chosen, labels16_ref[...], preferred_element_type=F32)
        return carry

    lax.fori_loop(0, n // BLOCK, rows, 0)


def near_product(khi, klo, whl):
    a = jnp.dot(khi, whl, preferred_element_type=F32)
    b = jnp.dot(klo, whl[:, 0:OUT], preferred_element_type=F32)
    return a[:, :OUT] + (a[:, OUT:] + b)


def build_body(scale, first_row, coords_ref, columns_ref, whl_ref, khi_ref, klo_ref, near_ref, own_ref):
    chunk, points = khi_ref.shape

    def block(i, carry):
        at = pl.multiple_of(i * BLOCK, BLOCK)
        for k in range(3):
            own_ref[k] = jnp.broadcast_to(
                columns_ref[pl.ds(first_row + at, BLOCK), k : k + 1], (BLOCK, OUT)
            )
        total = None
        waiting = None
        for j in range(points // BLOCK):
            for half in range(2):
                cols = slice(j * BLOCK + half * OUT, j * BLOCK + (half + 1) * OUT)
                other = [coords_ref[k : k + 1, cols] * LOG2E for k in range(3)]
                for t in range(BLOCK // TILE):
                    sub = slice(t * TILE, (t + 1) * TILE)
                    diff_sq = None
                    for k in range(3):
                        delta = own_ref[k, sub, :] - other[k]
                        diff_sq = delta * delta if diff_sq is None else diff_sq + delta * delta
                    dist = diff_sq * lax.rsqrt(jnp.maximum(diff_sq, 1e-37))
                    hi, lo = split(jnp.exp2(-dist))
                    rows = pl.ds(at + t * TILE, TILE)
                    khi_ref[rows, cols] = hi
                    klo_ref[rows, cols] = lo
            if j % 3 == 2:
                if waiting is not None:
                    part = near_product(*waiting)
                    total = part if total is None else total + part
                at_cols = slice((j - 2) * BLOCK, (j + 1) * BLOCK)
                rows = pl.ds(at, BLOCK)
                waiting = khi_ref[rows, at_cols], klo_ref[rows, at_cols], whl_ref[at_cols, :]
        near_ref[pl.ds(at, BLOCK), :] = (total + near_product(*waiting)) * scale
        return carry

    lax.fori_loop(0, chunk // BLOCK, block, 0)


def near_body(scale, khi_ref, klo_ref, whl_ref, near_ref):
    def block(i, carry):
        rows = pl.ds(pl.multiple_of(i * BLOCK, BLOCK), BLOCK)
        near_ref[rows, :] = near_product(khi_ref[rows, :], klo_ref[rows, :], whl_ref[...]) * scale
        return carry

    lax.fori_loop(0, khi_ref.shape[0] // BLOCK, block, 0)


def middle_body(own_ref, m1_ref, m2_ref, m3_ref, out_ref):
    tail = slice(RANK, RANK + 2 * QROWS)
    total = (own_ref[...] + m1_ref[tail, :]) + (m2_ref[tail, :] + m3_ref[tail, :])
    out_ref[...] = jnp.broadcast_to(total[None], out_ref.shape)


def couple_body(got_ref, couple_ref, g1_ref, s2_ref, spread_ref):
    s2 = jnp.zeros((QROWS, OUT), F32)
    for m in range(N_MID):
        spread_ref[m * RANK : (m + 1) * RANK, :] = wide(expand_packed(got_ref[m, 0:QROWS, :]))
        s2 = s2 + got_ref[m, QROWS:, :]
    g1_ref[...] = fold_and_pack(dot3(couple_ref[...], spread_ref[...]))
    s2_ref[...] = s2


def update_body(*refs):
    near_refs, messages, down_ref, tops = refs[:3], refs[3:6], refs[6], refs[7:11]
    w_ref, targets_ref, bcat_ref = refs[11:14]
    last = len(refs) == 15
    outs = refs[14:] if last else refs[16:]
    own = lax.axis_index("leaf")
    quarters = [lax.rem(own + N_LEAF - k, N_LEAF) for k in range(N_LEAF)]
    g1 = unpack_quarters([ref[0:QROWS, :] for ref in tops], quarters)
    s2 = unpack_quarters([ref[QROWS:, :] for ref in tops], quarters)
    parts = [ref[0:RANK, :] for ref in messages] + [g1, s2]
    g0 = dot3(down_ref[...], wide(jnp.concatenate(parts, axis=0)))
    hi, lo = split(g0)
    rhs = jnp.concatenate(
        [jnp.concatenate([hi, lo], axis=1), jnp.concatenate([hi, jnp.zeros_like(lo)], axis=1)], axis=0
    )
    chunk = near_refs[0].shape[0]
    w_out = outs[0]
    for j in range(w_ref.shape[0] // BLOCK):
        rows = slice(j * BLOCK, (j + 1) * BLOCK)
        at = j * BLOCK % chunk
        f = jnp.dot(bcat_ref[rows, :], rhs, preferred_element_type=F32)
        f = near_refs[j * BLOCK // chunk][at : at + BLOCK, :] + (f[:, :OUT] + f[:, OUT:])
        new = w_ref[rows, :] - ((0.5 * jnp.tanh(0.5 * f) + 0.5) - targets_ref[rows, :])
        w_out[rows, :] = new
        if not last:
            outs[1][rows, :] = wide(new)
    if not last:
        basis_t_ref, up_ref = refs[14:16]
        s0 = dot3(tall(basis_t_ref[...]), outs[1][...])
        emit_messages(s0, up_ref[...], outs[2], outs[3:])


def params(mib):
    return pltpu.CompilerParams(vmem_limit_bytes=mib << 20)


def shape(*dims, dtype=F32):
    return jax.ShapeDtypeStruct(dims, dtype)


def ring(k):
    return [(i, (i + k) % N_LEAF) for i in range(N_LEAF)]


def call(body, out, operands, mib, name, scratch=(), work=(0, 0, 0)):
    return pl.pallas_call(
        body,
        out_shape=out,
        in_specs=[VMEM] * len(operands),
        out_specs=jax.tree.map(lambda _: VMEM, out),
        scratch_shapes=scratch,
        compiler_params=params(mib),
        cost_estimate=pl.CostEstimate(flops=work[0], bytes_accessed=work[1], transcendentals=work[2]),
        name=name,
    )(*operands)


def on_device(
    coords,
    weights,
    labels,
    order,
    basis,
    transfer_leaf,
    transfer_mid,
    couple_leaf,
    couple_mid,
    couple_top,
):
    n = weights.shape[0]
    chunk = n // CHUNKS
    scale = 4.0 / math.sqrt(n)
    basis_t = basis.T
    message_shapes = [shape(2 * QROWS, OUT)] + [shape(RANK + 2 * QROWS, OUT)] * 3
    near_work = (chunk * n * 2 * 512, chunk * n * 4, 0)

    up, own, *messages = call(
        first_body,
        [shape(RANK, 2 * RANK), *message_shapes],
        (basis_t, weights, transfer_leaf, transfer_mid),
        8,
        "first",
    )
    columns, bcat, whl, couple, down = call(
        prepare_body,
        [
            shape(n, 8),
            shape(n, 2 * RANK, dtype=BF16),
            shape(n, 2 * OUT, dtype=BF16),
            shape(2 * RANK, N_MID * RANK, dtype=BF16),
            shape(2 * RANK, 5 * RANK, dtype=BF16),
        ],
        (coords, order, basis_t, weights, transfer_leaf, transfer_mid, couple_leaf, couple_mid, couple_top),
        12,
        "prepare",
    )
    targets = call(
        targets_body,
        shape(n, OUT),
        (columns, labels),
        12,
        "targets",
        [pltpu.VMEM((n, OUT), BF16)],
        (n * n * 2 * OUT, n * OUT * 8, 0),
    )
    kernels, near = [], []
    for c in range(CHUNKS):
        khi, klo, rows = call(
            functools.partial(build_body, scale, c * chunk),
            [shape(chunk, n, dtype=BF16)] * 2 + [shape(chunk, OUT)],
            (coords, columns, whl),
            12,
            "build",
            [pltpu.VMEM((3, BLOCK, OUT), F32)],
            (*near_work[:2], 2 * chunk * n),
        )
        kernels.append((khi, klo))
        near.append(rows)

    current = weights
    for step in range(STEPS):
        last = step == STEPS - 1
        if step:
            near = [
                call(
                    functools.partial(near_body, scale),
                    shape(chunk, OUT),
                    (khi, klo, whl),
                    8,
                    "near",
                    work=near_work,
                )
                for khi, klo in kernels
            ]
        messages = [lax.ppermute(m, "leaf", ring(k)) for k, m in enumerate(messages, 1)]
        spread = call(middle_body, shape(N_MID, 2 * QROWS, OUT), (own, *messages), 4, "middle")
        got = lax.all_to_all(spread, "mid", 0, 0)
        g1, s2 = call(
            couple_body,
            [shape(QROWS, OUT)] * 2,
            (got, couple),
            8,
            "couple",
            [pltpu.VMEM((N_MID * RANK, 2 * OUT), BF16)],
        )
        s2 = lax.ppermute(s2, "top", [(0, 1), (1, 0)])
        top = jnp.concatenate([g1, s2], axis=0)
        tops = [top] + [lax.ppermute(top, "leaf", ring(k)) for k in (1, 2, 3)]
        far = (*near, *messages, down, *tops, current, targets, bcat)
        if last:
            current = call(update_body, shape(n, OUT), far, 8, "last")
        else:
            current, whl, own, *messages = call(
                update_body,
                [shape(n, OUT), shape(n, 2 * OUT, dtype=BF16), *message_shapes],
                (*far, basis_t, up),
                12,
                "update",
            )
    return current


def solution(mesh):
    placed = (
        P(None, ("top", "mid", "leaf")),
        P(("top", "mid", "leaf"), None),
        P(("top", "mid", "leaf"), None),
        P(("top", "mid", "leaf"), None),
        P(("top", "mid", "leaf"), None),
        P(("top", "mid", "leaf"), None, None),
        P(("top", "mid"), None, None),
        P(("top", "mid", "leaf"), None, None, None),
        P(("top", "mid"), None, None, None),
        P("top", None, None, None),
    )
    return jax.shard_map(
        on_device,
        mesh=mesh,
        in_specs=placed,
        out_specs=P(("top", "mid", "leaf"), None),
        check_vma=False,
    )
```

```python
import functools
import math

import jax
import jax.numpy as jnp
from jax import lax
from jax.experimental import pallas as pl
from jax.experimental.pallas import tpu as pltpu
from jax.sharding import PartitionSpec as P

STEPS = 2
RANK = 64
OUT = 128
N_MID = 32
N_LEAF = 4
QROWS = RANK // N_LEAF
QCOLS = OUT // N_LEAF
HP = lax.Precision.HIGHEST
F32 = jnp.float32
BF16 = jnp.bfloat16
LOG2E = math.log2(math.e)
BLOCK = 256
REACH = 5
TILE = 32
VMEM = pl.BlockSpec(memory_space=pltpu.VMEM)


def split(x):
    hi = x.astype(BF16)
    return hi, (x - hi.astype(F32)).astype(BF16)


def wide(x):
    return jnp.concatenate(split(x), axis=1)


def dot3(tall, wide_rhs):
    d = jnp.dot(tall, wide_rhs, preferred_element_type=F32)
    m, n = d.shape[0] // 2, d.shape[1] // 2
    return d[:m, :n] + (d[:m, n:] + d[m:, :n])


def lane_group():
    return lax.broadcasted_iota(jnp.int32, (QROWS, OUT), 1) // QCOLS


def pack_quarter(full, quarter):
    group = lane_group()
    out = jnp.zeros((QROWS, OUT), F32)
    for k in range(N_LEAF):
        moved = pltpu.roll(
            full[k * QROWS : (k + 1) * QROWS], lax.rem((k - quarter + N_LEAF) * QCOLS, OUT), 1
        )
        out = jnp.where(group == k, moved, out)
    return out


def expand_packed(packed):
    group = lane_group()
    zero = jnp.zeros((QROWS, OUT), F32)
    return jnp.concatenate([jnp.where(group == k, packed, zero) for k in range(N_LEAF)], axis=0)


def fold_and_pack(grouped):
    both = grouped + pltpu.roll(grouped, 2 * QCOLS, 1)
    total = both + pltpu.roll(both, QCOLS, 1)
    group = lane_group()
    out = jnp.zeros((QROWS, OUT), F32)
    for k in range(N_LEAF):
        out = jnp.where(group == k, total[k * QROWS : (k + 1) * QROWS], out)
    return out


def unpack_quarters(packed, quarters):
    group = lane_group()
    rows = []
    for k in range(N_LEAF):
        out = jnp.zeros((QROWS, OUT), F32)
        for block, quarter in zip(packed, quarters):
            moved = pltpu.roll(block, lax.rem((quarter - k + N_LEAF) * QCOLS, OUT), 1)
            out = jnp.where(group == quarter, moved, out)
        rows.append(out)
    return jnp.concatenate(rows, axis=0)


def tall(x):
    return jnp.concatenate(split(x), axis=0)


def dot_rows(lhs, rhs):
    return lax.dot_general(
        lhs, rhs, (((0,), (0,)), ((), ())), precision=HP, preferred_element_type=F32
    )


def emit_messages(s0, up, own_ref, message_refs):
    own = lax.axis_index("leaf")
    both = dot_rows(up, s0)

    def quarter(q):
        return jnp.concatenate([pack_quarter(both[:RANK], q), pack_quarter(both[RANK:], q)], axis=0)

    own_ref[...] = quarter(own)
    for k, ref in enumerate(message_refs, 1):
        ref[0:RANK, :] = s0
        ref[RANK:, :] = quarter(lax.rem(own + k, N_LEAF))


def first_body(basis_t_ref, w_ref, leaf_ref, mid_ref, up_ref, own_ref, *message_refs):
    through = jnp.dot(leaf_ref[0], mid_ref[0], precision=HP, preferred_element_type=F32)
    up_ref[...] = jnp.concatenate([leaf_ref[0], through], axis=1)
    s0 = dot3(tall(basis_t_ref[...]), wide(w_ref[...]))
    emit_messages(s0, up_ref[...], own_ref, message_refs)


def prepare_body(
    coords_ref, order_ref, basis_t_ref, leaf_ref, mid_ref, couple_leaf_ref, couple_mid_ref,
    couple_top_ref, columns_ref, bcat_ref, couple_ref, down_ref,
):
    n = coords_ref.shape[1]
    order = order_ref[...].astype(F32)
    rows = jnp.concatenate([coords_ref[...] * LOG2E, order, jnp.zeros((4, n), F32)], axis=0)
    columns_ref[...] = rows.T
    for j in range(n // BLOCK):
        cols = slice(j * BLOCK, (j + 1) * BLOCK)
        bcat_ref[cols, :] = wide(basis_t_ref[:, cols].T)
    own_mid, own_leaf = lax.axis_index("mid"), lax.axis_index("leaf")
    for m in range(N_MID // 2):
        pair = [
            jnp.where(own_mid == i, 0.0, couple_mid_ref[0, i]) for i in (2 * m, 2 * m + 1)
        ]
        couple_ref[:, m * OUT : (m + 1) * OUT] = tall(jnp.concatenate(pair, axis=1))
    other = 1 - lax.axis_index("top")
    from_top = jnp.dot(mid_ref[0], couple_top_ref[0, other], precision=HP, preferred_element_type=F32)
    from_top = jnp.dot(leaf_ref[0], from_top, precision=HP, preferred_element_type=F32)
    siblings = [couple_leaf_ref[0, lax.rem(own_leaf + N_LEAF - k, N_LEAF)] for k in (1, 2, 3)]
    down_ref[...] = tall(jnp.concatenate([*siblings, leaf_ref[0], from_top], axis=1))


def targets_body(columns_ref, labels_ref, out_ref, labels16_ref):
    n = labels_ref.shape[0]
    labels16_ref[...] = labels_ref[...].astype(BF16)
    lane = lax.broadcasted_iota(jnp.int32, (BLOCK, n), 1).astype(F32)

    def rows(i, carry):
        at = pl.ds(pl.multiple_of(i * BLOCK, BLOCK), BLOCK)
        chosen = jnp.where(columns_ref[at, 3:4] == lane, 1.0, 0.0).astype(BF16)
        out_ref[at, :] = jnp.dot(chosen, labels16_ref[...], preferred_element_type=F32)
        return carry

    lax.fori_loop(0, n // BLOCK, rows, 0)


def near_body(scale, coords_ref, columns_ref, w_ref, near_ref, k_ref, sum_ref, own_ref, points_ref, wt_ref):
    n = w_ref.shape[0]
    blocks = n // BLOCK
    wrap = (REACH - 1) * BLOCK
    for j in range(blocks):
        cols = slice(j * BLOCK, (j + 1) * BLOCK)
        wt_ref[:, cols] = tall(w_ref[cols, :].T)
    points_ref[:, 0:n] = coords_ref[...] * LOG2E
    points_ref[:, n:] = points_ref[:, 0:wrap]
    wt_ref[:, n:] = wt_ref[:, 0:wrap]
    sum_ref[...] = jnp.zeros_like(sum_ref)

    def place(i):
        at = pl.multiple_of(i * BLOCK, BLOCK)
        for k in range(3):
            own_ref[k] = jnp.broadcast_to(columns_ref[pl.ds(at, BLOCK), k : k + 1], (BLOCK, OUT))
        return at

    def build(at, slot, d):
        for cols in (slice(c, c + OUT) for c in range(d * BLOCK, (d + 1) * BLOCK, OUT)):
            other = [points_ref[k : k + 1, pl.ds(at + cols.start, OUT)] for k in range(3)]
            for t in range(BLOCK // TILE):
                sub = slice(t * TILE, (t + 1) * TILE)
                diff_sq = None
                for k in range(3):
                    delta = own_ref[k, sub, :] - other[k]
                    diff_sq = delta * delta if diff_sq is None else diff_sq + delta * delta
                dist = diff_sq * lax.rsqrt(jnp.maximum(diff_sq, 1e-37))
                k_ref[slot, 0, sub, cols], k_ref[slot, 1, sub, cols] = split(jnp.exp2(-dist))

    def product(w, hi, lo, contract):
        dims = (((1,), (contract,)), ((), ()))
        a = lax.dot_general(w, hi, dims, preferred_element_type=F32)
        b = lax.dot_general(w[:OUT], lo, dims, preferred_element_type=F32)
        return a[:OUT] + (a[OUT:] + b)

    def use(at, slot, d, count):
        cols = slice(d * BLOCK, (d + count) * BLOCK)
        where = pl.ds(at + d * BLOCK, count * BLOCK)
        part = product(wt_ref[:, where], k_ref[slot, 0, :, cols], k_ref[slot, 1, :, cols], 1)
        if d:
            sum_ref[:, where] += product(
                wt_ref[:, pl.ds(at, BLOCK)], k_ref[slot, 0, :, cols], k_ref[slot, 1, :, cols], 0
            )
        return part

    def finish(at, parts):
        sum_ref[:, pl.ds(at, BLOCK)] += functools.reduce(jnp.add, parts)

    def pair(p, carry):
        for slot in range(2):
            prev = pl.multiple_of((2 * p + slot) * BLOCK, BLOCK)
            at = place(2 * p + slot + 1)
            total = None
            for d in range(REACH):
                part = use(prev, slot, d, 1)
                total = part if total is None else total + part
                build(at, 1 - slot, d)
            finish(prev, [total])
        return carry

    first = place(0)
    for d in range(REACH):
        build(first, 0, d)
    lax.fori_loop(0, (blocks - 1) // 2, pair, 0)
    last = (blocks - 1) * BLOCK
    finish(last, [use(last, 0, 0, 1), use(last, 0, 1, REACH - 1)])
    for j in range(blocks):
        cols = slice(j * BLOCK, (j + 1) * BLOCK)
        total = sum_ref[:, cols]
        if j < REACH - 1:
            total = total + sum_ref[:, n + j * BLOCK : n + (j + 1) * BLOCK]
        near_ref[cols, :] = total.T * scale


def middle_body(own_ref, m1_ref, m2_ref, m3_ref, out_ref):
    tail = slice(RANK, RANK + 2 * QROWS)
    total = (own_ref[...] + m1_ref[tail, :]) + (m2_ref[tail, :] + m3_ref[tail, :])
    out_ref[...] = jnp.broadcast_to(total[None], out_ref.shape)


def couple_body(got_ref, couple_ref, g1_ref, s2_ref, spread_ref):
    s2 = jnp.zeros((QROWS, OUT), F32)
    for m in range(N_MID):
        spread_ref[m * RANK : (m + 1) * RANK, :] = wide(expand_packed(got_ref[m, 0:QROWS, :]))
        s2 = s2 + got_ref[m, QROWS:, :]
    g1_ref[...] = fold_and_pack(dot3(couple_ref[...], spread_ref[...]))
    s2_ref[...] = s2


def update_body(*refs):
    near_ref, messages, down_ref, tops = refs[0], refs[1:4], refs[4], refs[5:9]
    w_ref, targets_ref, bcat_ref = refs[9:12]
    last = len(refs) == 13
    outs = refs[12:] if last else refs[14:]
    own = lax.axis_index("leaf")
    quarters = [lax.rem(own + N_LEAF - k, N_LEAF) for k in range(N_LEAF)]
    g1 = unpack_quarters([ref[0:QROWS, :] for ref in tops], quarters)
    s2 = unpack_quarters([ref[QROWS:, :] for ref in tops], quarters)
    parts = [ref[0:RANK, :] for ref in messages] + [g1, s2]
    g0 = dot3(down_ref[...], wide(jnp.concatenate(parts, axis=0)))
    hi, lo = split(g0)
    rhs = jnp.concatenate(
        [jnp.concatenate([hi, lo], axis=1), jnp.concatenate([hi, jnp.zeros_like(lo)], axis=1)], axis=0
    )
    w_out = outs[0]
    for j in range(w_ref.shape[0] // BLOCK):
        rows = slice(j * BLOCK, (j + 1) * BLOCK)
        f = jnp.dot(bcat_ref[rows, :], rhs, preferred_element_type=F32)
        f = near_ref[rows, :] + (f[:, :OUT] + f[:, OUT:])
        new = w_ref[rows, :] - ((0.5 * jnp.tanh(0.5 * f) + 0.5) - targets_ref[rows, :])
        w_out[rows, :] = new
        if not last:
            outs[-1][rows, :] = wide(new)
    if not last:
        basis_t_ref, up_ref = refs[12:14]
        s0 = dot3(tall(basis_t_ref[...]), outs[-1][...])
        emit_messages(s0, up_ref[...], outs[1], outs[2:5])


def params(mib):
    return pltpu.CompilerParams(vmem_limit_bytes=mib << 20)


def shape(*dims, dtype=F32):
    return jax.ShapeDtypeStruct(dims, dtype)


def ring(k):
    return [(i, (i + k) % N_LEAF) for i in range(N_LEAF)]


def call(body, out, operands, mib, name, scratch=(), work=(0, 0, 0)):
    return pl.pallas_call(
        body,
        out_shape=out,
        in_specs=[VMEM] * len(operands),
        out_specs=jax.tree.map(lambda _: VMEM, out),
        scratch_shapes=scratch,
        compiler_params=params(mib),
        cost_estimate=pl.CostEstimate(flops=work[0], bytes_accessed=work[1], transcendentals=work[2]),
        name=name,
    )(*operands)


def on_device(
    coords,
    weights,
    labels,
    order,
    basis,
    transfer_leaf,
    transfer_mid,
    couple_leaf,
    couple_mid,
    couple_top,
):
    n = weights.shape[0]
    scale = 4.0 / math.sqrt(n)
    basis_t = basis.T
    message_shapes = [shape(2 * QROWS, OUT)] + [shape(RANK + 2 * QROWS, OUT)] * 3

    up, own, *messages = call(
        first_body,
        [shape(RANK, 2 * RANK), *message_shapes],
        (basis_t, weights, transfer_leaf, transfer_mid),
        58,
        "first",
    )
    columns, bcat, couple, down = call(
        prepare_body,
        [
            shape(n, 8),
            shape(n, 2 * RANK, dtype=BF16),
            shape(2 * RANK, N_MID * RANK, dtype=BF16),
            shape(2 * RANK, 5 * RANK, dtype=BF16),
        ],
        (coords, order, basis_t, transfer_leaf, transfer_mid, couple_leaf, couple_mid, couple_top),
        58,
        "prepare",
    )
    targets = call(
        targets_body,
        shape(n, OUT),
        (columns, labels),
        12,
        "targets",
        [pltpu.VMEM((n, OUT), BF16)],
        (n * n * 2 * OUT, n * OUT * 8, 0),
    )
    own, columns = lax.optimization_barrier((own, columns))

    current = weights
    for step in range(STEPS):
        last = step == STEPS - 1
        near = call(
            functools.partial(near_body, scale),
            shape(n, OUT),
            (coords, columns, current),
            20,
            "near",
            [
                pltpu.VMEM((2, 2, BLOCK, REACH * BLOCK), BF16),
                pltpu.VMEM((OUT, n + (REACH - 1) * BLOCK), F32),
                pltpu.VMEM((3, BLOCK, OUT), F32),
                pltpu.VMEM((3, n + (REACH - 1) * BLOCK), F32),
                pltpu.VMEM((2 * OUT, n + (REACH - 1) * BLOCK), BF16),
            ],
            (6 * n * n * OUT, n * OUT * 12, n * n),
        )
        messages = [lax.ppermute(m, "leaf", ring(k)) for k, m in enumerate(messages, 1)]
        spread = call(middle_body, shape(N_MID, 2 * QROWS, OUT), (own, *messages), 4, "middle")
        got = lax.all_to_all(spread, "mid", 0, 0)
        got, near = lax.optimization_barrier((got, near))
        g1, s2 = call(
            couple_body,
            [shape(QROWS, OUT)] * 2,
            (got, couple),
            8,
            "couple",
            [pltpu.VMEM((N_MID * RANK, 2 * OUT), BF16)],
        )
        s2 = lax.ppermute(s2, "top", [(0, 1), (1, 0)])
        top = jnp.concatenate([g1, s2], axis=0)
        tops = [top] + [lax.ppermute(top, "leaf", ring(k)) for k in (1, 2, 3)]
        far = (near, *messages, down, *tops, current, targets, bcat)
        if last:
            current = call(update_body, shape(n, OUT), far, 8, "last")
        else:
            current, own, *messages = call(
                update_body,
                [shape(n, OUT), *message_shapes],
                (*far, basis_t, up),
                12,
                "update",
                [pltpu.VMEM((n, 2 * OUT), BF16)],
            )
    return current


def solution(mesh):
    placed = (
        P(None, ("top", "mid", "leaf")),
        P(("top", "mid", "leaf"), None),
        P(("top", "mid", "leaf"), None),
        P(("top", "mid", "leaf"), None),
        P(("top", "mid", "leaf"), None),
        P(("top", "mid", "leaf"), None, None),
        P(("top", "mid"), None, None),
        P(("top", "mid", "leaf"), None, None, None),
        P(("top", "mid"), None, None, None),
        P("top", None, None, None),
    )
    return jax.shard_map(
        on_device,
        mesh=mesh,
        in_specs=placed,
        out_specs=P(("top", "mid", "leaf"), None),
        check_vma=False,
    )
```

```python
import functools
import math

import jax
import jax.numpy as jnp
from jax import lax
from jax.experimental import pallas as pl
from jax.experimental.pallas import tpu as pltpu
from jax.sharding import PartitionSpec as P

STEPS = 2
RANK = 64
OUT = 128
N_MID = 32
N_LEAF = 4
QROWS = RANK // N_LEAF
QCOLS = OUT // N_LEAF
HP = lax.Precision.HIGHEST
F32 = jnp.float32
BF16 = jnp.bfloat16
LOG2E = math.log2(math.e)
BLOCK = 256
REACH = 5
BITS = 8
TILE = 32
VMEM = pl.BlockSpec(memory_space=pltpu.VMEM)
HBM = pl.BlockSpec(memory_space=pltpu.HBM)


def split(x):
    hi = x.astype(BF16)
    return hi, (x - hi.astype(F32)).astype(BF16)


def wide(x):
    return jnp.concatenate(split(x), axis=1)


def dot3(tall, wide_rhs):
    d = jnp.dot(tall, wide_rhs, preferred_element_type=F32)
    m, n = d.shape[0] // 2, d.shape[1] // 2
    return d[:m, :n] + (d[:m, n:] + d[m:, :n])


def lane_group():
    return lax.broadcasted_iota(jnp.int32, (QROWS, OUT), 1) // QCOLS


def pack_quarter(full, quarter):
    group = lane_group()
    out = jnp.zeros((QROWS, OUT), F32)
    for k in range(N_LEAF):
        moved = pltpu.roll(
            full[k * QROWS : (k + 1) * QROWS], lax.rem((k - quarter + N_LEAF) * QCOLS, OUT), 1
        )
        out = jnp.where(group == k, moved, out)
    return out


def expand_packed(packed):
    group = lane_group()
    zero = jnp.zeros((QROWS, OUT), F32)
    return jnp.concatenate([jnp.where(group == k, packed, zero) for k in range(N_LEAF)], axis=0)


def fold_and_pack(grouped):
    both = grouped + pltpu.roll(grouped, 2 * QCOLS, 1)
    total = both + pltpu.roll(both, QCOLS, 1)
    group = lane_group()
    out = jnp.zeros((QROWS, OUT), F32)
    for k in range(N_LEAF):
        out = jnp.where(group == k, total[k * QROWS : (k + 1) * QROWS], out)
    return out


def unpack_quarters(packed, quarters):
    group = lane_group()
    rows = []
    for k in range(N_LEAF):
        out = jnp.zeros((QROWS, OUT), F32)
        for block, quarter in zip(packed, quarters):
            moved = pltpu.roll(block, lax.rem((quarter - k + N_LEAF) * QCOLS, OUT), 1)
            out = jnp.where(group == quarter, moved, out)
        rows.append(out)
    return jnp.concatenate(rows, axis=0)


def tall(x):
    return jnp.concatenate(split(x), axis=0)


def dot_rows(lhs, rhs):
    return lax.dot_general(
        lhs, rhs, (((0,), (0,)), ((), ())), precision=HP, preferred_element_type=F32
    )


def emit_messages(s0, up, own_ref, message_refs):
    own = lax.axis_index("leaf")
    both = dot_rows(up, s0)

    def quarter(q):
        return jnp.concatenate([pack_quarter(both[:RANK], q), pack_quarter(both[RANK:], q)], axis=0)

    own_ref[...] = quarter(own)
    for k, ref in enumerate(message_refs, 1):
        ref[0:RANK, :] = s0
        ref[RANK:, :] = quarter(lax.rem(own + k, N_LEAF))


def first_body(basis_t_ref, w_ref, leaf_ref, mid_ref, up_ref, own_ref, *message_refs):
    through = jnp.dot(leaf_ref[0], mid_ref[0], precision=HP, preferred_element_type=F32)
    up_ref[...] = jnp.concatenate([leaf_ref[0], through], axis=1)
    s0 = dot3(tall(basis_t_ref[...]), wide(w_ref[...]))
    emit_messages(s0, up_ref[...], own_ref, message_refs)


def prepare_body(
    basis_t_ref, leaf_ref, mid_ref, couple_leaf_ref, couple_mid_ref, couple_top_ref,
    bcat_ref, couple_ref, down_ref,
):
    n = basis_t_ref.shape[1]
    for j in range(n // BLOCK):
        cols = slice(j * BLOCK, (j + 1) * BLOCK)
        bcat_ref[cols, :] = wide(basis_t_ref[:, cols].T)
    own_mid, own_leaf = lax.axis_index("mid"), lax.axis_index("leaf")
    for m in range(N_MID // 2):
        pair = [
            jnp.where(own_mid == i, 0.0, couple_mid_ref[0, i]) for i in (2 * m, 2 * m + 1)
        ]
        couple_ref[:, m * OUT : (m + 1) * OUT] = tall(jnp.concatenate(pair, axis=1))
    other = 1 - lax.axis_index("top")
    from_top = jnp.dot(mid_ref[0], couple_top_ref[0, other], precision=HP, preferred_element_type=F32)
    from_top = jnp.dot(leaf_ref[0], from_top, precision=HP, preferred_element_type=F32)
    siblings = [couple_leaf_ref[0, lax.rem(own_leaf + N_LEAF - k, N_LEAF)] for k in (1, 2, 3)]
    down_ref[...] = tall(jnp.concatenate([*siblings, leaf_ref[0], from_top], axis=1))


def targets_body(order_ref, labels_ref, out_ref):
    n = labels_ref.shape[0]
    group = n // BITS
    packed = jnp.zeros((group, OUT), F32)
    for g in range(BITS):
        packed = packed + labels_ref[g * group : (g + 1) * group, :].astype(F32) * float(1 << g)
    packed = packed.astype(BF16)
    order = order_ref[...]
    which = jnp.zeros_like(order)
    place = jnp.ones(order.shape, F32)
    for g in range(1, BITS):
        beyond = order >= g * group
        which = jnp.where(beyond, g * group, which)
        place = jnp.where(beyond, 1.0 / (1 << g), place)
    rows = jnp.concatenate([(order - which).astype(F32), place, jnp.zeros((6, n), F32)], axis=0)
    lane = lax.broadcasted_iota(jnp.int32, (BLOCK, group), 1).astype(F32)
    for j in range(n // BLOCK):
        at = slice(j * BLOCK, (j + 1) * BLOCK)
        columns = rows[:, at].T
        chosen = jnp.where(columns[:, 0:1] == lane, 1.0, 0.0).astype(BF16)
        value = jnp.dot(chosen, packed, preferred_element_type=F32) * columns[:, 1:2]
        value = jnp.floor(value)
        out_ref[at, :] = value - 2.0 * jnp.floor(0.5 * value)


def near_body(
    scale, coords_ref, w_hbm, near_hbm, k_ref, sum_ref, own_ref, points_ref, wt_ref, w_ref, near_ref, w_sem, near_sem
):
    n = w_hbm.shape[0]
    blocks = n // BLOCK
    wrap = (REACH - 1) * BLOCK
    fetch = pltpu.make_async_copy(w_hbm, w_ref, w_sem)
    fetch.start()
    points_ref[0:3, 0:n] = coords_ref[...] * LOG2E
    points_ref[3:, 0:n] = jnp.zeros((5, n), F32)
    points_ref[:, n:] = points_ref[:, 0:wrap]
    sum_ref[...] = jnp.zeros_like(sum_ref)

    def place(i):
        at = pl.multiple_of(i * BLOCK, BLOCK)
        columns = points_ref[:, pl.ds(at, BLOCK)].T
        for k in range(3):
            own_ref[k] = jnp.broadcast_to(columns[:, k : k + 1], (BLOCK, OUT))
        return at

    def build(at, slot, d):
        for cols in (slice(c, c + OUT) for c in range(d * BLOCK, (d + 1) * BLOCK, OUT)):
            other = [points_ref[k : k + 1, pl.ds(at + cols.start, OUT)] for k in range(3)]
            for t in range(BLOCK // TILE):
                sub = slice(t * TILE, (t + 1) * TILE)
                diff_sq = None
                for k in range(3):
                    delta = own_ref[k, sub, :] - other[k]
                    diff_sq = delta * delta if diff_sq is None else diff_sq + delta * delta
                dist = diff_sq * lax.rsqrt(jnp.maximum(diff_sq, 1e-37))
                k_ref[slot, 0, sub, cols], k_ref[slot, 1, sub, cols] = split(jnp.exp2(-dist))

    def product(w, hi, lo, contract):
        dims = (((1,), (contract,)), ((), ()))
        a = lax.dot_general(w, hi, dims, preferred_element_type=F32)
        b = lax.dot_general(w[:OUT], lo, dims, preferred_element_type=F32)
        return a[:OUT] + (a[OUT:] + b)

    def use(at, slot, d, count):
        cols = slice(d * BLOCK, (d + count) * BLOCK)
        where = pl.ds(at + d * BLOCK, count * BLOCK)
        part = product(wt_ref[:, where], k_ref[slot, 0, :, cols], k_ref[slot, 1, :, cols], 1)
        if d:
            sum_ref[:, where] += product(
                wt_ref[:, pl.ds(at, BLOCK)], k_ref[slot, 0, :, cols], k_ref[slot, 1, :, cols], 0
            )
        return part

    def finish(at, parts):
        sum_ref[:, pl.ds(at, BLOCK)] += functools.reduce(jnp.add, parts)

    def pair(p, carry):
        for slot in range(2):
            prev = pl.multiple_of((2 * p + slot) * BLOCK, BLOCK)
            at = place(2 * p + slot + 1)
            total = None
            for d in range(REACH):
                part = use(prev, slot, d, 1)
                total = part if total is None else total + part
                build(at, 1 - slot, d)
            finish(prev, [total])
        return carry

    first = place(0)
    for d in range(REACH):
        build(first, 0, d)
    fetch.wait()
    for j in range(blocks):
        cols = slice(j * BLOCK, (j + 1) * BLOCK)
        wt_ref[:, cols] = tall(w_ref[cols, :].T)
    wt_ref[:, n:] = wt_ref[:, 0:wrap]
    lax.fori_loop(0, (blocks - 1) // 2, pair, 0)
    last = (blocks - 1) * BLOCK
    finish(last, [use(last, 0, 0, 1), use(last, 0, 1, REACH - 1)])
    for j in range(blocks):
        cols = slice(j * BLOCK, (j + 1) * BLOCK)
        total = sum_ref[:, cols]
        if j < REACH - 1:
            total = total + sum_ref[:, n + j * BLOCK : n + (j + 1) * BLOCK]
        near_ref[cols, :] = total.T * scale
        pltpu.make_async_copy(near_ref.at[cols], near_hbm.at[cols], near_sem.at[j]).start()
    for j in range(blocks):
        cols = slice(j * BLOCK, (j + 1) * BLOCK)
        pltpu.make_async_copy(near_ref.at[cols], near_hbm.at[cols], near_sem.at[j]).wait()


def middle_body(own_ref, m1_ref, m2_ref, m3_ref, out_ref):
    tail = slice(RANK, RANK + 2 * QROWS)
    total = (own_ref[...] + m1_ref[tail, :]) + (m2_ref[tail, :] + m3_ref[tail, :])
    out_ref[...] = jnp.broadcast_to(total[None], out_ref.shape)


def couple_body(got_ref, couple_ref, g1_ref, s2_ref, spread_ref):
    s2 = jnp.zeros((QROWS, OUT), F32)
    for m in range(N_MID):
        spread_ref[m * RANK : (m + 1) * RANK, :] = wide(expand_packed(got_ref[m, 0:QROWS, :]))
        s2 = s2 + got_ref[m, QROWS:, :]
    g1_ref[...] = fold_and_pack(dot3(couple_ref[...], spread_ref[...]))
    s2_ref[...] = s2


def update_body(last, *refs):
    near_hbm, messages, down_ref, tops = refs[0], refs[1:4], refs[4], refs[5:9]
    w_ref, targets_ref, bcat_ref = refs[9:12]
    if last:
        out_hbm, near_ref, near_sem, out_ref, out_sem, w_own, w_sem = refs[12:]
    else:
        basis_t_ref, up_ref, out_hbm, own_ref = refs[12:16]
        message_refs = refs[16:19]
        near_ref, near_sem, out_ref, out_sem, whl_ref = refs[19:]
    blocks = [slice(j, j + BLOCK) for j in range(0, near_ref.shape[0], BLOCK)]
    loads = []
    for j, rows in enumerate(blocks):
        loads.append([pltpu.make_async_copy(near_hbm.at[rows], near_ref.at[rows], near_sem.at[j])])
        if last:
            loads[j].append(pltpu.make_async_copy(w_ref.at[rows], w_own.at[rows], w_sem.at[j]))
        for load in loads[j]:
            load.start()
    if last:
        w_ref = w_own
    own = lax.axis_index("leaf")
    quarters = [lax.rem(own + N_LEAF - k, N_LEAF) for k in range(N_LEAF)]
    g1 = unpack_quarters([ref[0:QROWS, :] for ref in tops], quarters)
    s2 = unpack_quarters([ref[QROWS:, :] for ref in tops], quarters)
    parts = [ref[0:RANK, :] for ref in messages] + [g1, s2]
    g0 = dot3(down_ref[...], wide(jnp.concatenate(parts, axis=0)))
    hi, lo = split(g0)
    rhs = jnp.concatenate(
        [jnp.concatenate([hi, lo], axis=1), jnp.concatenate([hi, jnp.zeros_like(lo)], axis=1)], axis=0
    )
    sends = []
    for j, rows in enumerate(blocks):
        f = jnp.dot(bcat_ref[rows, :], rhs, preferred_element_type=F32)
        for load in loads[j]:
            load.wait()
        f = near_ref[rows, :] + (f[:, :OUT] + f[:, OUT:])
        new = w_ref[rows, :] - ((0.5 * jnp.tanh(0.5 * f) + 0.5) - targets_ref[rows, :])
        out_ref[rows, :] = new
        if not last:
            whl_ref[rows, :] = wide(new)
        sends.append(pltpu.make_async_copy(out_ref.at[rows], out_hbm.at[rows], out_sem.at[j]))
        sends[j].start()
    if not last:
        s0 = dot3(tall(basis_t_ref[...]), whl_ref[...])
        emit_messages(s0, up_ref[...], own_ref, message_refs)
    for send in sends:
        send.wait()


def params(mib):
    return pltpu.CompilerParams(vmem_limit_bytes=mib << 20)


def shape(*dims, dtype=F32):
    return jax.ShapeDtypeStruct(dims, dtype)


def ring(k):
    return [(i, (i + k) % N_LEAF) for i in range(N_LEAF)]


def call(body, out, operands, mib, name, scratch=(), work=(0, 0, 0), far_in=(), far_out=()):
    out = [pltpu.HBM(o.shape, o.dtype) if i in far_out else o for i, o in enumerate(out)]
    operands = [
        pltpu.with_memory_space_constraint(x, pltpu.HBM) if i in far_in else x
        for i, x in enumerate(operands)
    ]
    return pl.pallas_call(
        body,
        out_shape=out,
        in_specs=[HBM if i in far_in else VMEM for i in range(len(operands))],
        out_specs=[HBM if i in far_out else VMEM for i in range(len(out))],
        scratch_shapes=scratch,
        compiler_params=params(mib),
        cost_estimate=pl.CostEstimate(flops=work[0], bytes_accessed=work[1], transcendentals=work[2]),
        name=name,
    )(*operands)


def on_device(
    coords,
    weights,
    labels,
    order,
    basis,
    transfer_leaf,
    transfer_mid,
    couple_leaf,
    couple_mid,
    couple_top,
):
    n = weights.shape[0]
    scale = 4.0 / math.sqrt(n)
    basis_t = basis.T
    wide_n = n + (REACH - 1) * BLOCK
    message_shapes = [shape(2 * QROWS, OUT)] + [shape(RANK + 2 * QROWS, OUT)] * 3

    up, own, *messages = call(
        first_body,
        [shape(RANK, 2 * RANK), *message_shapes],
        (basis_t, weights, transfer_leaf, transfer_mid),
        58,
        "first",
    )
    bcat, couple, down = call(
        prepare_body,
        [
            shape(n, 2 * RANK, dtype=BF16),
            shape(2 * RANK, N_MID * RANK, dtype=BF16),
            shape(2 * RANK, 5 * RANK, dtype=BF16),
        ],
        (basis_t, transfer_leaf, transfer_mid, couple_leaf, couple_mid, couple_top),
        58,
        "prepare",
    )
    (targets,) = call(
        targets_body,
        [shape(n, OUT)],
        (order, labels),
        12,
        "targets",
        work=(n * n // BITS * 2 * OUT, n * OUT * 8, 0),
    )
    own, couple = lax.optimization_barrier((own, couple))

    current = weights
    for step in range(STEPS):
        last = step == STEPS - 1
        (near,) = call(
            functools.partial(near_body, scale),
            [shape(n, OUT)],
            (coords, current),
            20,
            "near",
            [
                pltpu.VMEM((2, 2, BLOCK, REACH * BLOCK), BF16),
                pltpu.VMEM((OUT, wide_n), F32),
                pltpu.VMEM((3, BLOCK, OUT), F32),
                pltpu.VMEM((8, wide_n), F32),
                pltpu.VMEM((2 * OUT, wide_n), BF16),
                pltpu.VMEM((n, OUT), F32),
                pltpu.VMEM((n, OUT), F32),
                pltpu.SemaphoreType.DMA,
                pltpu.SemaphoreType.DMA((n // BLOCK,)),
            ],
            (6 * n * n * OUT, n * OUT * 12, n * n),
            (1,),
            (0,),
        )
        messages = [lax.ppermute(m, "leaf", ring(k)) for k, m in enumerate(messages, 1)]
        (spread,) = call(middle_body, [shape(N_MID, 2 * QROWS, OUT)], (own, *messages), 4, "middle")
        got = lax.all_to_all(spread, "mid", 0, 0)
        got, near = lax.optimization_barrier((got, near))
        g1, s2 = call(
            couple_body,
            [shape(QROWS, OUT)] * 2,
            (got, couple),
            8,
            "couple",
            [pltpu.VMEM((N_MID * RANK, 2 * OUT), BF16)],
        )
        s2 = lax.ppermute(s2, "top", [(0, 1), (1, 0)])
        top = jnp.concatenate([g1, s2], axis=0)
        tops = [top] + [lax.ppermute(top, "leaf", ring(k)) for k in (1, 2, 3)]
        far = (near, *messages, down, *tops, current, targets, bcat)
        rows_buffer = [pltpu.VMEM((n, OUT), F32), pltpu.SemaphoreType.DMA((n // BLOCK,))]
        body = functools.partial(update_body, last)
        if last:
            (current,) = call(
                body, [shape(n, OUT)], far, 12, "last", rows_buffer * 3, far_in=(0, 9), far_out=(0,)
            )
        else:
            current, own, *messages = call(
                body,
                [shape(n, OUT), *message_shapes],
                (*far, basis_t, up),
                16,
                "update",
                rows_buffer * 2 + [pltpu.VMEM((n, 2 * OUT), BF16)],
                far_in=(0,),
                far_out=(0,),
            )
    return current


def solution(mesh):
    placed = (
        P(None, ("top", "mid", "leaf")),
        P(("top", "mid", "leaf"), None),
        P(("top", "mid", "leaf"), None),
        P(("top", "mid", "leaf"), None),
        P(("top", "mid", "leaf"), None),
        P(("top", "mid", "leaf"), None, None),
        P(("top", "mid"), None, None),
        P(("top", "mid", "leaf"), None, None, None),
        P(("top", "mid"), None, None, None),
        P("top", None, None, None),
    )
    return jax.shard_map(
        on_device,
        mesh=mesh,
        in_specs=placed,
        out_specs=P(("top", "mid", "leaf"), None),
        check_vma=False,
    )
```

```python
import functools
import math

import jax
import jax.numpy as jnp
from jax import lax
from jax.experimental import pallas as pl
from jax.experimental.pallas import tpu as pltpu
from jax.sharding import PartitionSpec as P

STEPS = 2
RANK = 64
OUT = 128
N_MID = 32
N_LEAF = 4
QROWS = RANK // N_LEAF
QCOLS = OUT // N_LEAF
HP = lax.Precision.HIGHEST
F32 = jnp.float32
BF16 = jnp.bfloat16
LOG2E = math.log2(math.e)
BLOCK = 256
REACH = 5
BITS = 8
GROUP = 3
TILE = 32
VMEM = pl.BlockSpec(memory_space=pltpu.VMEM)
HBM = pl.BlockSpec(memory_space=pltpu.HBM)


def split(x):
    hi = x.astype(BF16)
    return hi, (x - hi.astype(F32)).astype(BF16)


def wide(x):
    return jnp.concatenate(split(x), axis=1)


def dot3(tall, wide_rhs):
    d = jnp.dot(tall, wide_rhs, preferred_element_type=F32)
    m, n = d.shape[0] // 2, d.shape[1] // 2
    return d[:m, :n] + (d[:m, n:] + d[m:, :n])


def lane_group():
    return lax.broadcasted_iota(jnp.int32, (QROWS, OUT), 1) // QCOLS


def pack_quarter(full, quarter):
    group = lane_group()
    out = jnp.zeros((QROWS, OUT), F32)
    for k in range(N_LEAF):
        moved = pltpu.roll(
            full[k * QROWS : (k + 1) * QROWS], lax.rem((k - quarter + N_LEAF) * QCOLS, OUT), 1
        )
        out = jnp.where(group == k, moved, out)
    return out


def expand_packed(packed):
    group = lane_group()
    zero = jnp.zeros((QROWS, OUT), F32)
    return jnp.concatenate([jnp.where(group == k, packed, zero) for k in range(N_LEAF)], axis=0)


def fold_and_pack(grouped):
    both = grouped + pltpu.roll(grouped, 2 * QCOLS, 1)
    total = both + pltpu.roll(both, QCOLS, 1)
    group = lane_group()
    out = jnp.zeros((QROWS, OUT), F32)
    for k in range(N_LEAF):
        out = jnp.where(group == k, total[k * QROWS : (k + 1) * QROWS], out)
    return out


def unpack_quarters(packed, quarters):
    group = lane_group()
    rows = []
    for k in range(N_LEAF):
        out = jnp.zeros((QROWS, OUT), F32)
        for block, quarter in zip(packed, quarters):
            moved = pltpu.roll(block, lax.rem((quarter - k + N_LEAF) * QCOLS, OUT), 1)
            out = jnp.where(group == quarter, moved, out)
        rows.append(out)
    return jnp.concatenate(rows, axis=0)


def tall(x):
    return jnp.concatenate(split(x), axis=0)


def dot_rows(lhs, rhs):
    return lax.dot_general(
        lhs, rhs, (((0,), (0,)), ((), ())), precision=HP, preferred_element_type=F32
    )


def emit_messages(s0, up, own_ref, message_refs):
    own = lax.axis_index("leaf")
    both = dot_rows(up, s0)

    def quarter(q):
        return jnp.concatenate([pack_quarter(both[:RANK], q), pack_quarter(both[RANK:], q)], axis=0)

    own_ref[...] = quarter(own)
    for k, ref in enumerate(message_refs, 1):
        ref[0:RANK, :] = s0
        ref[RANK:, :] = quarter(lax.rem(own + k, N_LEAF))


def first_body(basis_t_ref, w_ref, leaf_ref, mid_ref, up_ref, own_ref, *message_refs):
    through = jnp.dot(leaf_ref[0], mid_ref[0], precision=HP, preferred_element_type=F32)
    up_ref[...] = jnp.concatenate([leaf_ref[0], through], axis=1)
    s0 = dot3(tall(basis_t_ref[...]), wide(w_ref[...]))
    emit_messages(s0, up_ref[...], own_ref, message_refs)


def prepare_body(
    basis_t_ref, leaf_ref, mid_ref, couple_leaf_ref, couple_mid_ref, couple_top_ref,
    bcat_ref, couple_ref, down_ref,
):
    n = basis_t_ref.shape[1]
    for j in range(n // BLOCK):
        cols = slice(j * BLOCK, (j + 1) * BLOCK)
        bcat_ref[cols, :] = wide(basis_t_ref[:, cols].T)
    own_mid, own_leaf = lax.axis_index("mid"), lax.axis_index("leaf")
    for m in range(N_MID // 2):
        pair = [
            jnp.where(own_mid == i, 0.0, couple_mid_ref[0, i]) for i in (2 * m, 2 * m + 1)
        ]
        couple_ref[:, m * OUT : (m + 1) * OUT] = tall(jnp.concatenate(pair, axis=1))
    other = 1 - lax.axis_index("top")
    from_top = jnp.dot(mid_ref[0], couple_top_ref[0, other], precision=HP, preferred_element_type=F32)
    from_top = jnp.dot(leaf_ref[0], from_top, precision=HP, preferred_element_type=F32)
    siblings = [couple_leaf_ref[0, lax.rem(own_leaf + N_LEAF - k, N_LEAF)] for k in (1, 2, 3)]
    down_ref[...] = tall(jnp.concatenate([*siblings, leaf_ref[0], from_top], axis=1))


def targets_body(order_ref, labels_hbm, out_ref, labels_ref, sem):
    n = labels_ref.shape[0]
    group = n // BITS
    fetch = pltpu.make_async_copy(labels_hbm, labels_ref, sem)
    fetch.start()
    order = order_ref[...]
    which = jnp.zeros_like(order)
    place = jnp.ones(order.shape, F32)
    for g in range(1, BITS):
        beyond = order >= g * group
        which = jnp.where(beyond, g * group, which)
        place = jnp.where(beyond, 1.0 / (1 << g), place)
    rows = jnp.concatenate([(order - which).astype(F32), place, jnp.zeros((6, n), F32)], axis=0)
    fetch.wait()
    packed = jnp.zeros((group, OUT), F32)
    for g in range(BITS):
        packed = packed + labels_ref[g * group : (g + 1) * group, :].astype(F32) * float(1 << g)
    packed = packed.astype(BF16)
    lane = lax.broadcasted_iota(jnp.int32, (BLOCK, group), 1).astype(F32)
    for j in range(n // BLOCK):
        at = slice(j * BLOCK, (j + 1) * BLOCK)
        columns = rows[:, at].T
        chosen = jnp.where(columns[:, 0:1] == lane, 1.0, 0.0).astype(BF16)
        value = jnp.dot(chosen, packed, preferred_element_type=F32) * columns[:, 1:2]
        value = jnp.floor(value)
        out_ref[at, :] = value - 2.0 * jnp.floor(0.5 * value)


def near_body(
    scale, coords_ref, w_hbm, near_hbm, k_ref, sum_ref, own_ref, points_ref, wt_ref, w_ref, near_ref, w_sem, near_sem,
    columns_ref,
):
    n = w_hbm.shape[0]
    blocks = n // BLOCK
    wrap = (REACH - 1) * BLOCK
    fetch = pltpu.make_async_copy(w_hbm, w_ref, w_sem)
    fetch.start()
    points_ref[0:3, 0:n] = coords_ref[...] * LOG2E
    points_ref[3:, 0:n] = jnp.zeros((5, n), F32)
    points_ref[:, n:] = points_ref[:, 0:wrap]
    sum_ref[...] = jnp.zeros_like(sum_ref)

    for j in range(blocks):
        cols = slice(j * BLOCK, (j + 1) * BLOCK)
        columns_ref[cols, :] = points_ref[:, cols].T

    def place(i, slot):
        for k in range(3):
            own_ref[slot, k] = jnp.broadcast_to(
                columns_ref[pl.ds(pl.multiple_of(i * BLOCK, BLOCK), BLOCK), k : k + 1], (BLOCK, OUT)
            )

    def build(at, slot, d):
        for cols in (slice(c, c + OUT) for c in range(d * BLOCK, (d + 1) * BLOCK, OUT)):
            other = [points_ref[k : k + 1, pl.ds(at + cols.start, OUT)] for k in range(3)]
            for t in range(BLOCK // TILE):
                sub = slice(t * TILE, (t + 1) * TILE)
                diff_sq = None
                for k in range(3):
                    delta = own_ref[slot, k, sub, :] - other[k]
                    diff_sq = delta * delta if diff_sq is None else diff_sq + delta * delta
                dist = diff_sq * lax.rsqrt(jnp.maximum(diff_sq, 1e-37))
                k_ref[slot, 0, sub, cols], k_ref[slot, 1, sub, cols] = split(jnp.exp2(-dist))

    def product(w, hi, lo, contract):
        dims = (((1,), (contract,)), ((), ()))
        a = lax.dot_general(w, hi, dims, preferred_element_type=F32)
        b = lax.dot_general(w[:OUT], lo, dims, preferred_element_type=F32)
        return a[:OUT] + (a[OUT:] + b)

    def use(at, slot, d, count):
        cols = slice(d * BLOCK, (d + count) * BLOCK)
        where = pl.ds(at + d * BLOCK, count * BLOCK)
        part = product(wt_ref[:, where], k_ref[slot, 0, :, cols], k_ref[slot, 1, :, cols], 1)
        if d:
            sum_ref[:, where] += product(
                wt_ref[:, pl.ds(at, BLOCK)], k_ref[slot, 0, :, cols], k_ref[slot, 1, :, cols], 0
            )
        return part

    def finish(at, parts):
        sum_ref[:, pl.ds(at, BLOCK)] += functools.reduce(jnp.add, parts)

    def pair(p, carry):
        for slot in range(2):
            prev = pl.multiple_of((2 * p + slot) * BLOCK, BLOCK)
            at = pl.multiple_of(prev + BLOCK, BLOCK)
            place(lax.rem(2 * p + slot + 2, blocks), slot)
            total = None
            for d in range(REACH):
                part = use(prev, slot, d, 1)
                total = part if total is None else total + part
                build(at, 1 - slot, d)
            finish(prev, [total])
        return carry

    place(0, 0)
    place(1, 1)
    for d in range(REACH):
        build(0, 0, d)
    fetch.wait()
    for j in range(blocks):
        cols = slice(j * BLOCK, (j + 1) * BLOCK)
        wt_ref[:, cols] = tall(w_ref[cols, :].T)
    wt_ref[:, n:] = wt_ref[:, 0:wrap]
    lax.fori_loop(0, (blocks - 1) // 2, pair, 0)
    last = (blocks - 1) * BLOCK
    finish(last, [use(last, 0, 0, 1), use(last, 0, 1, REACH - 1)])
    sends = []
    for j in range(blocks):
        cols = slice(j * BLOCK, (j + 1) * BLOCK)
        total = sum_ref[:, cols]
        if j < REACH - 1:
            total = total + sum_ref[:, n + j * BLOCK : n + (j + 1) * BLOCK]
        near_ref[cols, :] = total.T * scale
        if j % GROUP == GROUP - 1:
            part = slice((j + 1 - GROUP) * BLOCK, (j + 1) * BLOCK)
            sends.append(pltpu.make_async_copy(near_ref.at[part], near_hbm.at[part], near_sem.at[j // GROUP]))
            sends[-1].start()
    for send in sends:
        send.wait()


def middle_body(own_ref, m1_ref, m2_ref, m3_ref, out_ref):
    tail = slice(RANK, RANK + 2 * QROWS)
    total = (own_ref[...] + m1_ref[tail, :]) + (m2_ref[tail, :] + m3_ref[tail, :])
    out_ref[...] = jnp.broadcast_to(total[None], out_ref.shape)


def couple_body(got_ref, couple_ref, g1_ref, s2_ref, spread_ref):
    s2 = jnp.zeros((QROWS, OUT), F32)
    for m in range(N_MID):
        spread_ref[m * RANK : (m + 1) * RANK, :] = wide(expand_packed(got_ref[m, 0:QROWS, :]))
        s2 = s2 + got_ref[m, QROWS:, :]
    g1_ref[...] = fold_and_pack(dot3(couple_ref[...], spread_ref[...]))
    s2_ref[...] = s2


def update_body(last, *refs):
    near_hbm, messages, down_ref, tops = refs[0], refs[1:4], refs[4], refs[5:9]
    w_ref, targets_ref, bcat_ref = refs[9:12]
    if last:
        out_hbm, near_ref, near_sem, out_ref, out_sem, w_own, w_sem = refs[12:]
    else:
        basis_t_ref, up_ref, out_hbm, own_ref = refs[12:16]
        message_refs = refs[16:19]
        near_ref, near_sem, out_ref, out_sem, whl_ref = refs[19:]
    blocks = [slice(j, j + BLOCK) for j in range(0, near_ref.shape[0], BLOCK)]
    parts = [slice(j, j + GROUP * BLOCK) for j in range(0, near_ref.shape[0], GROUP * BLOCK)]
    loads = [pltpu.make_async_copy(near_hbm.at[p], near_ref.at[p], near_sem.at[j]) for j, p in enumerate(parts)]
    if last:
        loads += [pltpu.make_async_copy(w_ref.at[p], w_own.at[p], w_sem.at[j]) for j, p in enumerate(parts)]
        w_ref = w_own
    for load in loads:
        load.start()
    own = lax.axis_index("leaf")
    quarters = [lax.rem(own + N_LEAF - k, N_LEAF) for k in range(N_LEAF)]
    g1 = unpack_quarters([ref[0:QROWS, :] for ref in tops], quarters)
    s2 = unpack_quarters([ref[QROWS:, :] for ref in tops], quarters)
    skeletons = [ref[0:RANK, :] for ref in messages] + [g1, s2]
    g0 = dot3(down_ref[...], wide(jnp.concatenate(skeletons, axis=0)))
    hi, lo = split(g0)
    rhs = jnp.concatenate(
        [jnp.concatenate([hi, lo], axis=1), jnp.concatenate([hi, jnp.zeros_like(lo)], axis=1)], axis=0
    )
    for rows in blocks:
        f = jnp.dot(bcat_ref[rows, :], rhs, preferred_element_type=F32)
        out_ref[rows, :] = f[:, :OUT] + f[:, OUT:]
    for load in loads:
        load.wait()
    sends = []
    for j, part in enumerate(parts):
        for rows in blocks[j * GROUP : (j + 1) * GROUP]:
            f = near_ref[rows, :] + out_ref[rows, :]
            new = w_ref[rows, :] - ((0.5 * jnp.tanh(0.5 * f) + 0.5) - targets_ref[rows, :])
            out_ref[rows, :] = new
            if not last:
                whl_ref[rows, :] = wide(new)
        sends.append(pltpu.make_async_copy(out_ref.at[part], out_hbm.at[part], out_sem.at[j]))
        sends[j].start()
    if not last:
        s0 = dot3(tall(basis_t_ref[...]), whl_ref[...])
        emit_messages(s0, up_ref[...], own_ref, message_refs)
    for send in sends:
        send.wait()


def params(mib):
    return pltpu.CompilerParams(vmem_limit_bytes=mib << 20)


def shape(*dims, dtype=F32):
    return jax.ShapeDtypeStruct(dims, dtype)


def ring(k):
    return [(i, (i + k) % N_LEAF) for i in range(N_LEAF)]


def call(body, out, operands, mib, name, scratch=(), work=(0, 0, 0), far_in=(), far_out=()):
    out = [pltpu.HBM(o.shape, o.dtype) if i in far_out else o for i, o in enumerate(out)]
    operands = [
        pltpu.with_memory_space_constraint(x, pltpu.HBM) if i in far_in else x
        for i, x in enumerate(operands)
    ]
    return pl.pallas_call(
        body,
        out_shape=out,
        in_specs=[HBM if i in far_in else VMEM for i in range(len(operands))],
        out_specs=[HBM if i in far_out else VMEM for i in range(len(out))],
        scratch_shapes=scratch,
        compiler_params=params(mib),
        cost_estimate=pl.CostEstimate(flops=work[0], bytes_accessed=work[1], transcendentals=work[2]),
        name=name,
    )(*operands)


def on_device(
    coords,
    weights,
    labels,
    order,
    basis,
    transfer_leaf,
    transfer_mid,
    couple_leaf,
    couple_mid,
    couple_top,
):
    n = weights.shape[0]
    scale = 4.0 / math.sqrt(n)
    basis_t = basis.T
    groups = n // (GROUP * BLOCK)
    wide_n = n + (REACH - 1) * BLOCK
    message_shapes = [shape(2 * QROWS, OUT)] + [shape(RANK + 2 * QROWS, OUT)] * 3

    up, own, *messages = call(
        first_body,
        [shape(RANK, 2 * RANK), *message_shapes],
        (basis_t, weights, transfer_leaf, transfer_mid),
        58,
        "first",
    )
    bcat, couple, down = call(
        prepare_body,
        [
            shape(n, 2 * RANK, dtype=BF16),
            shape(2 * RANK, N_MID * RANK, dtype=BF16),
            shape(2 * RANK, 5 * RANK, dtype=BF16),
        ],
        (basis_t, transfer_leaf, transfer_mid, couple_leaf, couple_mid, couple_top),
        58,
        "prepare",
    )
    (targets,) = call(
        targets_body,
        [shape(n, OUT)],
        (order, labels),
        12,
        "targets",
        [pltpu.VMEM((n, OUT), jnp.int32), pltpu.SemaphoreType.DMA],
        (n * n // BITS * 2 * OUT, n * OUT * 8, 0),
        far_in=(1,),
    )
    own, couple = lax.optimization_barrier((own, couple))

    current = weights
    for step in range(STEPS):
        last = step == STEPS - 1
        (near,) = call(
            functools.partial(near_body, scale),
            [shape(n, OUT)],
            (coords, current),
            20,
            "near",
            [
                pltpu.VMEM((2, 2, BLOCK, REACH * BLOCK), BF16),
                pltpu.VMEM((OUT, wide_n), F32),
                pltpu.VMEM((2, 3, BLOCK, OUT), F32),
                pltpu.VMEM((8, wide_n), F32),
                pltpu.VMEM((2 * OUT, wide_n), BF16),
                pltpu.VMEM((n, OUT), F32),
                pltpu.VMEM((n, OUT), F32),
                pltpu.SemaphoreType.DMA,
                pltpu.SemaphoreType.DMA((groups,)),
                pltpu.VMEM((n, 8), F32),
            ],
            (6 * n * n * OUT, n * OUT * 12, n * n),
            (1,),
            (0,),
        )
        messages = [lax.ppermute(m, "leaf", ring(k)) for k, m in enumerate(messages, 1)]
        (spread,) = call(middle_body, [shape(N_MID, 2 * QROWS, OUT)], (own, *messages), 4, "middle")
        got = lax.all_to_all(spread, "mid", 0, 0)
        got, near = lax.optimization_barrier((got, near))
        g1, s2 = call(
            couple_body,
            [shape(QROWS, OUT)] * 2,
            (got, couple),
            8,
            "couple",
            [pltpu.VMEM((N_MID * RANK, 2 * OUT), BF16)],
        )
        s2 = lax.ppermute(s2, "top", [(0, 1), (1, 0)])
        top = jnp.concatenate([g1, s2], axis=0)
        tops = [top] + [lax.ppermute(top, "leaf", ring(k)) for k in (1, 2, 3)]
        far = (near, *messages, down, *tops, current, targets, bcat)
        rows_buffer = [pltpu.VMEM((n, OUT), F32), pltpu.SemaphoreType.DMA((groups,))]
        body = functools.partial(update_body, last)
        if last:
            (current,) = call(
                body, [shape(n, OUT)], far, 12, "last", rows_buffer * 3, far_in=(0, 9), far_out=(0,)
            )
        else:
            current, own, *messages = call(
                body,
                [shape(n, OUT), *message_shapes],
                (*far, basis_t, up),
                16,
                "update",
                rows_buffer * 2 + [pltpu.VMEM((n, 2 * OUT), BF16)],
                far_in=(0,),
                far_out=(0,),
            )
    return current


def solution(mesh):
    placed = (
        P(None, ("top", "mid", "leaf")),
        P(("top", "mid", "leaf"), None),
        P(("top", "mid", "leaf"), None),
        P(("top", "mid", "leaf"), None),
        P(("top", "mid", "leaf"), None),
        P(("top", "mid", "leaf"), None, None),
        P(("top", "mid"), None, None),
        P(("top", "mid", "leaf"), None, None, None),
        P(("top", "mid"), None, None, None),
        P("top", None, None, None),
    )
    return jax.shard_map(
        on_device,
        mesh=mesh,
        in_specs=placed,
        out_specs=P(("top", "mid", "leaf"), None),
        check_vma=False,
    )
```

```python
import functools
import math

import jax
import jax.numpy as jnp
from jax import lax
from jax.experimental import pallas as pl
from jax.experimental.pallas import tpu as pltpu
from jax.sharding import PartitionSpec as P

STEPS = 2
RANK = 64
OUT = 128
N_MID = 32
N_LEAF = 4
QROWS = RANK // N_LEAF
QCOLS = OUT // N_LEAF
HP = lax.Precision.HIGHEST
F32 = jnp.float32
BF16 = jnp.bfloat16
LOG2E = math.log2(math.e)
BLOCK = 256
REACH = 5
BITS = 8
GROUP = 3
TILE = 32
VMEM = pl.BlockSpec(memory_space=pltpu.VMEM)
HBM = pl.BlockSpec(memory_space=pltpu.HBM)


def split(x):
    hi = x.astype(BF16)
    return hi, (x - hi.astype(F32)).astype(BF16)


def wide(x):
    return jnp.concatenate(split(x), axis=1)


def dot3(tall, wide_rhs):
    d = jnp.dot(tall, wide_rhs, preferred_element_type=F32)
    m, n = d.shape[0] // 2, d.shape[1] // 2
    return d[:m, :n] + (d[:m, n:] + d[m:, :n])


def lane_group():
    return lax.broadcasted_iota(jnp.int32, (QROWS, OUT), 1) // QCOLS


def pack_quarter(full, quarter):
    group = lane_group()
    out = jnp.zeros((QROWS, OUT), F32)
    for k in range(N_LEAF):
        moved = pltpu.roll(
            full[k * QROWS : (k + 1) * QROWS], lax.rem((k - quarter + N_LEAF) * QCOLS, OUT), 1
        )
        out = jnp.where(group == k, moved, out)
    return out


def expand_packed(packed):
    group = lane_group()
    zero = jnp.zeros((QROWS, OUT), F32)
    return jnp.concatenate([jnp.where(group == k, packed, zero) for k in range(N_LEAF)], axis=0)


def fold_and_pack(grouped):
    both = grouped + pltpu.roll(grouped, 2 * QCOLS, 1)
    total = both + pltpu.roll(both, QCOLS, 1)
    group = lane_group()
    out = jnp.zeros((QROWS, OUT), F32)
    for k in range(N_LEAF):
        out = jnp.where(group == k, total[k * QROWS : (k + 1) * QROWS], out)
    return out


def unpack_quarters(packed, quarters):
    group = lane_group()
    rows = []
    for k in range(N_LEAF):
        out = jnp.zeros((QROWS, OUT), F32)
        for block, quarter in zip(packed, quarters):
            moved = pltpu.roll(block, lax.rem((quarter - k + N_LEAF) * QCOLS, OUT), 1)
            out = jnp.where(group == quarter, moved, out)
        rows.append(out)
    return jnp.concatenate(rows, axis=0)


def tall(x):
    return jnp.concatenate(split(x), axis=0)


def dot_rows(lhs, rhs):
    return lax.dot_general(
        lhs, rhs, (((0,), (0,)), ((), ())), precision=HP, preferred_element_type=F32
    )


def emit_messages(s0, up, own_ref, message_refs):
    own = lax.axis_index("leaf")
    both = dot_rows(up, s0)

    def quarter(q):
        return jnp.concatenate([pack_quarter(both[:RANK], q), pack_quarter(both[RANK:], q)], axis=0)

    own_ref[...] = quarter(own)
    for k, ref in enumerate(message_refs, 1):
        ref[0:RANK, :] = s0
        ref[RANK:, :] = quarter(lax.rem(own + k, N_LEAF))


def first_body(basis_t_ref, w_ref, leaf_ref, mid_ref, up_ref, own_ref, *message_refs):
    through = jnp.dot(leaf_ref[0], mid_ref[0], precision=HP, preferred_element_type=F32)
    up_ref[...] = jnp.concatenate([leaf_ref[0], through], axis=1)
    s0 = dot3(tall(basis_t_ref[...]), wide(w_ref[...]))
    emit_messages(s0, up_ref[...], own_ref, message_refs)


def prepare_body(
    basis_t_ref, leaf_ref, mid_ref, couple_leaf_ref, couple_mid_ref, couple_top_ref,
    bcat_ref, couple_ref, down_ref,
):
    n = basis_t_ref.shape[1]
    for j in range(n // BLOCK):
        cols = slice(j * BLOCK, (j + 1) * BLOCK)
        bcat_ref[cols, :] = wide(basis_t_ref[:, cols].T)
    own_mid, own_leaf = lax.axis_index("mid"), lax.axis_index("leaf")
    for m in range(N_MID // 2):
        pair = [
            jnp.where(own_mid == i, 0.0, couple_mid_ref[0, i]) for i in (2 * m, 2 * m + 1)
        ]
        couple_ref[:, m * OUT : (m + 1) * OUT] = tall(jnp.concatenate(pair, axis=1))
    other = 1 - lax.axis_index("top")
    from_top = jnp.dot(mid_ref[0], couple_top_ref[0, other], precision=HP, preferred_element_type=F32)
    from_top = jnp.dot(leaf_ref[0], from_top, precision=HP, preferred_element_type=F32)
    siblings = [couple_leaf_ref[0, lax.rem(own_leaf + N_LEAF - k, N_LEAF)] for k in (1, 2, 3)]
    down_ref[...] = tall(jnp.concatenate([*siblings, leaf_ref[0], from_top], axis=1))


def permuted_labels(order, labels_ref):
    n = labels_ref.shape[0]
    group = n // BITS
    which = jnp.zeros_like(order)
    place = jnp.ones(order.shape, F32)
    for g in range(1, BITS):
        beyond = order >= g * group
        which = jnp.where(beyond, g * group, which)
        place = jnp.where(beyond, 1.0 / (1 << g), place)
    rows = jnp.concatenate([(order - which).astype(F32), place, jnp.zeros((6, n), F32)], axis=0)
    packed = jnp.zeros((group, OUT), F32)
    for g in range(BITS):
        packed = packed + labels_ref[g * group : (g + 1) * group, :].astype(F32) * float(1 << g)
    packed = packed.astype(BF16)
    lane = lax.broadcasted_iota(jnp.int32, (BLOCK, group), 1).astype(F32)
    for j in range(n // BLOCK):
        columns = rows[:, j * BLOCK : (j + 1) * BLOCK].T
        chosen = jnp.where(columns[:, 0:1] == lane, 1.0, 0.0).astype(BF16)
        value = jnp.dot(chosen, packed, preferred_element_type=F32) * columns[:, 1:2]
        value = jnp.floor(value)
        yield value - 2.0 * jnp.floor(0.5 * value)


def finish_body(scale, *refs):
    first = len(refs) == 13
    if first:
        sum_hbm, w_hbm, order_ref, labels_hbm, near_ref, base_ref, targets_hbm = refs[:7]
        sum_ref, w_ref, labels_ref, targets_ref, sems, sent = refs[7:13]
        pairs = [(labels_hbm, labels_ref), (w_hbm, w_ref), (sum_hbm, sum_ref)]
    else:
        sum_hbm, w_hbm, targets_hbm, near_ref, base_ref, sum_ref, w_ref, targets_ref, sems = refs
        pairs = [(sum_hbm, sum_ref), (w_hbm, w_ref), (targets_hbm, targets_ref)]
    loads = [pltpu.make_async_copy(a, b, sems.at[i]) for i, (a, b) in enumerate(pairs)]
    for load in loads:
        load.start()
    n = near_ref.shape[0]
    blocks = [slice(j, j + BLOCK) for j in range(0, n, BLOCK)]
    if first:
        loads[0].wait()
        for rows, found in zip(blocks, permuted_labels(order_ref[...], labels_ref)):
            targets_ref[rows, :] = found
        send = pltpu.make_async_copy(targets_ref, targets_hbm, sent)
        send.start()
    for load in loads[1:] if first else loads:
        load.wait()
    for rows in blocks:
        base_ref[rows, :] = w_ref[rows, :] + targets_ref[rows, :]
        near_ref[rows, :] = sum_ref[:, rows].T * scale
    if first:
        send.wait()


def turn_body(w_hbm, wt_hbm, w_ref, wt_ref, w_sem, wt_sem):
    n = w_hbm.shape[0]
    parts = [slice(j, j + GROUP * BLOCK) for j in range(0, n, GROUP * BLOCK)]
    loads = [pltpu.make_async_copy(w_hbm.at[p], w_ref.at[p], w_sem.at[j]) for j, p in enumerate(parts)]
    sends = [
        pltpu.make_async_copy(wt_ref.at[:, p], wt_hbm.at[:, p], wt_sem.at[j]) for j, p in enumerate(parts)
    ]
    for load in loads:
        load.start()
    for part, load, send in zip(parts, loads, sends):
        load.wait()
        for j in range(part.start, part.stop, BLOCK):
            wt_ref[:, j : j + BLOCK] = tall(w_ref[j : j + BLOCK, :].T)
        send.start()
    for send in sends:
        send.wait()


def near_body(
    turned, coords_ref, w_hbm, near_hbm, k_ref, sum_ref, own_ref, points_ref, wt_ref, columns_ref, w_sem, near_sem, *w_own
):
    n = coords_ref.shape[1]
    blocks = n // BLOCK
    wrap = (REACH - 1) * BLOCK
    fetch = pltpu.make_async_copy(w_hbm, wt_ref.at[:, 0:n] if turned else w_own[0], w_sem)
    fetch.start()
    points_ref[0:3, 0:n] = coords_ref[...] * LOG2E
    points_ref[3:, 0:n] = jnp.zeros((5, n), F32)
    points_ref[:, n:] = points_ref[:, 0:wrap]
    sum_ref[...] = jnp.zeros_like(sum_ref)

    for j in range(blocks):
        cols = slice(j * BLOCK, (j + 1) * BLOCK)
        columns_ref[cols, :] = points_ref[:, cols].T

    def place(i, slot):
        for k in range(3):
            own_ref[slot, k] = jnp.broadcast_to(
                columns_ref[pl.ds(pl.multiple_of(i * BLOCK, BLOCK), BLOCK), k : k + 1], (BLOCK, OUT)
            )

    def build(at, slot, d):
        for cols in (slice(c, c + OUT) for c in range(d * BLOCK, (d + 1) * BLOCK, OUT)):
            other = [points_ref[k : k + 1, pl.ds(at + cols.start, OUT)] for k in range(3)]
            for t in range(BLOCK // TILE):
                sub = slice(t * TILE, (t + 1) * TILE)
                diff_sq = None
                for k in range(3):
                    delta = own_ref[slot, k, sub, :] - other[k]
                    diff_sq = delta * delta if diff_sq is None else diff_sq + delta * delta
                dist = diff_sq * lax.rsqrt(jnp.maximum(diff_sq, 1e-37))
                k_ref[slot, 0, sub, cols], k_ref[slot, 1, sub, cols] = split(jnp.exp2(-dist))

    def product(w, hi, lo, contract):
        dims = (((1,), (contract,)), ((), ()))
        a = lax.dot_general(w, hi, dims, preferred_element_type=F32)
        b = lax.dot_general(w[:OUT], lo, dims, preferred_element_type=F32)
        return a[:OUT] + (a[OUT:] + b)

    def use(at, slot, d, count):
        cols = slice(d * BLOCK, (d + count) * BLOCK)
        where = pl.ds(at + d * BLOCK, count * BLOCK)
        part = product(wt_ref[:, where], k_ref[slot, 0, :, cols], k_ref[slot, 1, :, cols], 1)
        if d:
            sum_ref[:, where] += product(
                wt_ref[:, pl.ds(at, BLOCK)], k_ref[slot, 0, :, cols], k_ref[slot, 1, :, cols], 0
            )
        return part

    def finish(at, parts):
        sum_ref[:, pl.ds(at, BLOCK)] += functools.reduce(jnp.add, parts)

    def pair(p, carry):
        for slot in range(2):
            prev = pl.multiple_of((2 * p + slot) * BLOCK, BLOCK)
            at = pl.multiple_of(prev + BLOCK, BLOCK)
            place(lax.rem(2 * p + slot + 2, blocks), slot)
            total = None
            for d in range(REACH):
                part = use(prev, slot, d, 1)
                total = part if total is None else total + part
                build(at, 1 - slot, d)
            finish(prev, [total])
        return carry

    place(0, 0)
    place(1, 1)
    for d in range(REACH):
        build(0, 0, d)
    fetch.wait()
    if not turned:
        for j in range(blocks):
            cols = slice(j * BLOCK, (j + 1) * BLOCK)
            wt_ref[:, cols] = tall(w_own[0][cols, :].T)
    wt_ref[:, n:] = wt_ref[:, 0:wrap]
    lax.fori_loop(0, (blocks - 1) // 2, pair, 0)
    last = (blocks - 1) * BLOCK
    parts = [slice(wrap, last), slice(0, wrap), slice(last, n)]
    sends = [
        pltpu.make_async_copy(sum_ref.at[:, p], near_hbm.at[:, p], near_sem.at[j]) for j, p in enumerate(parts)
    ]
    sends[0].start()
    finish(last, [use(last, 0, 0, 1), use(last, 0, 1, REACH - 1)])
    sum_ref[:, 0:wrap] += sum_ref[:, n:]
    sends[1].start()
    sends[2].start()
    for send in sends:
        send.wait()


def middle_body(own_ref, m1_ref, m2_ref, m3_ref, out_ref):
    tail = slice(RANK, RANK + 2 * QROWS)
    total = (own_ref[...] + m1_ref[tail, :]) + (m2_ref[tail, :] + m3_ref[tail, :])
    out_ref[...] = jnp.broadcast_to(total[None], out_ref.shape)


def couple_body(got_ref, couple_ref, g1_ref, s2_ref, spread_ref):
    s2 = jnp.zeros((QROWS, OUT), F32)
    for m in range(N_MID):
        spread_ref[m * RANK : (m + 1) * RANK, :] = wide(expand_packed(got_ref[m, 0:QROWS, :]))
        s2 = s2 + got_ref[m, QROWS:, :]
    g1_ref[...] = fold_and_pack(dot3(couple_ref[...], spread_ref[...]))
    s2_ref[...] = s2


def update_body(last, *refs):
    near_ref, messages, down_ref, tops = refs[0], refs[1:4], refs[4], refs[5:9]
    base_ref, bcat_ref = refs[9:11]
    if last:
        out_hbm, out_ref, out_sem = refs[11:]
    else:
        basis_t_ref, up_ref, out_hbm, own_ref = refs[11:15]
        message_refs = refs[15:18]
        out_ref, out_sem, whl_ref = refs[18:]
    blocks = [slice(j, j + BLOCK) for j in range(0, base_ref.shape[0], BLOCK)]
    parts = [slice(j, j + GROUP * BLOCK) for j in range(0, base_ref.shape[0], GROUP * BLOCK)]
    own = lax.axis_index("leaf")
    quarters = [lax.rem(own + N_LEAF - k, N_LEAF) for k in range(N_LEAF)]
    g1 = unpack_quarters([ref[0:QROWS, :] for ref in tops], quarters)
    s2 = unpack_quarters([ref[QROWS:, :] for ref in tops], quarters)
    skeletons = [ref[0:RANK, :] for ref in messages] + [g1, s2]
    g0 = dot3(down_ref[...], wide(jnp.concatenate(skeletons, axis=0)))
    hi, lo = split(g0)
    rhs = jnp.concatenate(
        [jnp.concatenate([hi, lo], axis=1), jnp.concatenate([hi, jnp.zeros_like(lo)], axis=1)], axis=0
    )
    sends = []
    for j, part in enumerate(parts):
        for rows in blocks[j * GROUP : (j + 1) * GROUP]:
            f = jnp.dot(bcat_ref[rows, :], rhs, preferred_element_type=F32)
            f = near_ref[rows, :] + (f[:, :OUT] + f[:, OUT:])
            new = base_ref[rows, :] - (0.5 * jnp.tanh(0.5 * f) + 0.5)
            out_ref[rows, :] = new
            if not last:
                whl_ref[rows, :] = wide(new)
        sends.append(pltpu.make_async_copy(out_ref.at[part], out_hbm.at[part], out_sem.at[j]))
        sends[j].start()
    if not last:
        s0 = dot3(tall(basis_t_ref[...]), whl_ref[...])
        emit_messages(s0, up_ref[...], own_ref, message_refs)
    for send in sends:
        send.wait()


def params(mib):
    return pltpu.CompilerParams(vmem_limit_bytes=mib << 20)


def shape(*dims, dtype=F32):
    return jax.ShapeDtypeStruct(dims, dtype)


def ring(k):
    return [(i, (i + k) % N_LEAF) for i in range(N_LEAF)]


def call(body, out, operands, mib, name, scratch=(), work=(0, 0, 0), far_in=(), far_out=()):
    out = [pltpu.HBM(o.shape, o.dtype) if i in far_out else o for i, o in enumerate(out)]
    operands = [
        pltpu.with_memory_space_constraint(x, pltpu.HBM) if i in far_in else x
        for i, x in enumerate(operands)
    ]
    return pl.pallas_call(
        body,
        out_shape=out,
        in_specs=[HBM if i in far_in else VMEM for i in range(len(operands))],
        out_specs=[HBM if i in far_out else VMEM for i in range(len(out))],
        scratch_shapes=scratch,
        compiler_params=params(mib),
        cost_estimate=pl.CostEstimate(flops=work[0], bytes_accessed=work[1], transcendentals=work[2]),
        name=name,
    )(*operands)


def on_device(
    coords,
    weights,
    labels,
    order,
    basis,
    transfer_leaf,
    transfer_mid,
    couple_leaf,
    couple_mid,
    couple_top,
):
    n = weights.shape[0]
    scale = 4.0 / math.sqrt(n)
    basis_t = basis.T
    groups = n // (GROUP * BLOCK)
    wide_n = n + (REACH - 1) * BLOCK
    message_shapes = [shape(2 * QROWS, OUT)] + [shape(RANK + 2 * QROWS, OUT)] * 3

    up, own, *messages = call(
        first_body,
        [shape(RANK, 2 * RANK), *message_shapes],
        (basis_t, weights, transfer_leaf, transfer_mid),
        58,
        "first",
    )
    bcat, couple, down = call(
        prepare_body,
        [
            shape(n, 2 * RANK, dtype=BF16),
            shape(2 * RANK, N_MID * RANK, dtype=BF16),
            shape(2 * RANK, 5 * RANK, dtype=BF16),
        ],
        (basis_t, transfer_leaf, transfer_mid, couple_leaf, couple_mid, couple_top),
        58,
        "prepare",
    )
    own, couple = lax.optimization_barrier((own, couple))

    current = weights
    for step in range(STEPS):
        last = step == STEPS - 1
        if step:
            (w_near,) = call(
                turn_body,
                [shape(2 * OUT, n, dtype=BF16)],
                (current,),
                8,
                "turn",
                [
                    pltpu.VMEM((n, OUT), F32),
                    pltpu.VMEM((2 * OUT, n), BF16),
                    pltpu.SemaphoreType.DMA((groups,)),
                    pltpu.SemaphoreType.DMA((groups,)),
                ],
                (0, n * OUT * 8, 0),
                (0,),
                (0,),
            )
            own, w_near = lax.optimization_barrier((own, w_near))
        else:
            w_near = current
        (near_t,) = call(
            functools.partial(near_body, bool(step)),
            [shape(OUT, n)],
            (coords, w_near),
            20,
            "near",
            [
                pltpu.VMEM((2, 2, BLOCK, REACH * BLOCK), BF16),
                pltpu.VMEM((OUT, wide_n), F32),
                pltpu.VMEM((2, 3, BLOCK, OUT), F32),
                pltpu.VMEM((8, wide_n), F32),
                pltpu.VMEM((2 * OUT, wide_n), BF16),
                pltpu.VMEM((n, 8), F32),
                pltpu.SemaphoreType.DMA,
                pltpu.SemaphoreType.DMA((3,)),
            ]
            + ([] if step else [pltpu.VMEM((n, OUT), F32)]),
            (6 * n * n * OUT, n * OUT * 12, n * n),
            (1,),
            (0,),
        )
        messages = [lax.ppermute(m, "leaf", ring(k)) for k, m in enumerate(messages, 1)]
        (spread,) = call(middle_body, [shape(N_MID, 2 * QROWS, OUT)], (own, *messages), 4, "middle")
        got = lax.all_to_all(spread, "mid", 0, 0)
        got, near_t = lax.optimization_barrier((got, near_t))
        g1, s2 = call(
            couple_body,
            [shape(QROWS, OUT)] * 2,
            (got, couple),
            8,
            "couple",
            [pltpu.VMEM((N_MID * RANK, 2 * OUT), BF16)],
        )
        s2 = lax.ppermute(s2, "top", [(0, 1), (1, 0)])
        top = jnp.concatenate([g1, s2], axis=0)
        tops = [top] + [lax.ppermute(top, "leaf", ring(k)) for k in (1, 2, 3)]
        kept = [pltpu.VMEM((OUT, n), F32), pltpu.VMEM((n, OUT), F32)]
        if step:
            near, base = call(
                functools.partial(finish_body, scale),
                [shape(n, OUT)] * 2,
                (near_t, current, targets),
                8,
                "finish",
                [*kept, pltpu.VMEM((n, OUT), F32), pltpu.SemaphoreType.DMA((3,))],
                (n * OUT, n * OUT * 20, 0),
                (0, 1, 2),
            )
        else:
            near, base, targets = call(
                functools.partial(finish_body, scale),
                [shape(n, OUT)] * 3,
                (near_t, current, order, labels),
                12,
                "finish",
                [
                    *kept,
                    pltpu.VMEM((n, OUT), jnp.int32),
                    pltpu.VMEM((n, OUT), F32),
                    pltpu.SemaphoreType.DMA((3,)),
                    pltpu.SemaphoreType.DMA,
                ],
                (n * n // BITS * 2 * OUT, n * OUT * 24, 0),
                (0, 1, 3),
                (2,),
            )
        far = (near, *messages, down, *tops, base, bcat)
        rows_buffer = [pltpu.VMEM((n, OUT), F32), pltpu.SemaphoreType.DMA((groups,))]
        body = functools.partial(update_body, last)
        if last:
            (current,) = call(
                body, [shape(n, OUT)], far, 8, "last", rows_buffer, far_out=(0,)
            )
        else:
            current, own, *messages = call(
                body,
                [shape(n, OUT), *message_shapes],
                (*far, basis_t, up),
                12,
                "update",
                [*rows_buffer, pltpu.VMEM((n, 2 * OUT), BF16)],
                far_out=(0,),
            )
    return current


def solution(mesh):
    placed = (
        P(None, ("top", "mid", "leaf")),
        P(("top", "mid", "leaf"), None),
        P(("top", "mid", "leaf"), None),
        P(("top", "mid", "leaf"), None),
        P(("top", "mid", "leaf"), None),
        P(("top", "mid", "leaf"), None, None),
        P(("top", "mid"), None, None),
        P(("top", "mid", "leaf"), None, None, None),
        P(("top", "mid"), None, None, None),
        P("top", None, None, None),
    )
    return jax.shard_map(
        on_device,
        mesh=mesh,
        in_specs=placed,
        out_specs=P(("top", "mid", "leaf"), None),
        check_vma=False,
    )
```

```python
import functools
import math

import jax
import jax.numpy as jnp
from jax import lax
from jax.experimental import pallas as pl
from jax.experimental.pallas import tpu as pltpu
from jax.sharding import PartitionSpec as P

STEPS = 2
RANK = 64
OUT = 128
N_MID = 32
N_LEAF = 4
QROWS = RANK // N_LEAF
QCOLS = OUT // N_LEAF
HP = lax.Precision.HIGHEST
F32 = jnp.float32
BF16 = jnp.bfloat16
LOG2E = math.log2(math.e)
BLOCK = 256
REACH = 5
BITS = 8
GROUP = 3
DEPTH = 3
TILE = 32
VMEM = pl.BlockSpec(memory_space=pltpu.VMEM)
HBM = pl.BlockSpec(memory_space=pltpu.HBM)


def split(x):
    hi = x.astype(BF16)
    return hi, (x - hi.astype(F32)).astype(BF16)


def wide(x):
    return jnp.concatenate(split(x), axis=1)


def dot3(tall, wide_rhs):
    d = jnp.dot(tall, wide_rhs, preferred_element_type=F32)
    m, n = d.shape[0] // 2, d.shape[1] // 2
    return d[:m, :n] + (d[:m, n:] + d[m:, :n])


def lane_group():
    return lax.broadcasted_iota(jnp.int32, (QROWS, OUT), 1) // QCOLS


def pack_quarter(full, quarter):
    group = lane_group()
    out = jnp.zeros((QROWS, OUT), F32)
    for k in range(N_LEAF):
        moved = pltpu.roll(
            full[k * QROWS : (k + 1) * QROWS], lax.rem((k - quarter + N_LEAF) * QCOLS, OUT), 1
        )
        out = jnp.where(group == k, moved, out)
    return out


def expand_packed(packed):
    group = lane_group()
    zero = jnp.zeros((QROWS, OUT), F32)
    return jnp.concatenate([jnp.where(group == k, packed, zero) for k in range(N_LEAF)], axis=0)


def fold_and_pack(grouped):
    both = grouped + pltpu.roll(grouped, 2 * QCOLS, 1)
    total = both + pltpu.roll(both, QCOLS, 1)
    group = lane_group()
    out = jnp.zeros((QROWS, OUT), F32)
    for k in range(N_LEAF):
        out = jnp.where(group == k, total[k * QROWS : (k + 1) * QROWS], out)
    return out


def unpack_quarters(packed, quarters):
    group = lane_group()
    rows = []
    for k in range(N_LEAF):
        out = jnp.zeros((QROWS, OUT), F32)
        for block, quarter in zip(packed, quarters):
            moved = pltpu.roll(block, lax.rem((quarter - k + N_LEAF) * QCOLS, OUT), 1)
            out = jnp.where(group == quarter, moved, out)
        rows.append(out)
    return jnp.concatenate(rows, axis=0)


def tall(x):
    return jnp.concatenate(split(x), axis=0)


def dot_rows(lhs, rhs):
    return lax.dot_general(
        lhs, rhs, (((0,), (0,)), ((), ())), precision=HP, preferred_element_type=F32
    )


def emit_messages(s0, up, own_ref, message_refs):
    own = lax.axis_index("leaf")
    both = dot_rows(up, s0)

    def quarter(q):
        return jnp.concatenate([pack_quarter(both[:RANK], q), pack_quarter(both[RANK:], q)], axis=0)

    own_ref[...] = quarter(own)
    for k, ref in enumerate(message_refs, 1):
        ref[0:RANK, :] = s0
        ref[RANK:, :] = quarter(lax.rem(own + k, N_LEAF))


def first_body(basis_t_ref, w_ref, leaf_ref, mid_ref, up_ref, own_ref, *message_refs):
    through = jnp.dot(leaf_ref[0], mid_ref[0], precision=HP, preferred_element_type=F32)
    up_ref[...] = jnp.concatenate([leaf_ref[0], through], axis=1)
    s0 = dot3(tall(basis_t_ref[...]), wide(w_ref[...]))
    emit_messages(s0, up_ref[...], own_ref, message_refs)


def prepare_body(
    basis_t_ref, leaf_ref, mid_ref, couple_leaf_ref, couple_mid_ref, couple_top_ref,
    bcat_ref, couple_ref, down_ref,
):
    n = basis_t_ref.shape[1]
    for j in range(n // BLOCK):
        cols = slice(j * BLOCK, (j + 1) * BLOCK)
        bcat_ref[cols, :] = wide(basis_t_ref[:, cols].T)
    own_mid, own_leaf = lax.axis_index("mid"), lax.axis_index("leaf")
    for m in range(N_MID // 2):
        pair = [
            jnp.where(own_mid == i, 0.0, couple_mid_ref[0, i]) for i in (2 * m, 2 * m + 1)
        ]
        couple_ref[:, m * OUT : (m + 1) * OUT] = tall(jnp.concatenate(pair, axis=1))
    other = 1 - lax.axis_index("top")
    from_top = jnp.dot(mid_ref[0], couple_top_ref[0, other], precision=HP, preferred_element_type=F32)
    from_top = jnp.dot(leaf_ref[0], from_top, precision=HP, preferred_element_type=F32)
    siblings = [couple_leaf_ref[0, lax.rem(own_leaf + N_LEAF - k, N_LEAF)] for k in (1, 2, 3)]
    down_ref[...] = tall(jnp.concatenate([*siblings, leaf_ref[0], from_top], axis=1))


def permuted_labels(order, labels_ref):
    n = labels_ref.shape[0]
    group = n // BITS
    which = jnp.zeros_like(order)
    place = jnp.ones(order.shape, F32)
    for g in range(1, BITS):
        beyond = order >= g * group
        which = jnp.where(beyond, g * group, which)
        place = jnp.where(beyond, 1.0 / (1 << g), place)
    rows = jnp.concatenate([(order - which).astype(F32), place, jnp.zeros((6, n), F32)], axis=0)
    packed = jnp.zeros((group, OUT), F32)
    for g in range(BITS):
        packed = packed + labels_ref[g * group : (g + 1) * group, :].astype(F32) * float(1 << g)
    packed = packed.astype(BF16)
    lane = lax.broadcasted_iota(jnp.int32, (BLOCK, group), 1).astype(F32)
    for j in range(n // BLOCK):
        columns = rows[:, j * BLOCK : (j + 1) * BLOCK].T
        chosen = jnp.where(columns[:, 0:1] == lane, 1.0, 0.0).astype(BF16)
        value = jnp.dot(chosen, packed, preferred_element_type=F32) * columns[:, 1:2]
        value = jnp.floor(value)
        yield value - 2.0 * jnp.floor(0.5 * value)


def finish_body(scale, *refs):
    first = len(refs) == 13
    if first:
        sum_hbm, w_hbm, order_ref, labels_hbm, near_ref, base_ref, targets_hbm = refs[:7]
        sum_ref, w_ref, labels_ref, targets_ref, sems, sent = refs[7:13]
        pairs = [(labels_hbm, labels_ref), (w_hbm, w_ref), (sum_hbm, sum_ref)]
    else:
        sum_hbm, w_hbm, targets_hbm, near_ref, base_ref, sum_ref, w_ref, targets_ref, sems = refs
        pairs = [(sum_hbm, sum_ref), (w_hbm, w_ref), (targets_hbm, targets_ref)]
    loads = [pltpu.make_async_copy(a, b, sems.at[i]) for i, (a, b) in enumerate(pairs)]
    for load in loads:
        load.start()
    n = near_ref.shape[0]
    blocks = [slice(j, j + BLOCK) for j in range(0, n, BLOCK)]
    if first:
        loads[0].wait()
        for rows, found in zip(blocks, permuted_labels(order_ref[...], labels_ref)):
            targets_ref[rows, :] = found
        send = pltpu.make_async_copy(targets_ref, targets_hbm, sent)
        send.start()
    for load in loads[1:] if first else loads:
        load.wait()
    for rows in blocks:
        base_ref[rows, :] = w_ref[rows, :] + targets_ref[rows, :]
        near_ref[rows, :] = sum_ref[:, rows].T * scale
    if first:
        send.wait()


def turn_body(w_hbm, wt_hbm, w_ref, wt_ref, w_sem, wt_sem):
    n = w_hbm.shape[0]
    parts = [slice(j, j + GROUP * BLOCK) for j in range(0, n, GROUP * BLOCK)]
    loads = [pltpu.make_async_copy(w_hbm.at[p], w_ref.at[p], w_sem.at[j]) for j, p in enumerate(parts)]
    sends = [
        pltpu.make_async_copy(wt_ref.at[:, p], wt_hbm.at[:, p], wt_sem.at[j]) for j, p in enumerate(parts)
    ]
    for load in loads:
        load.start()
    for part, load, send in zip(parts, loads, sends):
        load.wait()
        for j in range(part.start, part.stop, BLOCK):
            wt_ref[:, j : j + BLOCK] = tall(w_ref[j : j + BLOCK, :].T)
        send.start()
    for send in sends:
        send.wait()


def product(w, hi, lo, contract):
    dims = (((1,), (contract,)), ((), ()))
    a = lax.dot_general(w, hi, dims, preferred_element_type=F32)
    b = lax.dot_general(w[:OUT], lo, dims, preferred_element_type=F32)
    return a[:OUT] + (a[OUT:] + b)


def use_block(wt_ref, k_ref, sum_ref, at, slot, d, count):
    cols = slice(d * BLOCK, (d + count) * BLOCK)
    where = pl.ds(at + d * BLOCK, count * BLOCK)
    hi, lo = k_ref[slot, 0, :, cols], k_ref[slot, 1, :, cols]
    part = product(wt_ref[:, where], hi, lo, 1)
    if d:
        sum_ref[:, where] += product(wt_ref[:, pl.ds(at, BLOCK)], hi, lo, 0)
    return part


def use_row(wt_ref, k_ref, sum_ref, at, slot):
    part = use_block(wt_ref, k_ref, sum_ref, at, slot, 0, 1)
    part = part + use_block(wt_ref, k_ref, sum_ref, at, slot, 1, REACH - 1)
    sum_ref[:, pl.ds(at, BLOCK)] += part


def send_sums(sum_ref, near_hbm, near_sem, use_last):
    n = near_hbm.shape[1]
    wrap, last = (REACH - 1) * BLOCK, n - BLOCK
    parts = [slice(wrap, last), slice(0, wrap), slice(last, n)]
    sends = [
        pltpu.make_async_copy(sum_ref.at[:, p], near_hbm.at[:, p], near_sem.at[j]) for j, p in enumerate(parts)
    ]
    sends[0].start()
    use_last()
    sum_ref[:, 0:wrap] += sum_ref[:, n:]
    sends[1].start()
    sends[2].start()
    for send in sends:
        send.wait()


def build_body(
    coords_ref, w_hbm, near_hbm, k_hbm, k_ref, sum_ref, own_ref, points_ref, wt_ref, columns_ref, w_ref, w_sem, near_sem,
    k_sem,
):
    n = coords_ref.shape[1]
    blocks = n // BLOCK
    wrap = (REACH - 1) * BLOCK
    fetch = pltpu.make_async_copy(w_hbm, w_ref, w_sem)
    fetch.start()
    points_ref[0:3, 0:n] = coords_ref[...] * LOG2E
    points_ref[3:, 0:n] = jnp.zeros((5, n), F32)
    points_ref[:, n:] = points_ref[:, 0:wrap]
    sum_ref[...] = jnp.zeros_like(sum_ref)
    for j in range(blocks):
        cols = slice(j * BLOCK, (j + 1) * BLOCK)
        columns_ref[cols, :] = points_ref[:, cols].T

    def place(i, slot):
        for k in range(3):
            own_ref[slot, k] = jnp.broadcast_to(
                columns_ref[pl.ds(pl.multiple_of(i * BLOCK, BLOCK), BLOCK), k : k + 1], (BLOCK, OUT)
            )

    def build(at, slot, d):
        for cols in (slice(c, c + OUT) for c in range(d * BLOCK, (d + 1) * BLOCK, OUT)):
            other = [points_ref[k : k + 1, pl.ds(at + cols.start, OUT)] for k in range(3)]
            for t in range(BLOCK // TILE):
                sub = slice(t * TILE, (t + 1) * TILE)
                diff_sq = None
                for k in range(3):
                    delta = own_ref[slot, k, sub, :] - other[k]
                    diff_sq = delta * delta if diff_sq is None else diff_sq + delta * delta
                dist = diff_sq * lax.rsqrt(jnp.maximum(diff_sq, 1e-37))
                k_ref[slot, 0, sub, cols], k_ref[slot, 1, sub, cols] = split(jnp.exp2(-dist))

    def keep(i, slot):
        return pltpu.make_async_copy(k_ref.at[slot], k_hbm.at[i], k_sem.at[slot])

    def step(i, slot, free):
        prev = pl.multiple_of(i * BLOCK, BLOCK)
        at = pl.multiple_of(prev + BLOCK, BLOCK)
        if not free:
            keep(i - 1, 1 - slot).wait()
        place(lax.rem(i + 2, blocks), slot)
        total = None
        for d in range(REACH):
            part = use_block(wt_ref, k_ref, sum_ref, prev, slot, d, 1)
            total = part if total is None else total + part
            build(at, 1 - slot, d)
        sum_ref[:, pl.ds(prev, BLOCK)] += total
        keep(i + 1, 1 - slot).start()

    place(0, 0)
    place(1, 1)
    for d in range(REACH):
        build(0, 0, d)
    keep(0, 0).start()
    fetch.wait()
    for j in range(blocks):
        cols = slice(j * BLOCK, (j + 1) * BLOCK)
        wt_ref[:, cols] = tall(w_ref[cols, :].T)
    wt_ref[:, n:] = wt_ref[:, 0:wrap]
    step(0, 0, True)
    step(1, 1, False)

    def pair(p, carry):
        step(2 * p, 0, False)
        step(2 * p + 1, 1, False)
        return carry

    lax.fori_loop(1, (blocks - 1) // 2, pair, 0)
    send_sums(
        sum_ref, near_hbm, near_sem, lambda: use_row(wt_ref, k_ref, sum_ref, (blocks - 1) * BLOCK, 0)
    )
    keep(blocks - 2, 1).wait()
    keep(blocks - 1, 0).wait()


def near_body(w_hbm, k_hbm, near_hbm, k_ref, sum_ref, wt_ref, w_sem, near_sem, k_sem):
    n = w_hbm.shape[1]
    blocks = n // BLOCK

    def load(i, slot):
        return pltpu.make_async_copy(k_hbm.at[i], k_ref.at[slot], k_sem.at[slot])

    fetch = pltpu.make_async_copy(w_hbm, wt_ref.at[:, 0:n], w_sem)
    fetch.start()
    for i in range(DEPTH - 1):
        load(i, i).start()
    sum_ref[...] = jnp.zeros_like(sum_ref)
    fetch.wait()
    wt_ref[:, n:] = wt_ref[:, 0 : (REACH - 1) * BLOCK]

    def several(p, carry):
        for slot in range(DEPTH):
            i = DEPTH * p + slot
            load(i + DEPTH - 1, (slot + DEPTH - 1) % DEPTH).start()
            load(i, slot).wait()
            use_row(wt_ref, k_ref, sum_ref, pl.multiple_of(i * BLOCK, BLOCK), slot)
        return carry

    lax.fori_loop(0, blocks // DEPTH - 1, several, 0)
    for i in range(blocks - DEPTH, blocks - 1):
        slot = i % DEPTH
        if i + DEPTH - 1 < blocks:
            load(i + DEPTH - 1, (slot + DEPTH - 1) % DEPTH).start()
        load(i, slot).wait()
        use_row(wt_ref, k_ref, sum_ref, i * BLOCK, slot)
    load(blocks - 1, (blocks - 1) % DEPTH).wait()
    send_sums(
        sum_ref, near_hbm, near_sem,
        lambda: use_row(wt_ref, k_ref, sum_ref, (blocks - 1) * BLOCK, (blocks - 1) % DEPTH),
    )


def middle_body(own_ref, m1_ref, m2_ref, m3_ref, out_ref):
    tail = slice(RANK, RANK + 2 * QROWS)
    total = (own_ref[...] + m1_ref[tail, :]) + (m2_ref[tail, :] + m3_ref[tail, :])
    out_ref[...] = jnp.broadcast_to(total[None], out_ref.shape)


def couple_body(got_ref, couple_ref, g1_ref, s2_ref, spread_ref):
    s2 = jnp.zeros((QROWS, OUT), F32)
    for m in range(N_MID):
        spread_ref[m * RANK : (m + 1) * RANK, :] = wide(expand_packed(got_ref[m, 0:QROWS, :]))
        s2 = s2 + got_ref[m, QROWS:, :]
    g1_ref[...] = fold_and_pack(dot3(couple_ref[...], spread_ref[...]))
    s2_ref[...] = s2


def update_body(last, *refs):
    near_ref, messages, down_ref, tops = refs[0], refs[1:4], refs[4], refs[5:9]
    base_ref, bcat_ref = refs[9:11]
    if last:
        out_hbm, out_ref, out_sem = refs[11:]
    else:
        basis_t_ref, up_ref, out_hbm, own_ref = refs[11:15]
        message_refs = refs[15:18]
        out_ref, out_sem, whl_ref = refs[18:]
    blocks = [slice(j, j + BLOCK) for j in range(0, base_ref.shape[0], BLOCK)]
    parts = [slice(j, j + GROUP * BLOCK) for j in range(0, base_ref.shape[0], GROUP * BLOCK)]
    own = lax.axis_index("leaf")
    quarters = [lax.rem(own + N_LEAF - k, N_LEAF) for k in range(N_LEAF)]
    g1 = unpack_quarters([ref[0:QROWS, :] for ref in tops], quarters)
    s2 = unpack_quarters([ref[QROWS:, :] for ref in tops], quarters)
    skeletons = [ref[0:RANK, :] for ref in messages] + [g1, s2]
    g0 = dot3(down_ref[...], wide(jnp.concatenate(skeletons, axis=0)))
    hi, lo = split(g0)
    rhs = jnp.concatenate(
        [jnp.concatenate([hi, lo], axis=1), jnp.concatenate([hi, jnp.zeros_like(lo)], axis=1)], axis=0
    )
    sends = []
    for j, part in enumerate(parts):
        for rows in blocks[j * GROUP : (j + 1) * GROUP]:
            f = jnp.dot(bcat_ref[rows, :], rhs, preferred_element_type=F32)
            f = near_ref[rows, :] + (f[:, :OUT] + f[:, OUT:])
            new = base_ref[rows, :] - (0.5 * jnp.tanh(0.5 * f) + 0.5)
            out_ref[rows, :] = new
            if not last:
                whl_ref[rows, :] = wide(new)
        sends.append(pltpu.make_async_copy(out_ref.at[part], out_hbm.at[part], out_sem.at[j]))
        sends[j].start()
    if not last:
        s0 = dot3(tall(basis_t_ref[...]), whl_ref[...])
        emit_messages(s0, up_ref[...], own_ref, message_refs)
    for send in sends:
        send.wait()


def params(mib):
    return pltpu.CompilerParams(vmem_limit_bytes=mib << 20)


def shape(*dims, dtype=F32):
    return jax.ShapeDtypeStruct(dims, dtype)


def ring(k):
    return [(i, (i + k) % N_LEAF) for i in range(N_LEAF)]


def call(body, out, operands, mib, name, scratch=(), work=(0, 0, 0), far_in=(), far_out=()):
    out = [pltpu.HBM(o.shape, o.dtype) if i in far_out else o for i, o in enumerate(out)]
    operands = [
        pltpu.with_memory_space_constraint(x, pltpu.HBM) if i in far_in else x
        for i, x in enumerate(operands)
    ]
    return pl.pallas_call(
        body,
        out_shape=out,
        in_specs=[HBM if i in far_in else VMEM for i in range(len(operands))],
        out_specs=[HBM if i in far_out else VMEM for i in range(len(out))],
        scratch_shapes=scratch,
        compiler_params=params(mib),
        cost_estimate=pl.CostEstimate(flops=work[0], bytes_accessed=work[1], transcendentals=work[2]),
        name=name,
    )(*operands)


def on_device(
    coords,
    weights,
    labels,
    order,
    basis,
    transfer_leaf,
    transfer_mid,
    couple_leaf,
    couple_mid,
    couple_top,
):
    n = weights.shape[0]
    scale = 4.0 / math.sqrt(n)
    basis_t = basis.T
    groups = n // (GROUP * BLOCK)
    wide_n = n + (REACH - 1) * BLOCK
    message_shapes = [shape(2 * QROWS, OUT)] + [shape(RANK + 2 * QROWS, OUT)] * 3

    up, own, *messages = call(
        first_body,
        [shape(RANK, 2 * RANK), *message_shapes],
        (basis_t, weights, transfer_leaf, transfer_mid),
        58,
        "first",
    )
    bcat, couple, down = call(
        prepare_body,
        [
            shape(n, 2 * RANK, dtype=BF16),
            shape(2 * RANK, N_MID * RANK, dtype=BF16),
            shape(2 * RANK, 5 * RANK, dtype=BF16),
        ],
        (basis_t, transfer_leaf, transfer_mid, couple_leaf, couple_mid, couple_top),
        58,
        "prepare",
    )
    own, couple = lax.optimization_barrier((own, couple))

    current = weights
    for step in range(STEPS):
        last = step == STEPS - 1
        row_blocks = n // BLOCK
        sums = pltpu.VMEM((OUT, wide_n), F32)
        turned = pltpu.VMEM((2 * OUT, wide_n), BF16)
        if step:
            (w_turned,) = call(
                turn_body,
                [shape(2 * OUT, n, dtype=BF16)],
                (current,),
                8,
                "turn",
                [
                    pltpu.VMEM((n, OUT), F32),
                    pltpu.VMEM((2 * OUT, n), BF16),
                    pltpu.SemaphoreType.DMA((groups,)),
                    pltpu.SemaphoreType.DMA((groups,)),
                ],
                (0, n * OUT * 8, 0),
                (0,),
                (0,),
            )
            own, w_turned = lax.optimization_barrier((own, w_turned))
            (near_t,) = call(
                near_body,
                [shape(OUT, n)],
                (w_turned, kept_blocks),
                20,
                "near",
                [
                    pltpu.VMEM((DEPTH, 2, BLOCK, REACH * BLOCK), BF16),
                    sums,
                    turned,
                    pltpu.SemaphoreType.DMA,
                    pltpu.SemaphoreType.DMA((3,)),
                    pltpu.SemaphoreType.DMA((DEPTH,)),
                ],
                (6 * n * n * OUT, n * OUT * 12 + n * n * 2, 0),
                (0, 1),
                (0,),
            )
        else:
            near_t, kept_blocks = call(
                build_body,
                [shape(OUT, n), shape(row_blocks, 2, BLOCK, REACH * BLOCK, dtype=BF16)],
                (coords, current),
                20,
                "build",
                [
                    pltpu.VMEM((2, 2, BLOCK, REACH * BLOCK), BF16),
                    sums,
                    pltpu.VMEM((2, 3, BLOCK, OUT), F32),
                    pltpu.VMEM((8, wide_n), F32),
                    turned,
                    pltpu.VMEM((n, 8), F32),
                    pltpu.VMEM((n, OUT), F32),
                    pltpu.SemaphoreType.DMA,
                    pltpu.SemaphoreType.DMA((3,)),
                    pltpu.SemaphoreType.DMA((2,)),
                ],
                (6 * n * n * OUT, n * OUT * 12, n * n),
                (1,),
                (0, 1),
            )
        messages = [lax.ppermute(m, "leaf", ring(k)) for k, m in enumerate(messages, 1)]
        (spread,) = call(middle_body, [shape(N_MID, 2 * QROWS, OUT)], (own, *messages), 4, "middle")
        got = lax.all_to_all(spread, "mid", 0, 0)
        got, near_t = lax.optimization_barrier((got, near_t))
        g1, s2 = call(
            couple_body,
            [shape(QROWS, OUT)] * 2,
            (got, couple),
            8,
            "couple",
            [pltpu.VMEM((N_MID * RANK, 2 * OUT), BF16)],
        )
        s2 = lax.ppermute(s2, "top", [(0, 1), (1, 0)])
        top = jnp.concatenate([g1, s2], axis=0)
        tops = [top] + [lax.ppermute(top, "leaf", ring(k)) for k in (1, 2, 3)]
        kept = [pltpu.VMEM((OUT, n), F32), pltpu.VMEM((n, OUT), F32)]
        if step:
            near, base = call(
                functools.partial(finish_body, scale),
                [shape(n, OUT)] * 2,
                (near_t, current, targets),
                8,
                "finish",
                [*kept, pltpu.VMEM((n, OUT), F32), pltpu.SemaphoreType.DMA((3,))],
                (n * OUT, n * OUT * 20, 0),
                (0, 1, 2),
            )
        else:
            near, base, targets = call(
                functools.partial(finish_body, scale),
                [shape(n, OUT)] * 3,
                (near_t, current, order, labels),
                12,
                "finish",
                [
                    *kept,
                    pltpu.VMEM((n, OUT), jnp.int32),
                    pltpu.VMEM((n, OUT), F32),
                    pltpu.SemaphoreType.DMA((3,)),
                    pltpu.SemaphoreType.DMA,
                ],
                (n * n // BITS * 2 * OUT, n * OUT * 24, 0),
                (0, 1, 3),
                (2,),
            )
        far = (near, *messages, down, *tops, base, bcat)
        rows_buffer = [pltpu.VMEM((n, OUT), F32), pltpu.SemaphoreType.DMA((groups,))]
        body = functools.partial(update_body, last)
        if last:
            (current,) = call(
                body, [shape(n, OUT)], far, 8, "last", rows_buffer, far_out=(0,)
            )
        else:
            current, own, *messages = call(
                body,
                [shape(n, OUT), *message_shapes],
                (*far, basis_t, up),
                12,
                "update",
                [*rows_buffer, pltpu.VMEM((n, 2 * OUT), BF16)],
                far_out=(0,),
            )
    return current


def solution(mesh):
    placed = (
        P(None, ("top", "mid", "leaf")),
        P(("top", "mid", "leaf"), None),
        P(("top", "mid", "leaf"), None),
        P(("top", "mid", "leaf"), None),
        P(("top", "mid", "leaf"), None),
        P(("top", "mid", "leaf"), None, None),
        P(("top", "mid"), None, None),
        P(("top", "mid", "leaf"), None, None, None),
        P(("top", "mid"), None, None, None),
        P("top", None, None, None),
    )
    return jax.shard_map(
        on_device,
        mesh=mesh,
        in_specs=placed,
        out_specs=P(("top", "mid", "leaf"), None),
        check_vma=False,
    )
```

```python
import functools
import math

import jax
import jax.numpy as jnp
from jax import lax
from jax.experimental import pallas as pl
from jax.experimental.pallas import tpu as pltpu
from jax.sharding import PartitionSpec as P

STEPS = 2
RANK = 64
OUT = 128
N_MID = 32
N_LEAF = 4
QROWS = RANK // N_LEAF
QCOLS = OUT // N_LEAF
HP = lax.Precision.HIGHEST
F32 = jnp.float32
BF16 = jnp.bfloat16
LOG2E = math.log2(math.e)
BLOCK = 256
REACH = 5
BITS = 8
GROUP = 3
TILE = 32
VMEM = pl.BlockSpec(memory_space=pltpu.VMEM)
HBM = pl.BlockSpec(memory_space=pltpu.HBM)


def split(x):
    hi = x.astype(BF16)
    return hi, (x - hi.astype(F32)).astype(BF16)


def wide(x):
    return jnp.concatenate(split(x), axis=1)


def dot3(tall, wide_rhs):
    d = jnp.dot(tall, wide_rhs, preferred_element_type=F32)
    m, n = d.shape[0] // 2, d.shape[1] // 2
    return d[:m, :n] + (d[:m, n:] + d[m:, :n])


def lane_group():
    return lax.broadcasted_iota(jnp.int32, (QROWS, OUT), 1) // QCOLS


def pack_quarter(full, quarter):
    group = lane_group()
    out = jnp.zeros((QROWS, OUT), F32)
    for k in range(N_LEAF):
        moved = pltpu.roll(
            full[k * QROWS : (k + 1) * QROWS], lax.rem((k - quarter + N_LEAF) * QCOLS, OUT), 1
        )
        out = jnp.where(group == k, moved, out)
    return out


def expand_packed(packed):
    group = lane_group()
    zero = jnp.zeros((QROWS, OUT), F32)
    return jnp.concatenate([jnp.where(group == k, packed, zero) for k in range(N_LEAF)], axis=0)


def fold_and_pack(grouped):
    both = grouped + pltpu.roll(grouped, 2 * QCOLS, 1)
    total = both + pltpu.roll(both, QCOLS, 1)
    group = lane_group()
    out = jnp.zeros((QROWS, OUT), F32)
    for k in range(N_LEAF):
        out = jnp.where(group == k, total[k * QROWS : (k + 1) * QROWS], out)
    return out


def unpack_quarters(packed, quarters):
    group = lane_group()
    rows = []
    for k in range(N_LEAF):
        out = jnp.zeros((QROWS, OUT), F32)
        for block, quarter in zip(packed, quarters):
            moved = pltpu.roll(block, lax.rem((quarter - k + N_LEAF) * QCOLS, OUT), 1)
            out = jnp.where(group == quarter, moved, out)
        rows.append(out)
    return jnp.concatenate(rows, axis=0)


def tall(x):
    return jnp.concatenate(split(x), axis=0)


def dot_rows(lhs, rhs):
    return lax.dot_general(
        lhs, rhs, (((0,), (0,)), ((), ())), precision=HP, preferred_element_type=F32
    )


def emit_messages(s0, up, own_ref, message_refs):
    own = lax.axis_index("leaf")
    both = dot_rows(up, s0)

    def quarter(q):
        return jnp.concatenate([pack_quarter(both[:RANK], q), pack_quarter(both[RANK:], q)], axis=0)

    own_ref[...] = quarter(own)
    for k, ref in enumerate(message_refs, 1):
        ref[0:RANK, :] = s0
        ref[RANK:, :] = quarter(lax.rem(own + k, N_LEAF))


def first_body(basis_t_hbm, w_hbm, leaf_ref, mid_ref, up_ref, own_ref, *refs):
    message_refs, (basis_t_ref, w_ref, basis_sem, w_sem) = refs[:3], refs[3:]
    n = w_hbm.shape[0]
    parts = [slice(j, j + GROUP * BLOCK) for j in range(0, n, GROUP * BLOCK)]
    basis = pltpu.make_async_copy(basis_t_hbm, basis_t_ref, basis_sem)
    loads = [pltpu.make_async_copy(w_hbm.at[p], w_ref.at[p], w_sem.at[j]) for j, p in enumerate(parts)]
    for load in (basis, *loads):
        load.start()
    through = jnp.dot(leaf_ref[0], mid_ref[0], precision=HP, preferred_element_type=F32)
    up_ref[...] = jnp.concatenate([leaf_ref[0], through], axis=1)
    basis.wait()
    s0 = None
    for part, load in zip(parts, loads):
        load.wait()
        term = dot3(tall(basis_t_ref[:, part]), wide(w_ref[part, :]))
        s0 = term if s0 is None else s0 + term
    emit_messages(s0, up_ref[...], own_ref, message_refs)


def prepare_body(
    basis_t_hbm, leaf_ref, mid_ref, couple_leaf_ref, couple_mid_hbm, couple_top_ref, bcat_hbm, couple_hbm, down_ref,
    basis_t_ref, couple_mid_ref, bcat_ref, couple_ref, sems,
):
    n = basis_t_ref.shape[1]
    blocks_in = pltpu.make_async_copy(couple_mid_hbm, couple_mid_ref, sems.at[0])
    basis_in = pltpu.make_async_copy(basis_t_hbm, basis_t_ref, sems.at[1])
    couple_out = pltpu.make_async_copy(couple_ref, couple_hbm, sems.at[2])
    bcat_out = pltpu.make_async_copy(bcat_ref, bcat_hbm, sems.at[3])
    blocks_in.start()
    basis_in.start()
    own_mid, own_leaf = lax.axis_index("mid"), lax.axis_index("leaf")
    blocks_in.wait()
    for m in range(N_MID // 2):
        pair = [
            jnp.where(own_mid == i, 0.0, couple_mid_ref[0, i]) for i in (2 * m, 2 * m + 1)
        ]
        couple_ref[:, m * OUT : (m + 1) * OUT] = tall(jnp.concatenate(pair, axis=1))
    couple_out.start()
    basis_in.wait()
    for j in range(n // BLOCK):
        cols = slice(j * BLOCK, (j + 1) * BLOCK)
        bcat_ref[cols, :] = wide(basis_t_ref[:, cols].T)
    bcat_out.start()
    other = 1 - lax.axis_index("top")
    from_top = jnp.dot(mid_ref[0], couple_top_ref[0, other], precision=HP, preferred_element_type=F32)
    from_top = jnp.dot(leaf_ref[0], from_top, precision=HP, preferred_element_type=F32)
    siblings = [couple_leaf_ref[0, lax.rem(own_leaf + N_LEAF - k, N_LEAF)] for k in (1, 2, 3)]
    down_ref[...] = tall(jnp.concatenate([*siblings, leaf_ref[0], from_top], axis=1))
    couple_out.wait()
    bcat_out.wait()


def permute_labels(order, fetch, labels_ref, chosen_ref, bit_ref, out_ref):
    n = labels_ref.shape[0]
    group = n // BITS
    blocks = [slice(j, j + BLOCK) for j in range(0, n, BLOCK)]
    which = jnp.zeros_like(order)
    place = jnp.ones(order.shape, F32)
    for g in range(1, BITS):
        beyond = order >= g * group
        which = jnp.where(beyond, g * group, which)
        place = jnp.where(beyond, 1.0 / (1 << g), place)
    rows = jnp.concatenate([(order - which).astype(F32), place, jnp.zeros((6, n), F32)], axis=0)
    lane = lax.broadcasted_iota(jnp.int32, (BLOCK, group), 1).astype(F32)
    for at in blocks:
        columns = rows[:, at].T
        chosen_ref[at, :] = jnp.where(columns[:, 0:1] == lane, 1.0, 0.0).astype(BF16)
        bit_ref[at, :] = columns
    fetch.wait()
    packed = jnp.zeros((group, OUT), F32)
    for g in range(BITS):
        packed = packed + labels_ref[g * group : (g + 1) * group, :].astype(F32) * float(1 << g)
    packed = packed.astype(BF16)
    for at in blocks:
        value = jnp.dot(chosen_ref[at, :], packed, preferred_element_type=F32) * bit_ref[at, 1:2]
        value = jnp.floor(value)
        out_ref[at, :] = value - 2.0 * jnp.floor(0.5 * value)


def finish_body(scale, *refs):
    first = len(refs) == 15
    if first:
        sum_hbm, w_hbm, order_ref, labels_hbm, near_ref, base_ref, targets_hbm = refs[:7]
        sum_ref, w_ref, labels_ref, targets_ref, chosen_ref, bit_ref, sems, sent = refs[7:]
        pairs = [(labels_hbm, labels_ref), (sum_hbm, sum_ref), (w_hbm, w_ref)]
    else:
        sum_hbm, w_hbm, targets_hbm, near_ref, base_ref, sum_ref, w_ref, targets_ref, sems = refs
        pairs = [(sum_hbm, sum_ref), (w_hbm, w_ref), (targets_hbm, targets_ref)]
    loads = [pltpu.make_async_copy(a, b, sems.at[i]) for i, (a, b) in enumerate(pairs)]
    for load in loads:
        load.start()
    n = near_ref.shape[0]
    blocks = [slice(j, j + BLOCK) for j in range(0, n, BLOCK)]
    if first:
        permute_labels(order_ref[...], loads[0], labels_ref, chosen_ref, bit_ref, targets_ref)
        send = pltpu.make_async_copy(targets_ref, targets_hbm, sent)
        send.start()
        loads = loads[1:]
    loads[0].wait()
    for rows in blocks:
        near_ref[rows, :] = sum_ref[:, rows].T * scale
    for load in loads[1:]:
        load.wait()
    for rows in blocks:
        base_ref[rows, :] = w_ref[rows, :] + targets_ref[rows, :]
    if first:
        send.wait()


def turn_body(w_hbm, wt_hbm, w_ref, wt_ref, w_sem, wt_sem):
    n = w_hbm.shape[0]
    parts = [slice(j, j + GROUP * BLOCK) for j in range(0, n, GROUP * BLOCK)]
    loads = [pltpu.make_async_copy(w_hbm.at[p], w_ref.at[p], w_sem.at[j]) for j, p in enumerate(parts)]
    sends = [
        pltpu.make_async_copy(wt_ref.at[:, p], wt_hbm.at[:, p], wt_sem.at[j]) for j, p in enumerate(parts)
    ]
    for load in loads:
        load.start()
    for part, load, send in zip(parts, loads, sends):
        load.wait()
        for j in range(part.start, part.stop, BLOCK):
            wt_ref[:, j : j + BLOCK] = tall(w_ref[j : j + BLOCK, :].T)
        send.start()
    for send in sends:
        send.wait()


def near_body(
    turned, coords_ref, w_hbm, near_hbm, k_ref, sum_ref, own_ref, points_ref, wt_ref, columns_ref, w_sem, near_sem, *w_own
):
    n = coords_ref.shape[1]
    blocks = n // BLOCK
    wrap = (REACH - 1) * BLOCK
    fetch = pltpu.make_async_copy(w_hbm, wt_ref.at[:, 0:n] if turned else w_own[0], w_sem)
    fetch.start()
    points_ref[0:3, 0:n] = coords_ref[...] * LOG2E
    points_ref[3:, 0:n] = jnp.zeros((5, n), F32)
    points_ref[:, n:] = points_ref[:, 0:wrap]
    sum_ref[...] = jnp.zeros_like(sum_ref)

    for j in range(blocks):
        cols = slice(j * BLOCK, (j + 1) * BLOCK)
        columns_ref[cols, :] = points_ref[:, cols].T

    def place(i, slot):
        for k in range(3):
            own_ref[slot, k] = jnp.broadcast_to(
                columns_ref[pl.ds(pl.multiple_of(i * BLOCK, BLOCK), BLOCK), k : k + 1], (BLOCK, OUT)
            )

    def build(at, slot, d):
        for cols in (slice(c, c + OUT) for c in range(d * BLOCK, (d + 1) * BLOCK, OUT)):
            other = [points_ref[k : k + 1, pl.ds(at + cols.start, OUT)] for k in range(3)]
            for t in range(BLOCK // TILE):
                sub = slice(t * TILE, (t + 1) * TILE)
                diff_sq = None
                for k in range(3):
                    delta = own_ref[slot, k, sub, :] - other[k]
                    diff_sq = delta * delta if diff_sq is None else diff_sq + delta * delta
                dist = diff_sq * lax.rsqrt(jnp.maximum(diff_sq, 1e-37))
                k_ref[slot, 0, sub, cols], k_ref[slot, 1, sub, cols] = split(jnp.exp2(-dist))

    def product(w, hi, lo, contract):
        dims = (((1,), (contract,)), ((), ()))
        a = lax.dot_general(w, hi, dims, preferred_element_type=F32)
        b = lax.dot_general(w[:OUT], lo, dims, preferred_element_type=F32)
        return a[:OUT] + (a[OUT:] + b)

    def use(at, slot, d, count):
        cols = slice(d * BLOCK, (d + count) * BLOCK)
        where = pl.ds(at + d * BLOCK, count * BLOCK)
        part = product(wt_ref[:, where], k_ref[slot, 0, :, cols], k_ref[slot, 1, :, cols], 1)
        if d:
            sum_ref[:, where] += product(
                wt_ref[:, pl.ds(at, BLOCK)], k_ref[slot, 0, :, cols], k_ref[slot, 1, :, cols], 0
            )
        return part

    def finish(at, parts):
        sum_ref[:, pl.ds(at, BLOCK)] += functools.reduce(jnp.add, parts)

    def pair(p, carry):
        for slot in range(2):
            prev = pl.multiple_of((2 * p + slot) * BLOCK, BLOCK)
            at = pl.multiple_of(prev + BLOCK, BLOCK)
            place(lax.rem(2 * p + slot + 2, blocks), slot)
            total = None
            for d in range(REACH):
                part = use(prev, slot, d, 1)
                total = part if total is None else total + part
                build(at, 1 - slot, d)
            finish(prev, [total])
        return carry

    place(0, 0)
    place(1, 1)
    for d in range(REACH):
        build(0, 0, d)
    fetch.wait()
    if not turned:
        for j in range(blocks):
            cols = slice(j * BLOCK, (j + 1) * BLOCK)
            wt_ref[:, cols] = tall(w_own[0][cols, :].T)
    wt_ref[:, n:] = wt_ref[:, 0:wrap]
    lax.fori_loop(0, (blocks - 1) // 2, pair, 0)
    last = (blocks - 1) * BLOCK
    parts = [slice(wrap, last), slice(0, wrap), slice(last, n)]
    sends = [
        pltpu.make_async_copy(sum_ref.at[:, p], near_hbm.at[:, p], near_sem.at[j]) for j, p in enumerate(parts)
    ]
    sends[0].start()
    finish(last, [use(last, 0, 0, 1), use(last, 0, 1, REACH - 1)])
    sum_ref[:, 0:wrap] += sum_ref[:, n:]
    sends[1].start()
    sends[2].start()
    for send in sends:
        send.wait()


def middle_body(own_ref, m1_ref, m2_ref, m3_ref, out_ref):
    tail = slice(RANK, RANK + 2 * QROWS)
    total = (own_ref[...] + m1_ref[tail, :]) + (m2_ref[tail, :] + m3_ref[tail, :])
    out_ref[...] = jnp.broadcast_to(total[None], out_ref.shape)


def couple_body(got_ref, couple_ref, g1_ref, s2_ref, spread_ref):
    s2 = jnp.zeros((QROWS, OUT), F32)
    for m in range(N_MID):
        spread_ref[m * RANK : (m + 1) * RANK, :] = wide(expand_packed(got_ref[m, 0:QROWS, :]))
        s2 = s2 + got_ref[m, QROWS:, :]
    g1_ref[...] = fold_and_pack(dot3(couple_ref[...], spread_ref[...]))
    s2_ref[...] = s2


def update_body(last, *refs):
    near_ref, messages, down_ref, tops = refs[0], refs[1:4], refs[4], refs[5:9]
    base_ref, bcat_ref = refs[9:11]
    if last:
        out_hbm, out_ref, out_sem = refs[11:]
    else:
        basis_t_ref, up_ref, out_hbm, own_ref = refs[11:15]
        message_refs = refs[15:18]
        out_ref, out_sem, whl_ref = refs[18:]
    blocks = [slice(j, j + BLOCK) for j in range(0, base_ref.shape[0], BLOCK)]
    parts = [slice(j, j + GROUP * BLOCK) for j in range(0, base_ref.shape[0], GROUP * BLOCK)]
    own = lax.axis_index("leaf")
    quarters = [lax.rem(own + N_LEAF - k, N_LEAF) for k in range(N_LEAF)]
    g1 = unpack_quarters([ref[0:QROWS, :] for ref in tops], quarters)
    s2 = unpack_quarters([ref[QROWS:, :] for ref in tops], quarters)
    skeletons = [ref[0:RANK, :] for ref in messages] + [g1, s2]
    g0 = dot3(down_ref[...], wide(jnp.concatenate(skeletons, axis=0)))
    hi, lo = split(g0)
    rhs = jnp.concatenate(
        [jnp.concatenate([hi, lo], axis=1), jnp.concatenate([hi, jnp.zeros_like(lo)], axis=1)], axis=0
    )
    sends = []
    for j, part in enumerate(parts):
        for rows in blocks[j * GROUP : (j + 1) * GROUP]:
            f = jnp.dot(bcat_ref[rows, :], rhs, preferred_element_type=F32)
            f = near_ref[rows, :] + (f[:, :OUT] + f[:, OUT:])
            new = base_ref[rows, :] - (0.5 * jnp.tanh(0.5 * f) + 0.5)
            out_ref[rows, :] = new
            if not last:
                whl_ref[rows, :] = wide(new)
        sends.append(pltpu.make_async_copy(out_ref.at[part], out_hbm.at[part], out_sem.at[j]))
        sends[j].start()
    if not last:
        s0 = dot3(tall(basis_t_ref[...]), whl_ref[...])
        emit_messages(s0, up_ref[...], own_ref, message_refs)
    for send in sends:
        send.wait()


def params(mib):
    return pltpu.CompilerParams(vmem_limit_bytes=mib << 20)


def shape(*dims, dtype=F32):
    return jax.ShapeDtypeStruct(dims, dtype)


def ring(k):
    return [(i, (i + k) % N_LEAF) for i in range(N_LEAF)]


def call(body, out, operands, mib, name, scratch=(), work=(0, 0, 0), far_in=(), far_out=()):
    out = [pltpu.HBM(o.shape, o.dtype) if i in far_out else o for i, o in enumerate(out)]
    operands = [
        pltpu.with_memory_space_constraint(x, pltpu.HBM) if i in far_in else x
        for i, x in enumerate(operands)
    ]
    return pl.pallas_call(
        body,
        out_shape=out,
        in_specs=[HBM if i in far_in else VMEM for i in range(len(operands))],
        out_specs=[HBM if i in far_out else VMEM for i in range(len(out))],
        scratch_shapes=scratch,
        compiler_params=params(mib),
        cost_estimate=pl.CostEstimate(flops=work[0], bytes_accessed=work[1], transcendentals=work[2]),
        name=name,
    )(*operands)


def on_device(
    coords,
    weights,
    labels,
    order,
    basis,
    transfer_leaf,
    transfer_mid,
    couple_leaf,
    couple_mid,
    couple_top,
):
    n = weights.shape[0]
    scale = 4.0 / math.sqrt(n)
    basis_t = basis.T
    groups = n // (GROUP * BLOCK)
    wide_n = n + (REACH - 1) * BLOCK
    message_shapes = [shape(2 * QROWS, OUT)] + [shape(RANK + 2 * QROWS, OUT)] * 3

    up, own, *messages = call(
        first_body,
        [shape(RANK, 2 * RANK), *message_shapes],
        (basis_t, weights, transfer_leaf, transfer_mid),
        58,
        "first",
        [
            pltpu.VMEM((RANK, n), F32),
            pltpu.VMEM((n, OUT), F32),
            pltpu.SemaphoreType.DMA,
            pltpu.SemaphoreType.DMA((groups,)),
        ],
        far_in=(0, 1),
    )
    bcat, couple, down = call(
        prepare_body,
        [
            shape(n, 2 * RANK, dtype=BF16),
            shape(2 * RANK, N_MID * RANK, dtype=BF16),
            shape(2 * RANK, 5 * RANK, dtype=BF16),
        ],
        (basis_t, transfer_leaf, transfer_mid, couple_leaf, couple_mid, couple_top),
        58,
        "prepare",
        [
            pltpu.VMEM((RANK, n), F32),
            pltpu.VMEM((1, N_MID, RANK, RANK), F32),
            pltpu.VMEM((n, 2 * RANK), BF16),
            pltpu.VMEM((2 * RANK, N_MID * RANK), BF16),
            pltpu.SemaphoreType.DMA((4,)),
        ],
        far_in=(0, 4),
        far_out=(0, 1),
    )
    own, couple = lax.optimization_barrier((own, couple))

    current = weights
    for step in range(STEPS):
        last = step == STEPS - 1
        if step:
            (w_near,) = call(
                turn_body,
                [shape(2 * OUT, n, dtype=BF16)],
                (current,),
                8,
                "turn",
                [
                    pltpu.VMEM((n, OUT), F32),
                    pltpu.VMEM((2 * OUT, n), BF16),
                    pltpu.SemaphoreType.DMA((groups,)),
                    pltpu.SemaphoreType.DMA((groups,)),
                ],
                (0, n * OUT * 8, 0),
                (0,),
                (0,),
            )
            own, w_near = lax.optimization_barrier((own, w_near))
        else:
            w_near = current
        (near_t,) = call(
            functools.partial(near_body, bool(step)),
            [shape(OUT, n)],
            (coords, w_near),
            20,
            "near",
            [
                pltpu.VMEM((2, 2, BLOCK, REACH * BLOCK), BF16),
                pltpu.VMEM((OUT, wide_n), F32),
                pltpu.VMEM((2, 3, BLOCK, OUT), F32),
                pltpu.VMEM((8, wide_n), F32),
                pltpu.VMEM((2 * OUT, wide_n), BF16),
                pltpu.VMEM((n, 8), F32),
                pltpu.SemaphoreType.DMA,
                pltpu.SemaphoreType.DMA((3,)),
            ]
            + ([] if step else [pltpu.VMEM((n, OUT), F32)]),
            (6 * n * n * OUT, n * OUT * 12, n * n),
            (1,),
            (0,),
        )
        messages = [lax.ppermute(m, "leaf", ring(k)) for k, m in enumerate(messages, 1)]
        (spread,) = call(middle_body, [shape(N_MID, 2 * QROWS, OUT)], (own, *messages), 4, "middle")
        got = lax.all_to_all(spread, "mid", 0, 0)
        got, near_t = lax.optimization_barrier((got, near_t))
        g1, s2 = call(
            couple_body,
            [shape(QROWS, OUT)] * 2,
            (got, couple),
            8,
            "couple",
            [pltpu.VMEM((N_MID * RANK, 2 * OUT), BF16)],
        )
        s2 = lax.ppermute(s2, "top", [(0, 1), (1, 0)])
        top = jnp.concatenate([g1, s2], axis=0)
        tops = [top] + [lax.ppermute(top, "leaf", ring(k)) for k in (1, 2, 3)]
        kept = [pltpu.VMEM((OUT, n), F32), pltpu.VMEM((n, OUT), F32)]
        if step:
            near, base = call(
                functools.partial(finish_body, scale),
                [shape(n, OUT)] * 2,
                (near_t, current, targets),
                8,
                "finish",
                [*kept, pltpu.VMEM((n, OUT), F32), pltpu.SemaphoreType.DMA((3,))],
                (n * OUT, n * OUT * 20, 0),
                (0, 1, 2),
            )
        else:
            near, base, targets = call(
                functools.partial(finish_body, scale),
                [shape(n, OUT)] * 3,
                (near_t, current, order, labels),
                16,
                "finish",
                [
                    *kept,
                    pltpu.VMEM((n, OUT), jnp.int32),
                    pltpu.VMEM((n, OUT), F32),
                    pltpu.VMEM((n, n // BITS), BF16),
                    pltpu.VMEM((n, 8), F32),
                    pltpu.SemaphoreType.DMA((3,)),
                    pltpu.SemaphoreType.DMA,
                ],
                (n * n // BITS * 2 * OUT, n * OUT * 24, 0),
                (0, 1, 3),
                (2,),
            )
        far = (near, *messages, down, *tops, base, bcat)
        rows_buffer = [pltpu.VMEM((n, OUT), F32), pltpu.SemaphoreType.DMA((groups,))]
        body = functools.partial(update_body, last)
        if last:
            (current,) = call(
                body, [shape(n, OUT)], far, 8, "last", rows_buffer, far_out=(0,)
            )
        else:
            current, own, *messages = call(
                body,
                [shape(n, OUT), *message_shapes],
                (*far, basis_t, up),
                12,
                "update",
                [*rows_buffer, pltpu.VMEM((n, 2 * OUT), BF16)],
                far_out=(0,),
            )
    return current


def solution(mesh):
    placed = (
        P(None, ("top", "mid", "leaf")),
        P(("top", "mid", "leaf"), None),
        P(("top", "mid", "leaf"), None),
        P(("top", "mid", "leaf"), None),
        P(("top", "mid", "leaf"), None),
        P(("top", "mid", "leaf"), None, None),
        P(("top", "mid"), None, None),
        P(("top", "mid", "leaf"), None, None, None),
        P(("top", "mid"), None, None, None),
        P("top", None, None, None),
    )
    return jax.shard_map(
        on_device,
        mesh=mesh,
        in_specs=placed,
        out_specs=P(("top", "mid", "leaf"), None),
        check_vma=False,
    )
```

```python
import functools
import math

import jax
import jax.numpy as jnp
from jax import lax
from jax.experimental import pallas as pl
from jax.experimental.pallas import tpu as pltpu
from jax.sharding import PartitionSpec as P

STEPS = 2
RANK = 64
OUT = 128
N_MID = 32
N_LEAF = 4
QROWS = RANK // N_LEAF
QCOLS = OUT // N_LEAF
HP = lax.Precision.HIGHEST
F32 = jnp.float32
BF16 = jnp.bfloat16
LOG2E = math.log2(math.e)
BLOCK = 256
REACH = 5
BITS = 8
GROUP = 3
TILE = 32
VMEM = pl.BlockSpec(memory_space=pltpu.VMEM)
HBM = pl.BlockSpec(memory_space=pltpu.HBM)


def split(x):
    hi = x.astype(BF16)
    return hi, (x - hi.astype(F32)).astype(BF16)


def wide(x):
    return jnp.concatenate(split(x), axis=1)


def dot3(tall, wide_rhs):
    d = jnp.dot(tall, wide_rhs, preferred_element_type=F32)
    m, n = d.shape[0] // 2, d.shape[1] // 2
    return d[:m, :n] + (d[:m, n:] + d[m:, :n])


def lane_group():
    return lax.broadcasted_iota(jnp.int32, (QROWS, OUT), 1) // QCOLS


def pack_quarter(full, quarter):
    group = lane_group()
    out = jnp.zeros((QROWS, OUT), F32)
    for k in range(N_LEAF):
        moved = pltpu.roll(
            full[k * QROWS : (k + 1) * QROWS], lax.rem((k - quarter + N_LEAF) * QCOLS, OUT), 1
        )
        out = jnp.where(group == k, moved, out)
    return out


def expand_packed(packed):
    group = lane_group()
    zero = jnp.zeros((QROWS, OUT), F32)
    return jnp.concatenate([jnp.where(group == k, packed, zero) for k in range(N_LEAF)], axis=0)


def fold_and_pack(grouped):
    both = grouped + pltpu.roll(grouped, 2 * QCOLS, 1)
    total = both + pltpu.roll(both, QCOLS, 1)
    group = lane_group()
    out = jnp.zeros((QROWS, OUT), F32)
    for k in range(N_LEAF):
        out = jnp.where(group == k, total[k * QROWS : (k + 1) * QROWS], out)
    return out


def unpack_quarters(packed, quarters):
    group = lane_group()
    rows = []
    for k in range(N_LEAF):
        out = jnp.zeros((QROWS, OUT), F32)
        for block, quarter in zip(packed, quarters):
            moved = pltpu.roll(block, lax.rem((quarter - k + N_LEAF) * QCOLS, OUT), 1)
            out = jnp.where(group == quarter, moved, out)
        rows.append(out)
    return jnp.concatenate(rows, axis=0)


def tall(x):
    return jnp.concatenate(split(x), axis=0)


def dot_rows(lhs, rhs):
    return lax.dot_general(
        lhs, rhs, (((0,), (0,)), ((), ())), precision=HP, preferred_element_type=F32
    )


def emit_messages(s0, up, own_ref, message_refs):
    own = lax.axis_index("leaf")
    both = dot_rows(up, s0)

    def quarter(q):
        return jnp.concatenate([pack_quarter(both[:RANK], q), pack_quarter(both[RANK:], q)], axis=0)

    own_ref[...] = quarter(own)
    for k, ref in enumerate(message_refs, 1):
        ref[0:RANK, :] = s0
        ref[RANK:, :] = quarter(lax.rem(own + k, N_LEAF))


def first_body(basis_t_ref, w_ref, leaf_ref, mid_ref, up_ref, own_ref, *message_refs):
    through = jnp.dot(leaf_ref[0], mid_ref[0], precision=HP, preferred_element_type=F32)
    up_ref[...] = jnp.concatenate([leaf_ref[0], through], axis=1)
    s0 = dot3(tall(basis_t_ref[...]), wide(w_ref[...]))
    emit_messages(s0, up_ref[...], own_ref, message_refs)


def prepare_body(
    basis_t_ref, leaf_ref, mid_ref, couple_leaf_ref, couple_mid_ref, couple_top_ref,
    bcat_ref, couple_ref, down_ref,
):
    n = basis_t_ref.shape[1]
    for j in range(n // BLOCK):
        cols = slice(j * BLOCK, (j + 1) * BLOCK)
        bcat_ref[cols, :] = wide(basis_t_ref[:, cols].T)
    own_mid, own_leaf = lax.axis_index("mid"), lax.axis_index("leaf")
    for m in range(N_MID // 2):
        pair = [
            jnp.where(own_mid == i, 0.0, couple_mid_ref[0, i]) for i in (2 * m, 2 * m + 1)
        ]
        couple_ref[:, m * OUT : (m + 1) * OUT] = tall(jnp.concatenate(pair, axis=1))
    other = 1 - lax.axis_index("top")
    from_top = jnp.dot(mid_ref[0], couple_top_ref[0, other], precision=HP, preferred_element_type=F32)
    from_top = jnp.dot(leaf_ref[0], from_top, precision=HP, preferred_element_type=F32)
    siblings = [couple_leaf_ref[0, lax.rem(own_leaf + N_LEAF - k, N_LEAF)] for k in (1, 2, 3)]
    down_ref[...] = tall(jnp.concatenate([*siblings, leaf_ref[0], from_top], axis=1))


def thirds(rows):
    size = -(-rows // 48) * 16
    return [slice(j, min(j + size, rows)) for j in range(0, rows, size)]


def permute_labels(order, fetch, labels_ref, chosen_ref, bit_ref, out_ref):
    n = labels_ref.shape[0]
    group = n // BITS
    blocks = [slice(j, j + BLOCK) for j in range(0, n, BLOCK)]
    which = jnp.zeros_like(order)
    place = jnp.ones(order.shape, F32)
    for g in range(1, BITS):
        beyond = order >= g * group
        which = jnp.where(beyond, g * group, which)
        place = jnp.where(beyond, 1.0 / (1 << g), place)
    rows = jnp.concatenate([(order - which).astype(F32), place, jnp.zeros((6, n), F32)], axis=0)
    lane = lax.broadcasted_iota(jnp.int32, (BLOCK, group), 1).astype(F32)
    for at in blocks:
        columns = rows[:, at].T
        chosen_ref[at, :] = jnp.where(columns[:, 0:1] == lane, 1.0, 0.0).astype(BF16)
        bit_ref[at, :] = columns
    for load in fetch:
        load.wait()
    packed = jnp.zeros((group, OUT), F32)
    for g in range(BITS):
        packed = packed + labels_ref[g * group : (g + 1) * group, :].astype(F32) * float(1 << g)
    packed = packed.astype(BF16)
    for at in blocks:
        value = jnp.dot(chosen_ref[at, :], packed, preferred_element_type=F32) * bit_ref[at, 1:2]
        value = jnp.floor(value)
        out_ref[at, :] = value - 2.0 * jnp.floor(0.5 * value)


def finish_body(scale, *refs):
    first = len(refs) == 15
    if first:
        sum_hbm, w_hbm, order_ref, labels_hbm, near_ref, base_ref, targets_hbm = refs[:7]
        sum_ref, w_ref, labels_ref, targets_ref, chosen_ref, bit_ref, sems, sent = refs[7:]
        pairs = [(labels_hbm, labels_ref), (sum_hbm, sum_ref), (w_hbm, w_ref)]
    else:
        sum_hbm, w_hbm, targets_hbm, near_ref, base_ref, sum_ref, w_ref, targets_ref, sems = refs
        pairs = [(sum_hbm, sum_ref), (w_hbm, w_ref), (targets_hbm, targets_ref)]
    loads = [
        [pltpu.make_async_copy(a.at[p], b.at[p], sems.at[i, j]) for j, p in enumerate(thirds(a.shape[0]))]
        for i, (a, b) in enumerate(pairs)
    ]
    for load in sum(loads, []):
        load.start()
    n = near_ref.shape[0]
    blocks = [slice(j, j + BLOCK) for j in range(0, n, BLOCK)]
    if first:
        permute_labels(order_ref[...], loads[0], labels_ref, chosen_ref, bit_ref, targets_ref)
        send = pltpu.make_async_copy(targets_ref, targets_hbm, sent)
        send.start()
        loads = loads[1:]
    for load in loads[0]:
        load.wait()
    for rows in blocks:
        near_ref[rows, :] = sum_ref[:, rows].T * scale
    for load in sum(loads[1:], []):
        load.wait()
    for rows in blocks:
        base_ref[rows, :] = w_ref[rows, :] + targets_ref[rows, :]
    if first:
        send.wait()


def turn_body(w_hbm, wt_hbm, w_ref, wt_ref, w_sem, wt_sem):
    n = w_hbm.shape[0]
    parts = [slice(j, j + GROUP * BLOCK) for j in range(0, n, GROUP * BLOCK)]
    loads = [pltpu.make_async_copy(w_hbm.at[p], w_ref.at[p], w_sem.at[j]) for j, p in enumerate(parts)]
    sends = [
        pltpu.make_async_copy(wt_ref.at[:, p], wt_hbm.at[:, p], wt_sem.at[j]) for j, p in enumerate(parts)
    ]
    for load in loads:
        load.start()
    for part, load, send in zip(parts, loads, sends):
        load.wait()
        for j in range(part.start, part.stop, BLOCK):
            wt_ref[:, j : j + BLOCK] = tall(w_ref[j : j + BLOCK, :].T)
        send.start()
    for send in sends:
        send.wait()


def near_body(
    turned, coords_ref, w_hbm, near_hbm, k_ref, sum_ref, own_ref, points_ref, wt_ref, columns_ref, w_sem, near_sem, *w_own
):
    n = coords_ref.shape[1]
    blocks = n // BLOCK
    wrap = (REACH - 1) * BLOCK
    fetch = pltpu.make_async_copy(w_hbm, wt_ref.at[:, 0:n] if turned else w_own[0], w_sem)
    fetch.start()
    points_ref[0:3, 0:n] = coords_ref[...] * LOG2E
    points_ref[3:, 0:n] = jnp.zeros((5, n), F32)
    points_ref[:, n:] = points_ref[:, 0:wrap]
    sum_ref[...] = jnp.zeros_like(sum_ref)

    for j in range(blocks):
        cols = slice(j * BLOCK, (j + 1) * BLOCK)
        columns_ref[cols, :] = points_ref[:, cols].T

    def place(i, slot):
        for k in range(3):
            own_ref[slot, k] = jnp.broadcast_to(
                columns_ref[pl.ds(pl.multiple_of(i * BLOCK, BLOCK), BLOCK), k : k + 1], (BLOCK, OUT)
            )

    def build(at, slot, d):
        for cols in (slice(c, c + OUT) for c in range(d * BLOCK, (d + 1) * BLOCK, OUT)):
            other = [points_ref[k : k + 1, pl.ds(at + cols.start, OUT)] for k in range(3)]
            for t in range(BLOCK // TILE):
                sub = slice(t * TILE, (t + 1) * TILE)
                diff_sq = None
                for k in range(3):
                    delta = own_ref[slot, k, sub, :] - other[k]
                    diff_sq = delta * delta if diff_sq is None else diff_sq + delta * delta
                dist = diff_sq * lax.rsqrt(jnp.maximum(diff_sq, 1e-37))
                k_ref[slot, 0, sub, cols], k_ref[slot, 1, sub, cols] = split(jnp.exp2(-dist))

    def product(w, hi, lo, contract):
        dims = (((1,), (contract,)), ((), ()))
        a = lax.dot_general(w, hi, dims, preferred_element_type=F32)
        b = lax.dot_general(w[:OUT], lo, dims, preferred_element_type=F32)
        return a[:OUT] + (a[OUT:] + b)

    def use(at, slot, d, count):
        cols = slice(d * BLOCK, (d + count) * BLOCK)
        where = pl.ds(at + d * BLOCK, count * BLOCK)
        part = product(wt_ref[:, where], k_ref[slot, 0, :, cols], k_ref[slot, 1, :, cols], 1)
        if d:
            sum_ref[:, where] += product(
                wt_ref[:, pl.ds(at, BLOCK)], k_ref[slot, 0, :, cols], k_ref[slot, 1, :, cols], 0
            )
        return part

    def finish(at, parts):
        sum_ref[:, pl.ds(at, BLOCK)] += functools.reduce(jnp.add, parts)

    def pair(p, carry):
        for slot in range(2):
            prev = pl.multiple_of((2 * p + slot) * BLOCK, BLOCK)
            at = pl.multiple_of(prev + BLOCK, BLOCK)
            place(lax.rem(2 * p + slot + 2, blocks), slot)
            total = None
            for d in range(REACH):
                part = use(prev, slot, d, 1)
                total = part if total is None else total + part
                build(at, 1 - slot, d)
            finish(prev, [total])
        return carry

    place(0, 0)
    place(1, 1)
    for d in range(REACH):
        build(0, 0, d)
    fetch.wait()
    if not turned:
        for j in range(blocks):
            cols = slice(j * BLOCK, (j + 1) * BLOCK)
            wt_ref[:, cols] = tall(w_own[0][cols, :].T)
    wt_ref[:, n:] = wt_ref[:, 0:wrap]
    lax.fori_loop(0, (blocks - 1) // 2, pair, 0)
    last = (blocks - 1) * BLOCK
    parts = [slice(wrap, last), slice(0, wrap), slice(last, n)]
    sends = [
        pltpu.make_async_copy(sum_ref.at[:, p], near_hbm.at[:, p], near_sem.at[j]) for j, p in enumerate(parts)
    ]
    sends[0].start()
    finish(last, [use(last, 0, 0, 1), use(last, 0, 1, REACH - 1)])
    sum_ref[:, 0:wrap] += sum_ref[:, n:]
    sends[1].start()
    sends[2].start()
    for send in sends:
        send.wait()


def middle_body(own_ref, m1_ref, m2_ref, m3_ref, out_ref):
    tail = slice(RANK, RANK + 2 * QROWS)
    total = (own_ref[...] + m1_ref[tail, :]) + (m2_ref[tail, :] + m3_ref[tail, :])
    out_ref[...] = jnp.broadcast_to(total[None], out_ref.shape)


def couple_body(got_ref, couple_ref, g1_ref, s2_ref, spread_ref):
    s2 = jnp.zeros((QROWS, OUT), F32)
    for m in range(N_MID):
        spread_ref[m * RANK : (m + 1) * RANK, :] = wide(expand_packed(got_ref[m, 0:QROWS, :]))
        s2 = s2 + got_ref[m, QROWS:, :]
    g1_ref[...] = fold_and_pack(dot3(couple_ref[...], spread_ref[...]))
    s2_ref[...] = s2


def update_body(last, *refs):
    near_ref, messages, down_ref, tops = refs[0], refs[1:4], refs[4], refs[5:9]
    base_ref, bcat_ref = refs[9:11]
    if last:
        out_hbm, out_ref, out_sem = refs[11:]
    else:
        basis_t_ref, up_ref, out_hbm, own_ref = refs[11:15]
        message_refs = refs[15:18]
        out_ref, out_sem, whl_ref = refs[18:]
    blocks = [slice(j, j + BLOCK) for j in range(0, base_ref.shape[0], BLOCK)]
    parts = [slice(j, j + GROUP * BLOCK) for j in range(0, base_ref.shape[0], GROUP * BLOCK)]
    own = lax.axis_index("leaf")
    quarters = [lax.rem(own + N_LEAF - k, N_LEAF) for k in range(N_LEAF)]
    g1 = unpack_quarters([ref[0:QROWS, :] for ref in tops], quarters)
    s2 = unpack_quarters([ref[QROWS:, :] for ref in tops], quarters)
    skeletons = [ref[0:RANK, :] for ref in messages] + [g1, s2]
    g0 = dot3(down_ref[...], wide(jnp.concatenate(skeletons, axis=0)))
    hi, lo = split(g0)
    rhs = jnp.concatenate(
        [jnp.concatenate([hi, lo], axis=1), jnp.concatenate([hi, jnp.zeros_like(lo)], axis=1)], axis=0
    )
    sends = []
    for j, part in enumerate(parts):
        for rows in blocks[j * GROUP : (j + 1) * GROUP]:
            f = jnp.dot(bcat_ref[rows, :], rhs, preferred_element_type=F32)
            f = near_ref[rows, :] + (f[:, :OUT] + f[:, OUT:])
            new = base_ref[rows, :] - (0.5 * jnp.tanh(0.5 * f) + 0.5)
            out_ref[rows, :] = new
            if not last:
                whl_ref[rows, :] = wide(new)
        for i, rows in enumerate(blocks[j * GROUP : (j + 1) * GROUP], j * GROUP):
            sends.append(pltpu.make_async_copy(out_ref.at[rows], out_hbm.at[rows], out_sem.at[i]))
            sends[i].start()
    if not last:
        s0 = dot3(tall(basis_t_ref[...]), whl_ref[...])
        emit_messages(s0, up_ref[...], own_ref, message_refs)
    for send in sends:
        send.wait()


def params(mib):
    return pltpu.CompilerParams(vmem_limit_bytes=mib << 20)


def shape(*dims, dtype=F32):
    return jax.ShapeDtypeStruct(dims, dtype)


def ring(k):
    return [(i, (i + k) % N_LEAF) for i in range(N_LEAF)]


def call(body, out, operands, mib, name, scratch=(), work=(0, 0, 0), far_in=(), far_out=()):
    out = [pltpu.HBM(o.shape, o.dtype) if i in far_out else o for i, o in enumerate(out)]
    operands = [
        pltpu.with_memory_space_constraint(x, pltpu.HBM) if i in far_in else x
        for i, x in enumerate(operands)
    ]
    return pl.pallas_call(
        body,
        out_shape=out,
        in_specs=[HBM if i in far_in else VMEM for i in range(len(operands))],
        out_specs=[HBM if i in far_out else VMEM for i in range(len(out))],
        scratch_shapes=scratch,
        compiler_params=params(mib),
        cost_estimate=pl.CostEstimate(flops=work[0], bytes_accessed=work[1], transcendentals=work[2]),
        name=name,
    )(*operands)


def on_device(
    coords,
    weights,
    labels,
    order,
    basis,
    transfer_leaf,
    transfer_mid,
    couple_leaf,
    couple_mid,
    couple_top,
):
    n = weights.shape[0]
    scale = 4.0 / math.sqrt(n)
    basis_t = basis.T
    groups = n // (GROUP * BLOCK)
    wide_n = n + (REACH - 1) * BLOCK
    message_shapes = [shape(2 * QROWS, OUT)] + [shape(RANK + 2 * QROWS, OUT)] * 3

    up, own, *messages = call(
        first_body,
        [shape(RANK, 2 * RANK), *message_shapes],
        (basis_t, weights, transfer_leaf, transfer_mid),
        58,
        "first",
    )
    bcat, couple, down = call(
        prepare_body,
        [
            shape(n, 2 * RANK, dtype=BF16),
            shape(2 * RANK, N_MID * RANK, dtype=BF16),
            shape(2 * RANK, 5 * RANK, dtype=BF16),
        ],
        (basis_t, transfer_leaf, transfer_mid, couple_leaf, couple_mid, couple_top),
        58,
        "prepare",
    )
    own, couple = lax.optimization_barrier((own, couple))

    current = weights
    for step in range(STEPS):
        last = step == STEPS - 1
        if step:
            (w_near,) = call(
                turn_body,
                [shape(2 * OUT, n, dtype=BF16)],
                (current,),
                8,
                "turn",
                [
                    pltpu.VMEM((n, OUT), F32),
                    pltpu.VMEM((2 * OUT, n), BF16),
                    pltpu.SemaphoreType.DMA((groups,)),
                    pltpu.SemaphoreType.DMA((groups,)),
                ],
                (0, n * OUT * 8, 0),
                (0,),
                (0,),
            )
            own, w_near = lax.optimization_barrier((own, w_near))
        else:
            w_near = current
        (near_t,) = call(
            functools.partial(near_body, bool(step)),
            [shape(OUT, n)],
            (coords, w_near),
            20,
            "near",
            [
                pltpu.VMEM((2, 2, BLOCK, REACH * BLOCK), BF16),
                pltpu.VMEM((OUT, wide_n), F32),
                pltpu.VMEM((2, 3, BLOCK, OUT), F32),
                pltpu.VMEM((8, wide_n), F32),
                pltpu.VMEM((2 * OUT, wide_n), BF16),
                pltpu.VMEM((n, 8), F32),
                pltpu.SemaphoreType.DMA,
                pltpu.SemaphoreType.DMA((3,)),
            ]
            + ([] if step else [pltpu.VMEM((n, OUT), F32)]),
            (6 * n * n * OUT, n * OUT * 12, n * n),
            (1,),
            (0,),
        )
        messages = [lax.ppermute(m, "leaf", ring(k)) for k, m in enumerate(messages, 1)]
        (spread,) = call(middle_body, [shape(N_MID, 2 * QROWS, OUT)], (own, *messages), 4, "middle")
        got = lax.all_to_all(spread, "mid", 0, 0)
        got, near_t = lax.optimization_barrier((got, near_t))
        g1, s2 = call(
            couple_body,
            [shape(QROWS, OUT)] * 2,
            (got, couple),
            8,
            "couple",
            [pltpu.VMEM((N_MID * RANK, 2 * OUT), BF16)],
        )
        s2 = lax.ppermute(s2, "top", [(0, 1), (1, 0)])
        top = jnp.concatenate([g1, s2], axis=0)
        tops = [top] + [lax.ppermute(top, "leaf", ring(k)) for k in (1, 2, 3)]
        kept = [pltpu.VMEM((OUT, n), F32), pltpu.VMEM((n, OUT), F32)]
        if step:
            near, base = call(
                functools.partial(finish_body, scale),
                [shape(n, OUT)] * 2,
                (near_t, current, targets),
                8,
                "finish",
                [*kept, pltpu.VMEM((n, OUT), F32), pltpu.SemaphoreType.DMA((3, 3))],
                (n * OUT, n * OUT * 20, 0),
                (0, 1, 2),
            )
        else:
            near, base, targets = call(
                functools.partial(finish_body, scale),
                [shape(n, OUT)] * 3,
                (near_t, current, order, labels),
                16,
                "finish",
                [
                    *kept,
                    pltpu.VMEM((n, OUT), jnp.int32),
                    pltpu.VMEM((n, OUT), F32),
                    pltpu.VMEM((n, n // BITS), BF16),
                    pltpu.VMEM((n, 8), F32),
                    pltpu.SemaphoreType.DMA((3, 3)),
                    pltpu.SemaphoreType.DMA,
                ],
                (n * n // BITS * 2 * OUT, n * OUT * 24, 0),
                (0, 1, 3),
                (2,),
            )
        far = (near, *messages, down, *tops, base, bcat)
        rows_buffer = [pltpu.VMEM((n, OUT), F32), pltpu.SemaphoreType.DMA((n // BLOCK,))]
        body = functools.partial(update_body, last)
        if last:
            (current,) = call(
                body, [shape(n, OUT)], far, 8, "last", rows_buffer, far_out=(0,)
            )
        else:
            current, own, *messages = call(
                body,
                [shape(n, OUT), *message_shapes],
                (*far, basis_t, up),
                12,
                "update",
                [*rows_buffer, pltpu.VMEM((n, 2 * OUT), BF16)],
                far_out=(0,),
            )
    return current


def solution(mesh):
    placed = (
        P(None, ("top", "mid", "leaf")),
        P(("top", "mid", "leaf"), None),
        P(("top", "mid", "leaf"), None),
        P(("top", "mid", "leaf"), None),
        P(("top", "mid", "leaf"), None),
        P(("top", "mid", "leaf"), None, None),
        P(("top", "mid"), None, None),
        P(("top", "mid", "leaf"), None, None, None),
        P(("top", "mid"), None, None, None),
        P("top", None, None, None),
    )
    return jax.shard_map(
        on_device,
        mesh=mesh,
        in_specs=placed,
        out_specs=P(("top", "mid", "leaf"), None),
        check_vma=False,
    )
```

```python
import functools
import math

import jax
import jax.numpy as jnp
from jax import lax
from jax.experimental import pallas as pl
from jax.experimental.pallas import tpu as pltpu
from jax.sharding import PartitionSpec as P

STEPS = 2
RANK = 64
OUT = 128
N_MID = 32
N_LEAF = 4
QROWS = RANK // N_LEAF
QCOLS = OUT // N_LEAF
HP = lax.Precision.HIGHEST
F32 = jnp.float32
BF16 = jnp.bfloat16
LOG2E = math.log2(math.e)
BLOCK = 256
REACH = 5
BITS = 8
GROUP = 3
TILE = 32
VMEM = pl.BlockSpec(memory_space=pltpu.VMEM)
HBM = pl.BlockSpec(memory_space=pltpu.HBM)


def split(x):
    hi = x.astype(BF16)
    return hi, (x - hi.astype(F32)).astype(BF16)


def wide(x):
    return jnp.concatenate(split(x), axis=1)


def dot3(tall, wide_rhs):
    d = jnp.dot(tall, wide_rhs, preferred_element_type=F32)
    m, n = d.shape[0] // 2, d.shape[1] // 2
    return d[:m, :n] + (d[:m, n:] + d[m:, :n])


def lane_group():
    return lax.broadcasted_iota(jnp.int32, (QROWS, OUT), 1) // QCOLS


def pack_quarter(full, quarter):
    group = lane_group()
    out = jnp.zeros((QROWS, OUT), F32)
    for k in range(N_LEAF):
        moved = pltpu.roll(
            full[k * QROWS : (k + 1) * QROWS], lax.rem((k - quarter + N_LEAF) * QCOLS, OUT), 1
        )
        out = jnp.where(group == k, moved, out)
    return out


def expand_packed(packed):
    group = lane_group()
    zero = jnp.zeros((QROWS, OUT), F32)
    return jnp.concatenate([jnp.where(group == k, packed, zero) for k in range(N_LEAF)], axis=0)


def fold_and_pack(grouped):
    both = grouped + pltpu.roll(grouped, 2 * QCOLS, 1)
    total = both + pltpu.roll(both, QCOLS, 1)
    group = lane_group()
    out = jnp.zeros((QROWS, OUT), F32)
    for k in range(N_LEAF):
        out = jnp.where(group == k, total[k * QROWS : (k + 1) * QROWS], out)
    return out


def unpack_quarters(packed, quarters):
    group = lane_group()
    rows = []
    for k in range(N_LEAF):
        out = jnp.zeros((QROWS, OUT), F32)
        for block, quarter in zip(packed, quarters):
            moved = pltpu.roll(block, lax.rem((quarter - k + N_LEAF) * QCOLS, OUT), 1)
            out = jnp.where(group == quarter, moved, out)
        rows.append(out)
    return jnp.concatenate(rows, axis=0)


def tall(x):
    return jnp.concatenate(split(x), axis=0)


def dot_rows(lhs, rhs):
    return lax.dot_general(
        lhs, rhs, (((0,), (0,)), ((), ())), precision=HP, preferred_element_type=F32
    )


def emit_messages(s0, up, own_ref, message_refs):
    own = lax.axis_index("leaf")
    both = dot_rows(up, s0)

    def quarter(q):
        return jnp.concatenate([pack_quarter(both[:RANK], q), pack_quarter(both[RANK:], q)], axis=0)

    own_ref[...] = quarter(own)
    for k, ref in enumerate(message_refs, 1):
        ref[0:RANK, :] = s0
        ref[RANK:, :] = quarter(lax.rem(own + k, N_LEAF))


def first_body(basis_t_ref, w_ref, leaf_ref, mid_ref, up_ref, own_ref, *message_refs):
    through = jnp.dot(leaf_ref[0], mid_ref[0], precision=HP, preferred_element_type=F32)
    up_ref[...] = jnp.concatenate([leaf_ref[0], through], axis=1)
    s0 = dot3(tall(basis_t_ref[...]), wide(w_ref[...]))
    emit_messages(s0, up_ref[...], own_ref, message_refs)


def prepare_body(
    basis_t_ref, leaf_ref, mid_ref, couple_leaf_ref, couple_mid_ref, couple_top_ref,
    bcat_ref, couple_ref, down_ref,
):
    n = basis_t_ref.shape[1]
    for j in range(n // BLOCK):
        cols = slice(j * BLOCK, (j + 1) * BLOCK)
        bcat_ref[cols, :] = wide(basis_t_ref[:, cols].T)
    own_mid, own_leaf = lax.axis_index("mid"), lax.axis_index("leaf")
    for m in range(N_MID // 2):
        pair = [
            jnp.where(own_mid == i, 0.0, couple_mid_ref[0, i]) for i in (2 * m, 2 * m + 1)
        ]
        couple_ref[:, m * OUT : (m + 1) * OUT] = tall(jnp.concatenate(pair, axis=1))
    other = 1 - lax.axis_index("top")
    from_top = jnp.dot(mid_ref[0], couple_top_ref[0, other], precision=HP, preferred_element_type=F32)
    from_top = jnp.dot(leaf_ref[0], from_top, precision=HP, preferred_element_type=F32)
    siblings = [couple_leaf_ref[0, lax.rem(own_leaf + N_LEAF - k, N_LEAF)] for k in (1, 2, 3)]
    down_ref[...] = tall(jnp.concatenate([*siblings, leaf_ref[0], from_top], axis=1))


def thirds(rows):
    size = -(-rows // 48) * 16
    return [slice(j, min(j + size, rows)) for j in range(0, rows, size)]


def permute_labels(order, fetch, labels_ref, chosen_ref, bit_ref, out_ref):
    n = labels_ref.shape[0]
    group = n // BITS
    blocks = [slice(j, j + BLOCK) for j in range(0, n, BLOCK)]
    which = jnp.zeros_like(order)
    place = jnp.ones(order.shape, F32)
    for g in range(1, BITS):
        beyond = order >= g * group
        which = jnp.where(beyond, g * group, which)
        place = jnp.where(beyond, 1.0 / (1 << g), place)
    rows = jnp.concatenate([(order - which).astype(F32), place, jnp.zeros((6, n), F32)], axis=0)
    lane = lax.broadcasted_iota(jnp.int32, (BLOCK, group), 1).astype(F32)
    for at in blocks:
        columns = rows[:, at].T
        chosen_ref[at, :] = jnp.where(columns[:, 0:1] == lane, 1.0, 0.0).astype(BF16)
        bit_ref[at, :] = columns
    for load in fetch:
        load.wait()
    packed = jnp.zeros((group, OUT), F32)
    for g in range(BITS):
        packed = packed + labels_ref[g * group : (g + 1) * group, :].astype(F32) * float(1 << g)
    packed = packed.astype(BF16)
    for at in blocks:
        value = jnp.dot(chosen_ref[at, :], packed, preferred_element_type=F32) * bit_ref[at, 1:2]
        value = jnp.floor(value)
        out_ref[at, :] = value - 2.0 * jnp.floor(0.5 * value)


def finish_body(scale, *refs):
    first = len(refs) == 15
    if first:
        sum_hbm, w_hbm, order_ref, labels_hbm, near_ref, base_ref, targets_hbm = refs[:7]
        sum_ref, w_ref, labels_ref, targets_ref, chosen_ref, bit_ref, sems, sent = refs[7:]
        pairs = [(labels_hbm, labels_ref), (sum_hbm, sum_ref), (w_hbm, w_ref)]
    else:
        sum_hbm, w_hbm, targets_hbm, near_ref, base_ref, sum_ref, w_ref, targets_ref, sems = refs
        pairs = [(sum_hbm, sum_ref), (w_hbm, w_ref), (targets_hbm, targets_ref)]
    loads = [
        [pltpu.make_async_copy(a.at[p], b.at[p], sems.at[i, j]) for j, p in enumerate(thirds(a.shape[0]))]
        for i, (a, b) in enumerate(pairs)
    ]
    for load in sum(loads, []):
        load.start()
    n = near_ref.shape[0]
    blocks = [slice(j, j + BLOCK) for j in range(0, n, BLOCK)]
    if first:
        permute_labels(order_ref[...], loads[0], labels_ref, chosen_ref, bit_ref, targets_ref)
        send = pltpu.make_async_copy(targets_ref, targets_hbm, sent)
        send.start()
        loads = loads[1:]
    for load in loads[0]:
        load.wait()
    for rows in blocks:
        near_ref[rows, :] = sum_ref[:, rows].T * scale
    for load in sum(loads[1:], []):
        load.wait()
    for rows in blocks:
        base_ref[rows, :] = w_ref[rows, :] + targets_ref[rows, :]
    if first:
        send.wait()


def turn_body(w_ref, wt_hbm, w_hbm, wt_ref, wt_sem, w_sem):
    n = w_ref.shape[0]
    parts = [slice(j, j + GROUP * BLOCK) for j in range(0, n, GROUP * BLOCK)]
    sends = [
        pltpu.make_async_copy(wt_ref.at[:, p], wt_hbm.at[:, p], wt_sem.at[j]) for j, p in enumerate(parts)
    ]
    copies = [pltpu.make_async_copy(w_ref.at[p], w_hbm.at[p], w_sem.at[j]) for j, p in enumerate(parts)]
    for copy in copies:
        copy.start()
    for part, send in zip(parts, sends):
        for j in range(part.start, part.stop, BLOCK):
            wt_ref[:, j : j + BLOCK] = tall(w_ref[j : j + BLOCK, :].T)
        send.start()
    for copy in copies + sends:
        copy.wait()


def near_body(
    turned, coords_ref, w_hbm, near_hbm, k_ref, sum_ref, own_ref, points_ref, wt_ref, columns_ref, w_sem, near_sem, *w_own
):
    n = coords_ref.shape[1]
    blocks = n // BLOCK
    wrap = (REACH - 1) * BLOCK
    fetch = pltpu.make_async_copy(w_hbm, wt_ref.at[:, 0:n] if turned else w_own[0], w_sem)
    fetch.start()
    points_ref[0:3, 0:n] = coords_ref[...] * LOG2E
    points_ref[3:, 0:n] = jnp.zeros((5, n), F32)
    points_ref[:, n:] = points_ref[:, 0:wrap]
    sum_ref[...] = jnp.zeros_like(sum_ref)

    for j in range(blocks):
        cols = slice(j * BLOCK, (j + 1) * BLOCK)
        columns_ref[cols, :] = points_ref[:, cols].T

    def place(i, slot):
        for k in range(3):
            own_ref[slot, k] = jnp.broadcast_to(
                columns_ref[pl.ds(pl.multiple_of(i * BLOCK, BLOCK), BLOCK), k : k + 1], (BLOCK, OUT)
            )

    def build(at, slot, d):
        for cols in (slice(c, c + OUT) for c in range(d * BLOCK, (d + 1) * BLOCK, OUT)):
            other = [points_ref[k : k + 1, pl.ds(at + cols.start, OUT)] for k in range(3)]
            for t in range(BLOCK // TILE):
                sub = slice(t * TILE, (t + 1) * TILE)
                diff_sq = None
                for k in range(3):
                    delta = own_ref[slot, k, sub, :] - other[k]
                    diff_sq = delta * delta if diff_sq is None else diff_sq + delta * delta
                dist = diff_sq * lax.rsqrt(jnp.maximum(diff_sq, 1e-37))
                k_ref[slot, 0, sub, cols], k_ref[slot, 1, sub, cols] = split(jnp.exp2(-dist))

    def product(w, hi, lo, contract):
        dims = (((1,), (contract,)), ((), ()))
        a = lax.dot_general(w, hi, dims, preferred_element_type=F32)
        b = lax.dot_general(w[:OUT], lo, dims, preferred_element_type=F32)
        return a[:OUT] + (a[OUT:] + b)

    def use(at, slot, d, count):
        cols = slice(d * BLOCK, (d + count) * BLOCK)
        where = pl.ds(at + d * BLOCK, count * BLOCK)
        part = product(wt_ref[:, where], k_ref[slot, 0, :, cols], k_ref[slot, 1, :, cols], 1)
        if d:
            sum_ref[:, where] += product(
                wt_ref[:, pl.ds(at, BLOCK)], k_ref[slot, 0, :, cols], k_ref[slot, 1, :, cols], 0
            )
        return part

    def finish(at, parts):
        sum_ref[:, pl.ds(at, BLOCK)] += functools.reduce(jnp.add, parts)

    def pair(p, carry):
        for slot in range(2):
            prev = pl.multiple_of((2 * p + slot) * BLOCK, BLOCK)
            at = pl.multiple_of(prev + BLOCK, BLOCK)
            place(lax.rem(2 * p + slot + 2, blocks), slot)
            total = None
            for d in range(REACH):
                part = use(prev, slot, d, 1)
                total = part if total is None else total + part
                build(at, 1 - slot, d)
            finish(prev, [total])
        return carry

    place(0, 0)
    place(1, 1)
    for d in range(REACH):
        build(0, 0, d)
    fetch.wait()
    if not turned:
        for j in range(blocks):
            cols = slice(j * BLOCK, (j + 1) * BLOCK)
            wt_ref[:, cols] = tall(w_own[0][cols, :].T)
    wt_ref[:, n:] = wt_ref[:, 0:wrap]
    lax.fori_loop(0, (blocks - 1) // 2, pair, 0)
    last = (blocks - 1) * BLOCK
    parts = [slice(wrap, last), slice(0, wrap), slice(last, n)]
    sends = [
        pltpu.make_async_copy(sum_ref.at[:, p], near_hbm.at[:, p], near_sem.at[j]) for j, p in enumerate(parts)
    ]
    sends[0].start()
    finish(last, [use(last, 0, 0, 1), use(last, 0, 1, REACH - 1)])
    sum_ref[:, 0:wrap] += sum_ref[:, n:]
    sends[1].start()
    sends[2].start()
    for send in sends:
        send.wait()


def middle_body(own_ref, m1_ref, m2_ref, m3_ref, out_ref):
    tail = slice(RANK, RANK + 2 * QROWS)
    total = (own_ref[...] + m1_ref[tail, :]) + (m2_ref[tail, :] + m3_ref[tail, :])
    out_ref[...] = jnp.broadcast_to(total[None], out_ref.shape)


def couple_body(got_ref, couple_ref, g1_ref, s2_ref, spread_ref):
    s2 = jnp.zeros((QROWS, OUT), F32)
    for m in range(N_MID):
        spread_ref[m * RANK : (m + 1) * RANK, :] = wide(expand_packed(got_ref[m, 0:QROWS, :]))
        s2 = s2 + got_ref[m, QROWS:, :]
    g1_ref[...] = fold_and_pack(dot3(couple_ref[...], spread_ref[...]))
    s2_ref[...] = s2


def update_body(last, *refs):
    near_ref, messages, down_ref, tops = refs[0], refs[1:4], refs[4], refs[5:9]
    base_ref, bcat_ref = refs[9:11]
    if last:
        out_hbm, out_ref, out_sem = refs[11:]
    else:
        basis_t_ref, up_ref, out_ref, own_ref = refs[11:15]
        message_refs = refs[15:18]
        (whl_ref,) = refs[18:]
    blocks = [slice(j, j + BLOCK) for j in range(0, base_ref.shape[0], BLOCK)]
    parts = [slice(j, j + GROUP * BLOCK) for j in range(0, base_ref.shape[0], GROUP * BLOCK)]
    own = lax.axis_index("leaf")
    quarters = [lax.rem(own + N_LEAF - k, N_LEAF) for k in range(N_LEAF)]
    g1 = unpack_quarters([ref[0:QROWS, :] for ref in tops], quarters)
    s2 = unpack_quarters([ref[QROWS:, :] for ref in tops], quarters)
    skeletons = [ref[0:RANK, :] for ref in messages] + [g1, s2]
    g0 = dot3(down_ref[...], wide(jnp.concatenate(skeletons, axis=0)))
    hi, lo = split(g0)
    rhs = jnp.concatenate(
        [jnp.concatenate([hi, lo], axis=1), jnp.concatenate([hi, jnp.zeros_like(lo)], axis=1)], axis=0
    )
    sends = []
    for j, part in enumerate(parts):
        for rows in blocks[j * GROUP : (j + 1) * GROUP]:
            f = jnp.dot(bcat_ref[rows, :], rhs, preferred_element_type=F32)
            f = near_ref[rows, :] + (f[:, :OUT] + f[:, OUT:])
            new = base_ref[rows, :] - (0.5 * jnp.tanh(0.5 * f) + 0.5)
            out_ref[rows, :] = new
            if not last:
                whl_ref[rows, :] = wide(new)
        for i, rows in enumerate(blocks[j * GROUP : (j + 1) * GROUP] if last else [], j * GROUP):
            sends.append(pltpu.make_async_copy(out_ref.at[rows], out_hbm.at[rows], out_sem.at[i]))
            sends[i].start()
    if not last:
        s0 = dot3(tall(basis_t_ref[...]), whl_ref[...])
        emit_messages(s0, up_ref[...], own_ref, message_refs)
    for send in sends:
        send.wait()


def params(mib):
    return pltpu.CompilerParams(vmem_limit_bytes=mib << 20)


def shape(*dims, dtype=F32):
    return jax.ShapeDtypeStruct(dims, dtype)


def ring(k):
    return [(i, (i + k) % N_LEAF) for i in range(N_LEAF)]


def call(body, out, operands, mib, name, scratch=(), work=(0, 0, 0), far_in=(), far_out=()):
    out = [pltpu.HBM(o.shape, o.dtype) if i in far_out else o for i, o in enumerate(out)]
    operands = [
        pltpu.with_memory_space_constraint(x, pltpu.HBM) if i in far_in else x
        for i, x in enumerate(operands)
    ]
    return pl.pallas_call(
        body,
        out_shape=out,
        in_specs=[HBM if i in far_in else VMEM for i in range(len(operands))],
        out_specs=[HBM if i in far_out else VMEM for i in range(len(out))],
        scratch_shapes=scratch,
        compiler_params=params(mib),
        cost_estimate=pl.CostEstimate(flops=work[0], bytes_accessed=work[1], transcendentals=work[2]),
        name=name,
    )(*operands)


def on_device(
    coords,
    weights,
    labels,
    order,
    basis,
    transfer_leaf,
    transfer_mid,
    couple_leaf,
    couple_mid,
    couple_top,
):
    n = weights.shape[0]
    scale = 4.0 / math.sqrt(n)
    basis_t = basis.T
    groups = n // (GROUP * BLOCK)
    wide_n = n + (REACH - 1) * BLOCK
    message_shapes = [shape(2 * QROWS, OUT)] + [shape(RANK + 2 * QROWS, OUT)] * 3

    up, own, *messages = call(
        first_body,
        [shape(RANK, 2 * RANK), *message_shapes],
        (basis_t, weights, transfer_leaf, transfer_mid),
        58,
        "first",
    )
    bcat, couple, down = call(
        prepare_body,
        [
            shape(n, 2 * RANK, dtype=BF16),
            shape(2 * RANK, N_MID * RANK, dtype=BF16),
            shape(2 * RANK, 5 * RANK, dtype=BF16),
        ],
        (basis_t, transfer_leaf, transfer_mid, couple_leaf, couple_mid, couple_top),
        58,
        "prepare",
    )
    own, couple = lax.optimization_barrier((own, couple))

    current = weights
    for step in range(STEPS):
        last = step == STEPS - 1
        if step:
            w_near, current = call(
                turn_body,
                [shape(2 * OUT, n, dtype=BF16), shape(n, OUT)],
                (current,),
                8,
                "turn",
                [
                    pltpu.VMEM((2 * OUT, n), BF16),
                    pltpu.SemaphoreType.DMA((groups,)),
                    pltpu.SemaphoreType.DMA((groups,)),
                ],
                (0, n * OUT * 12, 0),
                far_out=(0, 1),
            )
            own, w_near = lax.optimization_barrier((own, w_near))
        else:
            w_near = current
        (near_t,) = call(
            functools.partial(near_body, bool(step)),
            [shape(OUT, n)],
            (coords, w_near),
            20,
            "near",
            [
                pltpu.VMEM((2, 2, BLOCK, REACH * BLOCK), BF16),
                pltpu.VMEM((OUT, wide_n), F32),
                pltpu.VMEM((2, 3, BLOCK, OUT), F32),
                pltpu.VMEM((8, wide_n), F32),
                pltpu.VMEM((2 * OUT, wide_n), BF16),
                pltpu.VMEM((n, 8), F32),
                pltpu.SemaphoreType.DMA,
                pltpu.SemaphoreType.DMA((3,)),
            ]
            + ([] if step else [pltpu.VMEM((n, OUT), F32)]),
            (6 * n * n * OUT, n * OUT * 12, n * n),
            (1,),
            (0,),
        )
        messages = [lax.ppermute(m, "leaf", ring(k)) for k, m in enumerate(messages, 1)]
        (spread,) = call(middle_body, [shape(N_MID, 2 * QROWS, OUT)], (own, *messages), 4, "middle")
        got = lax.all_to_all(spread, "mid", 0, 0)
        got, near_t = lax.optimization_barrier((got, near_t))
        g1, s2 = call(
            couple_body,
            [shape(QROWS, OUT)] * 2,
            (got, couple),
            8,
            "couple",
            [pltpu.VMEM((N_MID * RANK, 2 * OUT), BF16)],
        )
        s2 = lax.ppermute(s2, "top", [(0, 1), (1, 0)])
        top = jnp.concatenate([g1, s2], axis=0)
        tops = [top] + [lax.ppermute(top, "leaf", ring(k)) for k in (1, 2, 3)]
        kept = [pltpu.VMEM((OUT, n), F32), pltpu.VMEM((n, OUT), F32)]
        if step:
            near, base = call(
                functools.partial(finish_body, scale),
                [shape(n, OUT)] * 2,
                (near_t, current, targets),
                8,
                "finish",
                [*kept, pltpu.VMEM((n, OUT), F32), pltpu.SemaphoreType.DMA((3, 3))],
                (n * OUT, n * OUT * 20, 0),
                (0, 1, 2),
            )
        else:
            near, base, targets = call(
                functools.partial(finish_body, scale),
                [shape(n, OUT)] * 3,
                (near_t, current, order, labels),
                16,
                "finish",
                [
                    *kept,
                    pltpu.VMEM((n, OUT), jnp.int32),
                    pltpu.VMEM((n, OUT), F32),
                    pltpu.VMEM((n, n // BITS), BF16),
                    pltpu.VMEM((n, 8), F32),
                    pltpu.SemaphoreType.DMA((3, 3)),
                    pltpu.SemaphoreType.DMA,
                ],
                (n * n // BITS * 2 * OUT, n * OUT * 24, 0),
                (0, 1, 3),
                (2,),
            )
        far = (near, *messages, down, *tops, base, bcat)
        rows_buffer = [pltpu.VMEM((n, OUT), F32), pltpu.SemaphoreType.DMA((n // BLOCK,))]
        body = functools.partial(update_body, last)
        if last:
            (current,) = call(
                body, [shape(n, OUT)], far, 8, "last", rows_buffer, far_out=(0,)
            )
        else:
            current, own, *messages = call(
                body,
                [shape(n, OUT), *message_shapes],
                (*far, basis_t, up),
                12,
                "update",
                [pltpu.VMEM((n, 2 * OUT), BF16)],
            )
    return current


def solution(mesh):
    placed = (
        P(None, ("top", "mid", "leaf")),
        P(("top", "mid", "leaf"), None),
        P(("top", "mid", "leaf"), None),
        P(("top", "mid", "leaf"), None),
        P(("top", "mid", "leaf"), None),
        P(("top", "mid", "leaf"), None, None),
        P(("top", "mid"), None, None),
        P(("top", "mid", "leaf"), None, None, None),
        P(("top", "mid"), None, None, None),
        P("top", None, None, None),
    )
    return jax.shard_map(
        on_device,
        mesh=mesh,
        in_specs=placed,
        out_specs=P(("top", "mid", "leaf"), None),
        check_vma=False,
    )
```

```python
import functools
import math

import jax
import jax.numpy as jnp
from jax import lax
from jax.experimental import pallas as pl
from jax.experimental.pallas import tpu as pltpu
from jax.sharding import PartitionSpec as P

STEPS = 2
RANK = 64
OUT = 128
N_MID = 32
N_LEAF = 4
QROWS = RANK // N_LEAF
QCOLS = OUT // N_LEAF
HP = lax.Precision.HIGHEST
F32 = jnp.float32
BF16 = jnp.bfloat16
LOG2E = math.log2(math.e)
BLOCK = 256
REACH = 5
BITS = 8
GROUP = 3
TILE = 32
VMEM = pl.BlockSpec(memory_space=pltpu.VMEM)
HBM = pl.BlockSpec(memory_space=pltpu.HBM)


def split(x):
    hi = x.astype(BF16)
    return hi, (x - hi.astype(F32)).astype(BF16)


def wide(x):
    return jnp.concatenate(split(x), axis=1)


def dot3(tall, wide_rhs):
    d = jnp.dot(tall, wide_rhs, preferred_element_type=F32)
    m, n = d.shape[0] // 2, d.shape[1] // 2
    return d[:m, :n] + (d[:m, n:] + d[m:, :n])


def lane_group():
    return lax.broadcasted_iota(jnp.int32, (QROWS, OUT), 1) // QCOLS


def pack_quarter(full, quarter):
    group = lane_group()
    out = jnp.zeros((QROWS, OUT), F32)
    for k in range(N_LEAF):
        moved = pltpu.roll(
            full[k * QROWS : (k + 1) * QROWS], lax.rem((k - quarter + N_LEAF) * QCOLS, OUT), 1
        )
        out = jnp.where(group == k, moved, out)
    return out


def expand_packed(packed):
    group = lane_group()
    zero = jnp.zeros((QROWS, OUT), F32)
    return jnp.concatenate([jnp.where(group == k, packed, zero) for k in range(N_LEAF)], axis=0)


def fold_and_pack(grouped):
    both = grouped + pltpu.roll(grouped, 2 * QCOLS, 1)
    total = both + pltpu.roll(both, QCOLS, 1)
    group = lane_group()
    out = jnp.zeros((QROWS, OUT), F32)
    for k in range(N_LEAF):
        out = jnp.where(group == k, total[k * QROWS : (k + 1) * QROWS], out)
    return out


def unpack_quarters(packed, quarters):
    group = lane_group()
    rows = []
    for k in range(N_LEAF):
        out = jnp.zeros((QROWS, OUT), F32)
        for block, quarter in zip(packed, quarters):
            moved = pltpu.roll(block, lax.rem((quarter - k + N_LEAF) * QCOLS, OUT), 1)
            out = jnp.where(group == quarter, moved, out)
        rows.append(out)
    return jnp.concatenate(rows, axis=0)


def tall(x):
    return jnp.concatenate(split(x), axis=0)


def dot_rows(lhs, rhs):
    return lax.dot_general(
        lhs, rhs, (((0,), (0,)), ((), ())), precision=HP, preferred_element_type=F32
    )


def emit_messages(s0, up, own_ref, message_refs):
    own = lax.axis_index("leaf")
    both = dot_rows(up, s0)

    def quarter(q):
        return jnp.concatenate([pack_quarter(both[:RANK], q), pack_quarter(both[RANK:], q)], axis=0)

    own_ref[...] = quarter(own)
    for k, ref in enumerate(message_refs, 1):
        ref[0:RANK, :] = s0
        ref[RANK:, :] = quarter(lax.rem(own + k, N_LEAF))


def first_body(basis_t_hbm, w_hbm, leaf_hbm, mid_hbm, up_ref, own_ref, *refs):
    message_refs, (basis_t_ref, w_ref, leaf_ref, mid_ref, sems) = refs[:3], refs[3:]
    pairs = [(w_hbm, w_ref), (basis_t_hbm, basis_t_ref), (leaf_hbm, leaf_ref), (mid_hbm, mid_ref)]
    loads = [pltpu.make_async_copy(a, b, sems.at[i]) for i, (a, b) in enumerate(pairs)]
    for load in loads:
        load.start()
    for load in loads[::-1]:
        load.wait()
    through = jnp.dot(leaf_ref[0], mid_ref[0], precision=HP, preferred_element_type=F32)
    up_ref[...] = jnp.concatenate([leaf_ref[0], through], axis=1)
    s0 = dot3(tall(basis_t_ref[...]), wide(w_ref[...]))
    emit_messages(s0, up_ref[...], own_ref, message_refs)


def prepare_body(
    basis_t_ref, leaf_ref, mid_ref, couple_leaf_ref, couple_mid_ref, couple_top_ref,
    bcat_ref, couple_ref, down_ref,
):
    n = basis_t_ref.shape[1]
    for j in range(n // BLOCK):
        cols = slice(j * BLOCK, (j + 1) * BLOCK)
        bcat_ref[cols, :] = wide(basis_t_ref[:, cols].T)
    own_mid, own_leaf = lax.axis_index("mid"), lax.axis_index("leaf")
    for m in range(N_MID // 2):
        pair = [
            jnp.where(own_mid == i, 0.0, couple_mid_ref[0, i]) for i in (2 * m, 2 * m + 1)
        ]
        couple_ref[:, m * OUT : (m + 1) * OUT] = tall(jnp.concatenate(pair, axis=1))
    other = 1 - lax.axis_index("top")
    from_top = jnp.dot(mid_ref[0], couple_top_ref[0, other], precision=HP, preferred_element_type=F32)
    from_top = jnp.dot(leaf_ref[0], from_top, precision=HP, preferred_element_type=F32)
    siblings = [couple_leaf_ref[0, lax.rem(own_leaf + N_LEAF - k, N_LEAF)] for k in (1, 2, 3)]
    down_ref[...] = tall(jnp.concatenate([*siblings, leaf_ref[0], from_top], axis=1))


def thirds(rows):
    size = -(-rows // 48) * 16
    return [slice(j, min(j + size, rows)) for j in range(0, rows, size)]


def permute_labels(order, fetch, labels_ref, chosen_ref, bit_ref, out_ref):
    n = labels_ref.shape[0]
    group = n // BITS
    blocks = [slice(j, j + BLOCK) for j in range(0, n, BLOCK)]
    which = jnp.zeros_like(order)
    place = jnp.ones(order.shape, F32)
    for g in range(1, BITS):
        beyond = order >= g * group
        which = jnp.where(beyond, g * group, which)
        place = jnp.where(beyond, 1.0 / (1 << g), place)
    rows = jnp.concatenate([(order - which).astype(F32), place, jnp.zeros((6, n), F32)], axis=0)
    lane = lax.broadcasted_iota(jnp.int32, (BLOCK, group), 1).astype(F32)
    for at in blocks:
        columns = rows[:, at].T
        chosen_ref[at, :] = jnp.where(columns[:, 0:1] == lane, 1.0, 0.0).astype(BF16)
        bit_ref[at, :] = columns
    for load in fetch:
        load.wait()
    packed = jnp.zeros((group, OUT), F32)
    for g in range(BITS):
        packed = packed + labels_ref[g * group : (g + 1) * group, :].astype(F32) * float(1 << g)
    packed = packed.astype(BF16)
    for at in blocks:
        value = jnp.dot(chosen_ref[at, :], packed, preferred_element_type=F32) * bit_ref[at, 1:2]
        value = jnp.floor(value)
        out_ref[at, :] = value - 2.0 * jnp.floor(0.5 * value)


def finish_body(scale, *refs):
    first = len(refs) == 15
    if first:
        sum_hbm, w_hbm, order_ref, labels_hbm, near_ref, base_ref, targets_hbm = refs[:7]
        sum_ref, w_ref, labels_ref, targets_ref, chosen_ref, bit_ref, sems, sent = refs[7:]
        pairs = [(labels_hbm, labels_ref), (sum_hbm, sum_ref), (w_hbm, w_ref)]
    else:
        sum_hbm, w_hbm, targets_hbm, near_ref, base_ref, sum_ref, w_ref, targets_ref, sems = refs
        pairs = [(sum_hbm, sum_ref), (w_hbm, w_ref), (targets_hbm, targets_ref)]
    loads = [
        [pltpu.make_async_copy(a.at[p], b.at[p], sems.at[i, j]) for j, p in enumerate(thirds(a.shape[0]))]
        for i, (a, b) in enumerate(pairs)
    ]
    for load in sum(loads, []):
        load.start()
    n = near_ref.shape[0]
    blocks = [slice(j, j + BLOCK) for j in range(0, n, BLOCK)]
    if first:
        permute_labels(order_ref[...], loads[0], labels_ref, chosen_ref, bit_ref, targets_ref)
        send = pltpu.make_async_copy(targets_ref, targets_hbm, sent)
        send.start()
        loads = loads[1:]
    for load in loads[0]:
        load.wait()
    for rows in blocks:
        near_ref[rows, :] = sum_ref[:, rows].T * scale
    for load in sum(loads[1:], []):
        load.wait()
    for rows in blocks:
        base_ref[rows, :] = w_ref[rows, :] + targets_ref[rows, :]
    if first:
        send.wait()


def turn_body(w_ref, wt_hbm, w_hbm, wt_ref, wt_sem, w_sem):
    n = w_ref.shape[0]
    parts = [slice(j, j + GROUP * BLOCK) for j in range(0, n, GROUP * BLOCK)]
    sends = [
        pltpu.make_async_copy(wt_ref.at[:, p], wt_hbm.at[:, p], wt_sem.at[j]) for j, p in enumerate(parts)
    ]
    copies = [pltpu.make_async_copy(w_ref.at[p], w_hbm.at[p], w_sem.at[j]) for j, p in enumerate(parts)]
    for copy in copies:
        copy.start()
    for part, send in zip(parts, sends):
        for j in range(part.start, part.stop, BLOCK):
            wt_ref[:, j : j + BLOCK] = tall(w_ref[j : j + BLOCK, :].T)
        send.start()
    for copy in copies + sends:
        copy.wait()


def near_body(
    turned, coords_ref, w_hbm, near_hbm, k_ref, sum_ref, own_ref, points_ref, wt_ref, columns_ref, w_sem, near_sem, *w_own
):
    n = coords_ref.shape[1]
    blocks = n // BLOCK
    wrap = (REACH - 1) * BLOCK
    fetch = pltpu.make_async_copy(w_hbm, wt_ref.at[:, 0:n] if turned else w_own[0], w_sem)
    fetch.start()
    points_ref[0:3, 0:n] = coords_ref[...] * LOG2E
    points_ref[3:, 0:n] = jnp.zeros((5, n), F32)
    points_ref[:, n:] = points_ref[:, 0:wrap]
    sum_ref[...] = jnp.zeros_like(sum_ref)

    for j in range(blocks):
        cols = slice(j * BLOCK, (j + 1) * BLOCK)
        columns_ref[cols, :] = points_ref[:, cols].T

    def place(i, slot):
        for k in range(3):
            own_ref[slot, k] = jnp.broadcast_to(
                columns_ref[pl.ds(pl.multiple_of(i * BLOCK, BLOCK), BLOCK), k : k + 1], (BLOCK, OUT)
            )

    def build(at, slot, d):
        for cols in (slice(c, c + OUT) for c in range(d * BLOCK, (d + 1) * BLOCK, OUT)):
            other = [points_ref[k : k + 1, pl.ds(at + cols.start, OUT)] for k in range(3)]
            for t in range(BLOCK // TILE):
                sub = slice(t * TILE, (t + 1) * TILE)
                diff_sq = None
                for k in range(3):
                    delta = own_ref[slot, k, sub, :] - other[k]
                    diff_sq = delta * delta if diff_sq is None else diff_sq + delta * delta
                dist = diff_sq * lax.rsqrt(jnp.maximum(diff_sq, 1e-37))
                k_ref[slot, 0, sub, cols], k_ref[slot, 1, sub, cols] = split(jnp.exp2(-dist))

    def product(w, hi, lo, contract):
        dims = (((1,), (contract,)), ((), ()))
        a = lax.dot_general(w, hi, dims, preferred_element_type=F32)
        b = lax.dot_general(w[:OUT], lo, dims, preferred_element_type=F32)
        return a[:OUT] + (a[OUT:] + b)

    def use(at, slot, d, count):
        cols = slice(d * BLOCK, (d + count) * BLOCK)
        where = pl.ds(at + d * BLOCK, count * BLOCK)
        part = product(wt_ref[:, where], k_ref[slot, 0, :, cols], k_ref[slot, 1, :, cols], 1)
        if d:
            sum_ref[:, where] += product(
                wt_ref[:, pl.ds(at, BLOCK)], k_ref[slot, 0, :, cols], k_ref[slot, 1, :, cols], 0
            )
        return part

    def finish(at, parts):
        sum_ref[:, pl.ds(at, BLOCK)] += functools.reduce(jnp.add, parts)

    def pair(p, carry):
        for slot in range(2):
            prev = pl.multiple_of((2 * p + slot) * BLOCK, BLOCK)
            at = pl.multiple_of(prev + BLOCK, BLOCK)
            place(lax.rem(2 * p + slot + 2, blocks), slot)
            total = None
            for d in range(REACH):
                part = use(prev, slot, d, 1)
                total = part if total is None else total + part
                build(at, 1 - slot, d)
            finish(prev, [total])
        return carry

    place(0, 0)
    place(1, 1)
    for d in range(REACH):
        build(0, 0, d)
    fetch.wait()
    if not turned:
        for j in range(blocks):
            cols = slice(j * BLOCK, (j + 1) * BLOCK)
            wt_ref[:, cols] = tall(w_own[0][cols, :].T)
    wt_ref[:, n:] = wt_ref[:, 0:wrap]
    lax.fori_loop(0, (blocks - 1) // 2, pair, 0)
    last = (blocks - 1) * BLOCK
    parts = [slice(wrap, last), slice(0, wrap), slice(last, n)]
    sends = [
        pltpu.make_async_copy(sum_ref.at[:, p], near_hbm.at[:, p], near_sem.at[j]) for j, p in enumerate(parts)
    ]
    sends[0].start()
    finish(last, [use(last, 0, 0, 1), use(last, 0, 1, REACH - 1)])
    sum_ref[:, 0:wrap] += sum_ref[:, n:]
    sends[1].start()
    sends[2].start()
    for send in sends:
        send.wait()


def middle_body(own_ref, m1_ref, m2_ref, m3_ref, out_ref):
    tail = slice(RANK, RANK + 2 * QROWS)
    total = (own_ref[...] + m1_ref[tail, :]) + (m2_ref[tail, :] + m3_ref[tail, :])
    out_ref[...] = jnp.broadcast_to(total[None], out_ref.shape)


def couple_body(got_ref, couple_ref, g1_ref, s2_ref, spread_ref):
    s2 = jnp.zeros((QROWS, OUT), F32)
    for m in range(N_MID):
        spread_ref[m * RANK : (m + 1) * RANK, :] = wide(expand_packed(got_ref[m, 0:QROWS, :]))
        s2 = s2 + got_ref[m, QROWS:, :]
    g1_ref[...] = fold_and_pack(dot3(couple_ref[...], spread_ref[...]))
    s2_ref[...] = s2


def update_body(last, *refs):
    near_ref, messages, down_ref, tops = refs[0], refs[1:4], refs[4], refs[5:9]
    base_ref, bcat_ref = refs[9:11]
    if last:
        out_hbm, out_ref, out_sem = refs[11:]
    else:
        basis_t_ref, up_ref, out_ref, own_ref = refs[11:15]
        message_refs = refs[15:18]
        (whl_ref,) = refs[18:]
    blocks = [slice(j, j + BLOCK) for j in range(0, base_ref.shape[0], BLOCK)]
    parts = [slice(j, j + GROUP * BLOCK) for j in range(0, base_ref.shape[0], GROUP * BLOCK)]
    own = lax.axis_index("leaf")
    quarters = [lax.rem(own + N_LEAF - k, N_LEAF) for k in range(N_LEAF)]
    g1 = unpack_quarters([ref[0:QROWS, :] for ref in tops], quarters)
    s2 = unpack_quarters([ref[QROWS:, :] for ref in tops], quarters)
    skeletons = [ref[0:RANK, :] for ref in messages] + [g1, s2]
    g0 = dot3(down_ref[...], wide(jnp.concatenate(skeletons, axis=0)))
    hi, lo = split(g0)
    rhs = jnp.concatenate(
        [jnp.concatenate([hi, lo], axis=1), jnp.concatenate([hi, jnp.zeros_like(lo)], axis=1)], axis=0
    )
    sends = []
    for j, part in enumerate(parts):
        for rows in blocks[j * GROUP : (j + 1) * GROUP]:
            f = jnp.dot(bcat_ref[rows, :], rhs, preferred_element_type=F32)
            f = near_ref[rows, :] + (f[:, :OUT] + f[:, OUT:])
            new = base_ref[rows, :] - (0.5 * jnp.tanh(0.5 * f) + 0.5)
            out_ref[rows, :] = new
            if not last:
                whl_ref[rows, :] = wide(new)
        for i, rows in enumerate(blocks[j * GROUP : (j + 1) * GROUP] if last else [], j * GROUP):
            sends.append(pltpu.make_async_copy(out_ref.at[rows], out_hbm.at[rows], out_sem.at[i]))
            sends[i].start()
    if not last:
        s0 = dot3(tall(basis_t_ref[...]), whl_ref[...])
        emit_messages(s0, up_ref[...], own_ref, message_refs)
    for send in sends:
        send.wait()


def params(mib):
    return pltpu.CompilerParams(vmem_limit_bytes=mib << 20)


def shape(*dims, dtype=F32):
    return jax.ShapeDtypeStruct(dims, dtype)


def ring(k):
    return [(i, (i + k) % N_LEAF) for i in range(N_LEAF)]


def call(body, out, operands, mib, name, scratch=(), work=(0, 0, 0), far_in=(), far_out=()):
    out = [pltpu.HBM(o.shape, o.dtype) if i in far_out else o for i, o in enumerate(out)]
    operands = [
        pltpu.with_memory_space_constraint(x, pltpu.HBM) if i in far_in else x
        for i, x in enumerate(operands)
    ]
    return pl.pallas_call(
        body,
        out_shape=out,
        in_specs=[HBM if i in far_in else VMEM for i in range(len(operands))],
        out_specs=[HBM if i in far_out else VMEM for i in range(len(out))],
        scratch_shapes=scratch,
        compiler_params=params(mib),
        cost_estimate=pl.CostEstimate(flops=work[0], bytes_accessed=work[1], transcendentals=work[2]),
        name=name,
    )(*operands)


def on_device(
    coords,
    weights,
    labels,
    order,
    basis,
    transfer_leaf,
    transfer_mid,
    couple_leaf,
    couple_mid,
    couple_top,
):
    n = weights.shape[0]
    scale = 4.0 / math.sqrt(n)
    basis_t = basis.T
    groups = n // (GROUP * BLOCK)
    wide_n = n + (REACH - 1) * BLOCK
    message_shapes = [shape(2 * QROWS, OUT)] + [shape(RANK + 2 * QROWS, OUT)] * 3

    up, own, *messages = call(
        first_body,
        [shape(RANK, 2 * RANK), *message_shapes],
        (basis_t, weights, transfer_leaf, transfer_mid),
        8,
        "first",
        [
            pltpu.VMEM((RANK, n), F32),
            pltpu.VMEM((n, OUT), F32),
            pltpu.VMEM((1, RANK, RANK), F32),
            pltpu.VMEM((1, RANK, RANK), F32),
            pltpu.SemaphoreType.DMA((4,)),
        ],
        far_in=(0, 1, 2, 3),
    )
    bcat, couple, down = call(
        prepare_body,
        [
            shape(n, 2 * RANK, dtype=BF16),
            shape(2 * RANK, N_MID * RANK, dtype=BF16),
            shape(2 * RANK, 5 * RANK, dtype=BF16),
        ],
        (basis_t, transfer_leaf, transfer_mid, couple_leaf, couple_mid, couple_top),
        58,
        "prepare",
    )
    own, couple = lax.optimization_barrier((own, couple))

    current = weights
    for step in range(STEPS):
        last = step == STEPS - 1
        if step:
            w_near, current = call(
                turn_body,
                [shape(2 * OUT, n, dtype=BF16), shape(n, OUT)],
                (current,),
                8,
                "turn",
                [
                    pltpu.VMEM((2 * OUT, n), BF16),
                    pltpu.SemaphoreType.DMA((groups,)),
                    pltpu.SemaphoreType.DMA((groups,)),
                ],
                (0, n * OUT * 12, 0),
                far_out=(0, 1),
            )
            own, w_near = lax.optimization_barrier((own, w_near))
        else:
            w_near = current
        (near_t,) = call(
            functools.partial(near_body, bool(step)),
            [shape(OUT, n)],
            (coords, w_near),
            20,
            "near",
            [
                pltpu.VMEM((2, 2, BLOCK, REACH * BLOCK), BF16),
                pltpu.VMEM((OUT, wide_n), F32),
                pltpu.VMEM((2, 3, BLOCK, OUT), F32),
                pltpu.VMEM((8, wide_n), F32),
                pltpu.VMEM((2 * OUT, wide_n), BF16),
                pltpu.VMEM((n, 8), F32),
                pltpu.SemaphoreType.DMA,
                pltpu.SemaphoreType.DMA((3,)),
            ]
            + ([] if step else [pltpu.VMEM((n, OUT), F32)]),
            (6 * n * n * OUT, n * OUT * 12, n * n),
            (1,),
            (0,),
        )
        messages = [lax.ppermute(m, "leaf", ring(k)) for k, m in enumerate(messages, 1)]
        (spread,) = call(middle_body, [shape(N_MID, 2 * QROWS, OUT)], (own, *messages), 4, "middle")
        got = lax.all_to_all(spread, "mid", 0, 0)
        got, near_t = lax.optimization_barrier((got, near_t))
        g1, s2 = call(
            couple_body,
            [shape(QROWS, OUT)] * 2,
            (got, couple),
            8,
            "couple",
            [pltpu.VMEM((N_MID * RANK, 2 * OUT), BF16)],
        )
        s2 = lax.ppermute(s2, "top", [(0, 1), (1, 0)])
        top = jnp.concatenate([g1, s2], axis=0)
        tops = [top] + [lax.ppermute(top, "leaf", ring(k)) for k in (1, 2, 3)]
        kept = [pltpu.VMEM((OUT, n), F32), pltpu.VMEM((n, OUT), F32)]
        if step:
            near, base = call(
                functools.partial(finish_body, scale),
                [shape(n, OUT)] * 2,
                (near_t, current, targets),
                8,
                "finish",
                [*kept, pltpu.VMEM((n, OUT), F32), pltpu.SemaphoreType.DMA((3, 3))],
                (n * OUT, n * OUT * 20, 0),
                (0, 1, 2),
            )
        else:
            near, base, targets = call(
                functools.partial(finish_body, scale),
                [shape(n, OUT)] * 3,
                (near_t, current, order, labels),
                16,
                "finish",
                [
                    *kept,
                    pltpu.VMEM((n, OUT), jnp.int32),
                    pltpu.VMEM((n, OUT), F32),
                    pltpu.VMEM((n, n // BITS), BF16),
                    pltpu.VMEM((n, 8), F32),
                    pltpu.SemaphoreType.DMA((3, 3)),
                    pltpu.SemaphoreType.DMA,
                ],
                (n * n // BITS * 2 * OUT, n * OUT * 24, 0),
                (0, 1, 3),
                (2,),
            )
        far = (near, *messages, down, *tops, base, bcat)
        rows_buffer = [pltpu.VMEM((n, OUT), F32), pltpu.SemaphoreType.DMA((n // BLOCK,))]
        body = functools.partial(update_body, last)
        if last:
            (current,) = call(
                body, [shape(n, OUT)], far, 8, "last", rows_buffer, far_out=(0,)
            )
        else:
            current, own, *messages = call(
                body,
                [shape(n, OUT), *message_shapes],
                (*far, basis_t, up),
                12,
                "update",
                [pltpu.VMEM((n, 2 * OUT), BF16)],
            )
    return current


def solution(mesh):
    placed = (
        P(None, ("top", "mid", "leaf")),
        P(("top", "mid", "leaf"), None),
        P(("top", "mid", "leaf"), None),
        P(("top", "mid", "leaf"), None),
        P(("top", "mid", "leaf"), None),
        P(("top", "mid", "leaf"), None, None),
        P(("top", "mid"), None, None),
        P(("top", "mid", "leaf"), None, None, None),
        P(("top", "mid"), None, None, None),
        P("top", None, None, None),
    )
    return jax.shard_map(
        on_device,
        mesh=mesh,
        in_specs=placed,
        out_specs=P(("top", "mid", "leaf"), None),
        check_vma=False,
    )
```
